32 devices in a mesh: expert: 8 (over z, y), hid: 4 (over x, core).
Axes of the slice: x: 2, y: 2, z: 4, core: 2. Of those that a mesh axis runs over, the one named last changes fastest.
Arguments:
- tokens_in: bfloat16 [8192, 768], P(('expert', 'hid')), may hold values from -6 to 6
- out_cotangent: bfloat16 [8192, 768], P(('expert', 'hid')), may hold values from -6 to 6
- qkv_weight: float32 [768, 2304], P(('expert', 'hid')), may hold values from -0.21875 to 0.21875
- proj_weight: float32 [768, 768], P(('expert', 'hid')), may hold values from -2 to 2
- router_weight: float32 [768, 8], P(('expert', 'hid')), may hold values from -0.15625 to 0.15625
- pre_gain: float32 [768], P(('expert', 'hid')), may hold values from 0.5 to 1.5
- pre_shift: float32 [768], P(('expert', 'hid')), may hold values from -0.6 to 0.6
- mid_gain: float32 [768], P(('expert', 'hid')), may hold values from 0.5 to 1.5
- mid_shift: float32 [768], P(('expert', 'hid')), may hold values from -0.6 to 0.6
- expert_in: float32 [8, 768, 3072], P('expert', None, 'hid'), may hold values from -0.21875 to 0.21875
- expert_down: float32 [8, 3072, 768], P('expert', 'hid'), may hold values from -0.875 to 0.875
- assignment: int32 [8192], P(('expert', 'hid')), may hold values from 0 to 7, as said below
Outputs:
- layer_output: bfloat16 [8192, 768], P(('expert', 'hid'))
- balance_loss: float32 [], replicated
- input_grad: bfloat16 [8192, 768], P(('expert', 'hid'))
- qkv_grad: float32 [768, 2304], P(('expert', 'hid'))
- proj_grad: float32 [768, 768], P(('expert', 'hid'))
- router_grad: float32 [768, 8], P(('expert', 'hid'))
- pre_gain_grad: float32 [768], P(('expert', 'hid'))
- pre_shift_grad: float32 [768], P(('expert', 'hid'))
- mid_gain_grad: float32 [768], P(('expert', 'hid'))
- mid_shift_grad: float32 [768], P(('expert', 'hid'))
- expert_in_grad: float32 [8, 768, 3072], P('expert', None, 'hid')
- expert_down_grad: float32 [8, 3072, 768], P('expert', 'hid')
The draws below stay inside these ranges and needn't reach their ends.
Inputs may be any that keep to these rules, and one draw needn't show every extreme that they name: `assignment`: in each aligned block of 256 tokens (the tokens of one device) no expert is named by more than 64 tokens; one expert, drawn from the seed, is named by exactly 64 tokens of every block.
All inputs are finite; a program needn't handle non-finite values.
Results may differ from the reference program's by a relative error of at most 0.015.
The reference program's roundings to bfloat16 on the way count: a program that leaves them out, or rounds other values in their place, can miss the bound.
Values may be sent and summed in bfloat16 or wider, within the bound.
A program may use at most 192 MiB of HBM per device.

```python
import jax
import jax.numpy as jnp
from jax import lax

D = 768
HEADS = 12
HEAD_DIM = 64
FF = 3072
TOK_DEV = 256
EXPERTS = 8
TOKENS = 8192


def draw_assignment(key, part):
    key = jax.random.fold_in(key, 11)
    pick_key, popular_key, block_key = jax.random.split(key, 3)
    capacity = 2 * TOK_DEV // EXPERTS
    slot_total = EXPERTS * capacity
    device_count = TOKENS // TOK_DEV
    chosen = jax.random.randint(pick_key, (), 0, EXPERTS)
    popular = jax.random.randint(popular_key, (EXPERTS,), 0, 4096)
    slot_expert = jnp.repeat(jnp.arange(EXPERTS, dtype=jnp.int32), capacity)

    def one_block(single_key):
        noise_key, order_key = jax.random.split(single_key)
        noise = jax.random.randint(noise_key, (slot_total,), 0, 4096)
        score = noise + popular[slot_expert]
        score = jnp.where(slot_expert == chosen, 16384, score)
        score = score * slot_total + jnp.arange(slot_total, dtype=jnp.int32)
        ordering = jnp.argsort(-score, stable=True)
        picked = slot_expert[ordering[:TOK_DEV]]
        return jax.random.permutation(order_key, picked)
    block_keys = jax.random.split(block_key, device_count)
    blocks = jax.vmap(one_block)(block_keys)
    return blocks.reshape(TOKENS).astype(jnp.int32)


def block_levels(rng, dims, cuts, least, largest):
    level, own = 1.0, jax.random.fold_in(rng, 6)
    for axis_at, parts in cuts:
        draws = jnp.exp(jax.random.uniform(jax.random.fold_in(own, axis_at), (parts,), jnp.float32, least / len(cuts), largest / len(cuts)))
        level = level * jnp.repeat(draws, dims[axis_at] // parts).reshape([-1 if axis == axis_at else 1 for axis in range(len(dims))])
    return level


def normal_values(stream_key, shape, scale, limit, cuts=(), kind=jnp.bfloat16):
    drawn = scale * jax.random.normal(stream_key, shape, jnp.float32)
    if cuts:
        drawn = drawn * block_levels(stream_key, shape, cuts, -0.22, 0.18)
    return jnp.clip(drawn, -limit, limit).astype(kind)


def setup_inputs(seed: int = 0) -> dict:
    arg_keys = jax.random.split(jax.random.key(seed), 13)
    return {
        "tokens_in": normal_values(arg_keys[0], (TOKENS, D), 1.0, 6.0, ((0, 32),)),
        "out_cotangent": normal_values(arg_keys[1], (TOKENS, D), 1.0, 6.0, ((0, 32),)),
        "qkv_weight": normal_values(arg_keys[2], (D, 3 * D), D ** -0.5, 0.21875, ((0, 32),), jnp.float32),
        "proj_weight": normal_values(arg_keys[3], (D, D), (D // 96) ** -0.5, 2.0, ((0, 32),), jnp.float32),
        "router_weight": normal_values(arg_keys[4], (D, EXPERTS), (2 * D) ** -0.5, 0.15625, ((0, 32),), jnp.float32),
        "pre_gain": jnp.clip(1.0 + 0.1 * jax.random.normal(arg_keys[5], (D,), jnp.float32), 0.5, 1.5),
        "pre_shift": normal_values(arg_keys[6], (D,), 0.1, 0.6, ((0, 32),), jnp.float32),
        "mid_gain": jnp.clip(1.0 + 0.1 * jax.random.normal(arg_keys[7], (D,), jnp.float32), 0.5, 1.5),
        "mid_shift": normal_values(arg_keys[8], (D,), 0.1, 0.6, ((0, 32),), jnp.float32),
        "expert_in": normal_values(arg_keys[9], (EXPERTS, D, FF), D ** -0.5, 0.21875, ((0, 8), (2, 4)), jnp.float32),
        "expert_down": normal_values(arg_keys[10], (EXPERTS, FF, D), (max(1, FF // (EXPERTS * EXPERTS))) ** -0.5, 0.875, ((0, 8), (1, 4)), jnp.float32),
        "assignment": draw_assignment(jax.random.fold_in(arg_keys[12], 71), 0),
    }


@jax.custom_vjp
def low(v):
    return lax.optimization_barrier(v.astype(jnp.bfloat16)).astype(jnp.float32)

@jax.custom_vjp
def low_back(v):
    return v

def low_keep(v):
    return (low(v), None)

def low_pass(kept, grad):
    return (grad,)

def back_keep(v):
    return (v, None)

def back_low(kept, grad):
    return (low(grad),)
low.defvjp(low_keep, low_pass)
low_back.defvjp(back_keep, back_low)
highest = lax.Precision.HIGHEST
epsilon = 1e-05
balance_weight = 3.0
masked_score = -1000000000.0

def norm_apply(values, gain, shift):
    average = lax.optimization_barrier(jnp.mean(values, axis=-1, keepdims=True))
    centred = values - average
    spread = lax.optimization_barrier(jnp.mean(centred * centred, axis=-1, keepdims=True))
    return centred * lax.rsqrt(spread + epsilon) * gain + shift

def group_layer(inputs, params, assign_block, expert_scale):
    qkv_w, proj_w, router_w, gain_a, shift_a, gain_b, shift_b, in_w, down_w = params
    sequences = assign_block.shape[0]
    row_count = inputs.shape[0]
    capacity = 2 * TOK_DEV // EXPERTS
    hidden_a = low(norm_apply(inputs, gain_a, shift_a))
    qkv_rows = low_back(low(jnp.dot(hidden_a, qkv_w, precision=highest)))
    qkv_rows = qkv_rows.reshape(sequences, TOK_DEV, 3, HEADS, HEAD_DIM)
    queries = qkv_rows[:, :, 0]
    key_rows = qkv_rows[:, :, 1]
    value_rows = qkv_rows[:, :, 2]
    score_scale = HEAD_DIM ** (-0.5)
    scores = low_back(jnp.einsum('sqhd,skhd->shqk', queries, key_rows, precision=highest) * score_scale)
    positions = jnp.arange(TOK_DEV, dtype=jnp.int32)
    allowed = positions[None, :] <= positions[:, None]
    scores = jnp.where(allowed[None, None], scores, masked_score)
    row_max = lax.optimization_barrier(jnp.max(scores, axis=-1, keepdims=True))
    logsum = row_max + jnp.log(lax.optimization_barrier(jnp.sum(jnp.exp(scores - row_max), axis=-1, keepdims=True)))
    weights = low(jnp.exp(scores - logsum))
    mixed_rows = low_back(low(jnp.einsum('shqk,skhd->sqhd', weights, value_rows, precision=highest)))
    mixed_rows = mixed_rows.reshape(row_count, HEADS * HEAD_DIM)
    residual = inputs + low_back(jnp.dot(mixed_rows, proj_w, precision=highest))
    hidden_b = low(norm_apply(residual, gain_b, shift_b))
    logits = low_back(jnp.dot(hidden_b, router_w, precision=highest))
    router_probs = jax.nn.softmax(logits, axis=-1)
    labels = jnp.arange(EXPERTS, dtype=jnp.int32)
    onehot = (assign_block[:, :, None] == labels[None, None, :]).astype(jnp.int32)
    ranking = jnp.cumsum(onehot, axis=1) - 1
    slot_index = lax.optimization_barrier(jnp.sum(ranking * onehot, axis=2)) + jnp.arange(sequences, dtype=jnp.int32)[:, None] * capacity
    position = (assign_block * (sequences * capacity) + slot_index).reshape(row_count)
    slot_owner = jnp.full((EXPERTS * sequences * capacity,), row_count, jnp.int32)
    slot_owner = slot_owner.at[position].set(jnp.arange(row_count, dtype=jnp.int32))
    gate_value = lax.optimization_barrier(jnp.sum(router_probs * onehot.reshape(row_count, EXPERTS).astype(jnp.float32), axis=1))
    dispatched = low_back(hidden_b)
    padded = jnp.concatenate([dispatched, jnp.zeros((1, dispatched.shape[1]), jnp.float32)], axis=0)
    expert_rows = padded[slot_owner].reshape(EXPERTS, sequences * capacity, D)
    before = low_back(jnp.einsum('erd,edf->erf', expert_rows, in_w, precision=highest))
    active = low(jax.nn.gelu(before, approximate=False))
    expert_out = low_back(low(jnp.einsum('erf,efd->erd', active, down_w, precision=highest)))
    token_out = expert_out.reshape(EXPERTS * sequences * capacity, D)[position]
    output = residual + gate_value[:, None] * token_out
    balance = jnp.sum(router_probs * expert_scale[None, :]) / TOKENS
    return (output, balance)

def reference(tokens_in, out_cotangent, qkv_weight, proj_weight, router_weight, pre_gain, pre_shift, mid_gain, mid_shift, expert_in, expert_down, assignment):
    labels = jnp.arange(EXPERTS, dtype=jnp.int32)
    counts = lax.optimization_barrier(jnp.sum((assignment[:, None] == labels[None, :]).astype(jnp.float32), axis=0))
    expert_scale = balance_weight * EXPERTS * counts / TOKENS
    groups = TOKENS // (8 * TOK_DEV)
    assign_groups = assignment.reshape(groups, 8, TOK_DEV)

    def forward(inputs, qkv_w, proj_w, router_w, gain_a, shift_a, gain_b, shift_b, in_w, down_w):
        params = (low(qkv_w), low(proj_w), low(router_w), low(gain_a), low(shift_a), low(gain_b), low(shift_b), low(in_w), low(down_w))

        def one_group(loss_total, pieces):
            input_rows, assign_block = pieces
            output, balance = group_layer(input_rows, params, assign_block, expert_scale)
            return (loss_total + balance, output)
        loss_total, outputs = lax.scan(jax.checkpoint(one_group), jnp.zeros((), jnp.float32), (inputs.reshape(groups, 8 * TOK_DEV, D), assign_groups))
        return (outputs.reshape(TOKENS, D), loss_total)
    (output, balance_loss), pullback = jax.vjp(forward, tokens_in.astype(jnp.float32), qkv_weight, proj_weight, router_weight, pre_gain, pre_shift, mid_gain, mid_shift, expert_in, expert_down)
    gradients = pullback((out_cotangent.astype(jnp.float32), jnp.full((), TOKENS, jnp.float32)))
    return (output.astype(jnp.bfloat16), balance_loss, gradients[0].astype(jnp.bfloat16), gradients[1], gradients[2], gradients[3], gradients[4], gradients[5], gradients[6], gradients[7], gradients[8], gradients[9])
```

```python
import functools

import jax
import jax.numpy as jnp
from jax import lax
from jax.experimental import pallas as pl
from jax.experimental.pallas import tpu as pltpu
from jax.sharding import PartitionSpec as P

HEADS = 12


epsilon = 1e-05
balance_weight = 3.0
masked_score = -1000000000.0
MESH = pl.DeviceIdType.MESH
half = jnp.bfloat16
single = jnp.float32


def remote(src, dst, send_sem, recv_sem, device):
    return pltpu.make_async_remote_copy(
        src_ref=src, dst_ref=dst, send_sem=send_sem, recv_sem=recv_sem,
        device_id=device, device_id_type=MESH,
    )


def dot(a, b):
    return jnp.dot(a, b, preferred_element_type=single)


def dot_cols(a, b):
    return lax.dot_general(a, b, (((1,), (1,)), ((), ())), preferred_element_type=single)


def dot_rows(a, b):
    return lax.dot_general(a, b, (((0,), (0,)), ((), ())), preferred_element_type=single)


def expert_kernel(
    E, X, G, out_h, out_g, w_in, w_dn, ret_o, ret_g, in_grad, dn_grad,
    xh, xg, win, wdn, act, gbef, po, pg, so, sg, ro, rg, to, tg, gs, gr, before, ga,
    send_a, recv_a, send_x, recv_x, send_p, recv_p, send_r, recv_r, send_w, recv_w, send_d, recv_d,
):
    e = lax.axis_index("expert")
    h = lax.axis_index("hid")
    x = lax.div(h, 2)
    c = lax.rem(h, 2)
    other = 1 - c
    D = w_in.shape[0]
    Fq = w_in.shape[1]
    cap = out_h.shape[1]
    NG = E // G
    rows = G * cap
    core_peer = (e, x * 2 + other)

    def expert_peer(k):
        return (lax.rem(e + k, E), h)

    def x_peer(d):
        return (e, lax.rem(x + d, X) * 2 + c)

    barrier = pltpu.get_barrier_semaphore()

    @pl.loop(1, E)
    def _(k):
        pl.semaphore_signal(barrier, inc=1, device_id=expert_peer(k), device_id_type=MESH)

    for d in range(1, X):
        pl.semaphore_signal(barrier, inc=1, device_id=x_peer(d), device_id_type=MESH)
    pl.semaphore_signal(barrier, inc=1, device_id=core_peer, device_id_type=MESH)
    pl.semaphore_wait(barrier, E - 1 + X - 1 + 1)

    def dispatch(k, part):
        to_e = lax.rem(e + E - k, E)
        src, dst = ((out_h, xh), (out_g, xg))[part]
        return remote(src.at[to_e], dst.at[0, k], send_a.at[part, k], recv_a.at[part, k], (to_e, h))

    def forward(k, part, d):
        dst = (xh, xg)[part]
        return remote(
            dst.at[0, k], dst.at[X - d, k], send_x.at[part, d - 1, k], recv_x.at[part, X - d - 1, k],
            x_peer(d),
        )

    @pl.loop(1, E)
    def _(k):
        dispatch(k, 0).start()
        dispatch(k, 1).start()

    xh[0, 0] = out_h[e]
    xg[0, 0] = out_g[e]

    step = 32

    @pl.loop(0, D // step)
    def _(i):
        at = pl.ds(pl.multiple_of(i * step, step), step)
        win[c, at, :] = w_in[at, :].astype(half)

    @pl.loop(0, Fq // step)
    def _(i):
        at = pl.ds(pl.multiple_of(i * step, step), step)
        wdn[c, at, :] = w_dn[at, :].astype(half)

    win_copy = remote(win.at[c], win.at[c], send_w.at[0], recv_w.at[0], core_peer)
    wdn_copy = remote(wdn.at[c], wdn.at[c], send_w.at[1], recv_w.at[1], core_peer)
    win_copy.start()
    wdn_copy.start()

    def pass_on(g):
        @pl.loop(0, G)
        def _(i):
            k = g * G + i

            @pl.when(k > 0)
            def _():
                dispatch(k, 0).wait_recv()
                dispatch(k, 1).wait_recv()

            for d in range(1, X):
                forward(k, 0, d).start()
                forward(k, 1, d).start()

    def take(j, g):
        @pl.loop(0, G)
        def _(i):
            k = g * G + i
            forward(k, 0, X - j).wait_recv()
            forward(k, 1, X - j).wait_recv()

    def compute(j, g):
        slots = pl.ds(g * G, G)
        t = j * NG + g
        xh_g = xh[j, slots].reshape(rows, D)
        xg_g = xg[j, slots].reshape(rows, D)
        for q in range(2):
            before[...] = dot(xh_g, win[q])
            ga[...] = dot_cols(xg_g, wdn[q])

            @pl.loop(0, rows // step)
            def _(i):
                at = pl.ds(pl.multiple_of(i * step, step), step)
                v = before[at, :]
                cdf = 0.5 * (1.0 + lax.erf(v * (0.5 ** 0.5)))
                slope = cdf + v * (jnp.exp(-0.5 * v * v) * 0.3989422804014327)
                act[q, t, at, :] = (v * cdf).astype(half)
                gbef[q, t, at, :] = (slope * ga[at, :]).astype(half)

        out = dot(act[0, t], wdn[0]) + dot(act[1, t], wdn[1])
        gin = dot_cols(gbef[0, t], win[0]) + dot_cols(gbef[1, t], win[1])
        return out, gin

    def partial(j, g, part):
        src, dst = ((so, ro), (sg, rg))[part]
        return remote(
            src.at[j - 1, pl.ds(g * G, G)], dst.at[X - j - 1, pl.ds(g * G, G)],
            send_p.at[part, j - 1, g], recv_p.at[part, X - j - 1, g], x_peer(j),
        )

    def give_back(k, part):
        src, dst = ((to, ret_o), (tg, ret_g))[part]
        return remote(src.at[k], dst.at[e], send_r.at[part, k], recv_r.at[part, k], expert_peer(k))

    def finish(g):
        for j in range(1, X):
            for part in range(2):
                partial(X - j, g, part).wait_recv()

        @pl.loop(0, G)
        def _(i):
            k = g * G + i
            for part, own, got, total in ((0, po, ro, to), (1, pg, rg, tg)):
                value = own[k]
                for j in range(X - 1):
                    value = value + got[j, k].astype(single)
                total[k] = value.astype(half)

            @pl.when(k > 0)
            def _():
                give_back(k, 0).start()
                give_back(k, 1).start()

            @pl.when(k == 0)
            def _():
                ret_o[e] = to[0]
                ret_g[e] = tg[0]

    @pl.loop(0, NG * X)
    def _(t):
        g = lax.div(t, X)
        j = lax.rem(t, X)

        @pl.when(j == 0)
        def _():
            pass_on(g)

        for d in range(1, X):
            @pl.when(j == d)
            def _():
                take(d, g)

        @pl.when(t == 0)
        def _():
            win_copy.wait_recv()
            wdn_copy.wait_recv()

        out, gin = compute(j, g)
        slots = pl.ds(g * G, G)

        @pl.when(j == 0)
        def _():
            po[slots] = out.reshape(G, cap, D)
            pg[slots] = gin.reshape(G, cap, D)

        for d in range(1, X):
            @pl.when(j == d)
            def _():
                so[d - 1, slots] = out.astype(half).reshape(G, cap, D)
                sg[d - 1, slots] = gin.astype(half).reshape(G, cap, D)
                partial(d, g, 0).start()
                partial(d, g, 1).start()

        @pl.when((j == 0) & (g > 0))
        def _():
            finish(g - 1)

    finish(NG - 1)

    T = X * NG * rows
    tile = 256 if Fq % 256 == 0 else 128

    def grad_in(q, i):
        lhs = xh[:, :, :, pl.ds(pl.multiple_of(i * tile, tile), tile)].reshape(T, tile)
        return dot_rows(lhs, gbef[q].reshape(T, Fq))

    def grad_dn(q, i):
        lhs = act[q, :, :, pl.ds(pl.multiple_of(i * tile, tile), tile)].reshape(T, tile)
        return dot_rows(lhs, xg[...].reshape(T, D))

    @pl.loop(0, D // tile)
    def _(i):
        gs[0, pl.ds(pl.multiple_of(i * tile, tile), tile), :Fq] = grad_in(other, i)

    in_copy = remote(gs.at[0, :, :Fq], gr.at[0, :, :Fq], send_d.at[0], recv_d.at[0], core_peer)
    in_copy.start()

    @pl.loop(0, Fq // tile)
    def _(i):
        gs[1, pl.ds(pl.multiple_of(i * tile, tile), tile), :] = grad_dn(other, i)

    dn_copy = remote(gs.at[1, :Fq], gr.at[1, :Fq], send_d.at[1], recv_d.at[1], core_peer)
    dn_copy.start()

    @pl.loop(0, D // tile)
    def _(i):
        in_grad[pl.ds(pl.multiple_of(i * tile, tile), tile), :] = grad_in(c, i)

    @pl.loop(0, Fq // tile)
    def _(i):
        dn_grad[pl.ds(pl.multiple_of(i * tile, tile), tile), :] = grad_dn(c, i)

    in_copy.wait_recv()

    @pl.loop(0, D // step)
    def _(i):
        at = pl.ds(pl.multiple_of(i * step, step), step)
        in_grad[at, :] += gr[0, at, :Fq]

    dn_copy.wait_recv()

    @pl.loop(0, Fq // step)
    def _(i):
        at = pl.ds(pl.multiple_of(i * step, step), step)
        dn_grad[at, :] += gr[1, at, :]

    win_copy.wait_send()
    wdn_copy.wait_send()
    in_copy.wait_send()
    dn_copy.wait_send()

    @pl.loop(0, E)
    def _(k):
        for part in range(2):
            @pl.when(k > 0)
            def _():
                dispatch(k, part).wait_send()
                give_back(k, part).wait()

            for d in range(1, X):
                forward(k, part, d).wait_send()

    for g in range(NG):
        for part in range(2):
            for j in range(1, X):
                partial(j, g, part).wait_send()


def expert_call(out_h, out_g, w_in, w_dn, X):
    E, cap, D = out_h.shape
    Fq = w_in.shape[1]
    G = max(1, min(E, 256 // cap))
    NG = E // G
    rows = G * cap
    dma = pltpu.SemaphoreType.DMA
    token = jax.ShapeDtypeStruct((E, cap, D), half)
    vmem = pl.BlockSpec(memory_space=pltpu.VMEM)
    return pl.pallas_call(
        functools.partial(expert_kernel, E, X, G),
        out_shape=(
            token, token,
            jax.ShapeDtypeStruct((D, Fq), single), jax.ShapeDtypeStruct((Fq, D), single),
        ),
        in_specs=[vmem] * 4,
        out_specs=(vmem,) * 4,
        scratch_shapes=[
            pltpu.VMEM((X, E, cap, D), half), pltpu.VMEM((X, E, cap, D), half),
            pltpu.VMEM((2, D, Fq), half), pltpu.VMEM((2, Fq, D), half),
            pltpu.VMEM((2, X * NG, rows, Fq), half), pltpu.VMEM((2, X * NG, rows, Fq), half),
            pltpu.VMEM((E, cap, D), single), pltpu.VMEM((E, cap, D), single),
            pltpu.VMEM((X - 1, E, cap, D), half), pltpu.VMEM((X - 1, E, cap, D), half),
            pltpu.VMEM((X - 1, E, cap, D), half), pltpu.VMEM((X - 1, E, cap, D), half),
            pltpu.VMEM((E, cap, D), half), pltpu.VMEM((E, cap, D), half),
            pltpu.VMEM((2, D, D), single), pltpu.VMEM((2, D, D), single),
            pltpu.VMEM((rows, Fq), single), pltpu.VMEM((rows, Fq), single),
            dma((2, E)), dma((2, E)),
            dma((2, X - 1, E)), dma((2, X - 1, E)),
            dma((2, X - 1, NG)), dma((2, X - 1, NG)),
            dma((2, E)), dma((2, E)),
            dma((2,)), dma((2,)), dma((2,)), dma((2,)),
        ],
        compiler_params=pltpu.CompilerParams(
            collective_id=1, has_side_effects=True, vmem_limit_bytes=60 * 1024 * 1024,
        ),
        name="experts",
    )(out_h, out_g, w_in, w_dn)


def norm_apply(values, gain, shift):
    average = jnp.mean(values, axis=-1, keepdims=True)
    centred = values - average
    spread = jnp.mean(centred * centred, axis=-1, keepdims=True)
    return centred * lax.rsqrt(spread + epsilon) * gain + shift


def contract_rows(left, right):
    return lax.dot_general(
        left, right, (((0,), (0,)), ((), ())), preferred_element_type=jnp.float32
    )


def contract_cols(left, right):
    return lax.dot_general(
        left, right, (((1,), (1,)), ((), ())), preferred_element_type=jnp.float32
    )


def build_slots(assignment, experts, capacity):
    token_count = assignment.shape[0]
    labels = jnp.arange(experts, dtype=jnp.int32)
    onehot = (assignment[:, None] == labels[None, :]).astype(jnp.int32)
    ranking = jnp.cumsum(onehot, axis=0) - 1
    slot_index = jnp.sum(ranking * onehot, axis=1)
    position = assignment * capacity + slot_index
    slot_owner = jnp.full((experts * capacity,), token_count, jnp.int32)
    slot_owner = slot_owner.at[position].set(jnp.arange(token_count, dtype=jnp.int32))
    return (position, slot_owner, onehot)


def take_rows(values, slot_owner):
    padded = jnp.concatenate([values, jnp.zeros((1, values.shape[1]), values.dtype)], axis=0)
    return padded[slot_owner]


def on_device(
    tokens_in,
    out_cotangent,
    qkv_weight,
    proj_weight,
    router_weight,
    pre_gain,
    pre_shift,
    mid_gain,
    mid_shift,
    expert_in,
    expert_down,
    assignment,
):
    token_count, model_width = tokens_in.shape
    experts = lax.axis_size("expert")
    capacity = 2 * token_count // experts
    total_tokens = token_count * experts * lax.axis_size("hid")
    head_dim = model_width // HEADS
    score_scale = head_dim ** (-0.5)
    half = jnp.bfloat16
    single = jnp.float32
    gathered = (
        lax.all_gather(qkv_weight.astype(half), ("expert", "hid"), axis=0, tiled=True),
        lax.all_gather(proj_weight.astype(half), ("expert", "hid"), axis=0, tiled=True),
        lax.all_gather(router_weight.astype(half), ("expert", "hid"), axis=0, tiled=True),
        lax.all_gather(pre_gain.astype(half), ("expert", "hid"), axis=0, tiled=True),
        lax.all_gather(pre_shift.astype(half), ("expert", "hid"), axis=0, tiled=True),
        lax.all_gather(mid_gain.astype(half), ("expert", "hid"), axis=0, tiled=True),
        lax.all_gather(mid_shift.astype(half), ("expert", "hid"), axis=0, tiled=True),
    )
    w_qkv, w_proj, w_router, gain_a, shift_a, gain_b, shift_b = gathered
    inputs = tokens_in.astype(single)
    normed_a, pre_back = jax.vjp(norm_apply, inputs, gain_a.astype(single), shift_a.astype(single))
    hidden_a = normed_a.astype(half)
    qkv_rows = jnp.dot(hidden_a, w_qkv, preferred_element_type=single).astype(half)
    queries = qkv_rows[:, :model_width].reshape(token_count, HEADS, head_dim)
    key_rows = qkv_rows[:, model_width : 2 * model_width].reshape(token_count, HEADS, head_dim)
    value_rows = qkv_rows[:, 2 * model_width :].reshape(token_count, HEADS, head_dim)
    block_rows = min(token_count, 512)
    block_count = token_count // block_rows
    key_index = jnp.arange(token_count, dtype=jnp.int32)

    def block_scores(first_row, query_block):
        raw_scores = (
            jnp.einsum("qhd,khd->hqk", query_block, key_rows, preferred_element_type=single)
            * score_scale
        )
        query_index = first_row + jnp.arange(block_rows, dtype=jnp.int32)
        allowed = key_index[None, :] <= query_index[:, None]
        return jnp.where(allowed[None], raw_scores, masked_score)

    def attend(block_index):
        first_row = block_index * block_rows
        scores = block_scores(first_row, queries)
        row_max = jnp.max(scores, axis=-1, keepdims=True)
        logsum = row_max + jnp.log(jnp.sum(jnp.exp(scores - row_max), axis=-1, keepdims=True))
        weights = jnp.exp(scores - logsum).astype(half)
        mixed_rows = jnp.einsum("hqk,khd->qhd", weights, value_rows, preferred_element_type=single)
        return (mixed_rows.astype(half), logsum)

    mixed_blocks, logsum_blocks = lax.map(attend, jnp.arange(block_count, dtype=jnp.int32))
    attended = mixed_blocks.reshape(token_count, model_width)
    residual = inputs + jnp.dot(attended, w_proj, preferred_element_type=single)
    normed_b, mid_back = jax.vjp(
        norm_apply, residual, gain_b.astype(single), shift_b.astype(single)
    )
    hidden_b = normed_b.astype(half)
    logits = jnp.dot(hidden_b, w_router, preferred_element_type=single)
    router_probs = jax.nn.softmax(logits, axis=-1)
    position, slot_owner, onehot = build_slots(assignment, experts, capacity)
    onehot_f = onehot.astype(single)
    gate_value = jnp.sum(router_probs * onehot_f, axis=1)
    counts, prob_total = lax.psum(
        (jnp.sum(onehot_f, axis=0), jnp.sum(router_probs, axis=0)), ("expert", "hid")
    )
    expert_scale = balance_weight * experts * counts / total_tokens
    balance_loss = jnp.sum(expert_scale * prob_total) / total_tokens
    outgoing = take_rows(hidden_b, slot_owner).reshape(experts, capacity, model_width)
    cotangent = out_cotangent.astype(single)
    grad_expert = (gate_value[:, None] * cotangent).astype(half)
    outgoing_grad = take_rows(grad_expert, slot_owner).reshape(experts, capacity, model_width)
    arrived, back_rows, in_grad, down_grad = expert_call(
        outgoing, outgoing_grad, expert_in[0], expert_down[0], lax.axis_size("hid") // 2
    )
    local_rows = experts * capacity
    expert_tok = arrived.reshape(local_rows, model_width)[position]
    layer_output = (residual + gate_value[:, None] * expert_tok.astype(single)).astype(half)
    grad_gate = jnp.sum(cotangent * expert_tok.astype(single), axis=1)
    grad_dispatch = back_rows.reshape(local_rows, model_width)[position].astype(single)
    grad_probs = onehot_f * grad_gate[:, None] + expert_scale[None, :]
    grad_logits = (
        router_probs * (grad_probs - jnp.sum(router_probs * grad_probs, axis=1, keepdims=True))
    ).astype(half)
    router_local = contract_rows(hidden_b, grad_logits)
    grad_hidden_b = grad_dispatch + contract_cols(grad_logits, w_router)
    grad_resid_n, mid_gain_local, mid_shift_local = mid_back(grad_hidden_b)
    grad_resid = cotangent + grad_resid_n
    grad_proj = grad_resid.astype(half)
    proj_local = contract_rows(attended, grad_proj)
    grad_attended = (
        contract_cols(grad_proj, w_proj).astype(half).reshape(token_count, HEADS, head_dim)
    )

    def attend_back(carry, block_index):
        key_total, value_total = carry
        first_row = block_index * block_rows
        scores = block_scores(first_row, queries)
        probs_f = jnp.exp(scores - logsum_blocks[block_index])
        weights = probs_f.astype(half)
        value_total = value_total + jnp.einsum(
            "hqk,qhd->khd", weights, grad_attended, preferred_element_type=single
        )
        grad_weights = jnp.einsum(
            "qhd,khd->hqk", grad_attended, value_rows, preferred_element_type=single
        )
        grad_scores = (
            probs_f * (grad_weights - jnp.sum(probs_f * grad_weights, axis=-1, keepdims=True))
        ).astype(half)
        grad_query = (
            jnp.einsum("hqk,khd->qhd", grad_scores, key_rows, preferred_element_type=single)
            * score_scale
        )
        key_total = (
            key_total
            + jnp.einsum("hqk,qhd->khd", grad_scores, queries, preferred_element_type=single)
            * score_scale
        )
        return ((key_total, value_total), grad_query.astype(half))

    zero_heads = jnp.zeros((token_count, HEADS, head_dim), single)
    (key_total, value_total), grad_query_blocks = lax.scan(
        attend_back, (zero_heads, zero_heads), jnp.arange(block_count, dtype=jnp.int32)
    )
    grad_qkv = jnp.concatenate(
        [
            grad_query_blocks.reshape(token_count, model_width),
            key_total.reshape(token_count, model_width).astype(half),
            value_total.reshape(token_count, model_width).astype(half),
        ],
        axis=1,
    )
    qkv_local = contract_rows(hidden_a, grad_qkv)
    grad_hidden_a = contract_cols(grad_qkv, w_qkv)
    grad_in_n, pre_gain_local, pre_shift_local = pre_back(grad_hidden_a)
    input_grad = (grad_resid + grad_in_n).astype(half)
    summed = (
        lax.psum_scatter(qkv_local, ("expert", "hid"), scatter_dimension=0, tiled=True),
        lax.psum_scatter(proj_local, ("expert", "hid"), scatter_dimension=0, tiled=True),
        lax.psum_scatter(router_local, ("expert", "hid"), scatter_dimension=0, tiled=True),
        lax.psum_scatter(pre_gain_local, ("expert", "hid"), scatter_dimension=0, tiled=True),
        lax.psum_scatter(pre_shift_local, ("expert", "hid"), scatter_dimension=0, tiled=True),
        lax.psum_scatter(mid_gain_local, ("expert", "hid"), scatter_dimension=0, tiled=True),
        lax.psum_scatter(mid_shift_local, ("expert", "hid"), scatter_dimension=0, tiled=True),
    )
    (
        qkv_grad,
        proj_grad,
        router_grad,
        pre_gain_grad,
        pre_shift_grad,
        mid_gain_grad,
        mid_shift_grad,
    ) = summed
    return (
        layer_output,
        balance_loss,
        input_grad,
        qkv_grad,
        proj_grad,
        router_grad,
        pre_gain_grad,
        pre_shift_grad,
        mid_gain_grad,
        mid_shift_grad,
        in_grad[None],
        down_grad[None],
    )


def solution(mesh):
    in_specs = (
        P(("expert", "hid"), None),
        P(("expert", "hid"), None),
        P(("expert", "hid"), None),
        P(("expert", "hid"), None),
        P(("expert", "hid"), None),
        P(("expert", "hid")),
        P(("expert", "hid")),
        P(("expert", "hid")),
        P(("expert", "hid")),
        P("expert", None, "hid"),
        P("expert", "hid", None),
        P(("expert", "hid")),
    )
    out_specs = (
        P(("expert", "hid"), None),
        P(),
        P(("expert", "hid"), None),
        P(("expert", "hid"), None),
        P(("expert", "hid"), None),
        P(("expert", "hid"), None),
        P(("expert", "hid")),
        P(("expert", "hid")),
        P(("expert", "hid")),
        P(("expert", "hid")),
        P("expert", None, "hid"),
        P("expert", "hid", None),
    )
    return jax.shard_map(
        on_device, mesh=mesh, in_specs=in_specs, out_specs=out_specs, check_vma=False
    )
```

```python
import functools

import jax
import jax.numpy as jnp
from jax import lax
from jax.experimental import pallas as pl
from jax.experimental.pallas import tpu as pltpu
from jax.sharding import PartitionSpec as P

epsilon = 1e-05
balance_weight = 3.0
masked_score = -1000000000.0
MESH = pl.DeviceIdType.MESH
half = jnp.bfloat16
single = jnp.float32


def remote(src, dst, send_sem, recv_sem, device):
    return pltpu.make_async_remote_copy(
        src_ref=src, dst_ref=dst, send_sem=send_sem, recv_sem=recv_sem,
        device_id=device, device_id_type=MESH,
    )


def dot(a, b):
    return jnp.dot(a, b, preferred_element_type=single)


def dot_cols(a, b):
    return lax.dot_general(a, b, (((1,), (1,)), ((), ())), preferred_element_type=single)


def dot_rows(a, b):
    return lax.dot_general(a, b, (((0,), (0,)), ((), ())), preferred_element_type=single)


def expert_kernel(
    E, X, G, out_h, out_g, w_in, w_dn, ret_o, ret_g, in_grad, dn_grad,
    xh, xg, win, wdn, act, gbef, po, pg, so, sg, ro, rg, to, tg, gs, gr, before, ga,
    send_a, recv_a, send_x, recv_x, send_p, recv_p, send_r, recv_r, send_w, recv_w, send_d, recv_d,
):
    e = lax.axis_index("expert")
    h = lax.axis_index("hid")
    x = lax.div(h, 2)
    c = lax.rem(h, 2)
    other = 1 - c
    D = w_in.shape[0]
    Fq = w_in.shape[1]
    cap = out_h.shape[1]
    NG = E // G
    rows = G * cap
    core_peer = (e, x * 2 + other)

    def expert_peer(k):
        return (lax.rem(e + k, E), h)

    def x_peer(d):
        return (e, lax.rem(x + d, X) * 2 + c)

    barrier = pltpu.get_barrier_semaphore()

    @pl.loop(1, E)
    def _(k):
        pl.semaphore_signal(barrier, inc=1, device_id=expert_peer(k), device_id_type=MESH)

    for d in range(1, X):
        pl.semaphore_signal(barrier, inc=1, device_id=x_peer(d), device_id_type=MESH)
    pl.semaphore_signal(barrier, inc=1, device_id=core_peer, device_id_type=MESH)
    pl.semaphore_wait(barrier, E - 1 + X - 1 + 1)

    def dispatch(k, part):
        to_e = lax.rem(e + E - k, E)
        src, dst = ((out_h, xh), (out_g, xg))[part]
        return remote(src.at[to_e], dst.at[0, k], send_a.at[part, k], recv_a.at[part, k], (to_e, h))

    def forward(k, part, d):
        dst = (xh, xg)[part]
        return remote(
            dst.at[0, k], dst.at[X - d, k], send_x.at[part, d - 1, k], recv_x.at[part, X - d - 1, k],
            x_peer(d),
        )

    @pl.loop(1, E)
    def _(k):
        dispatch(k, 0).start()
        dispatch(k, 1).start()

    xh[0, 0] = out_h[e]
    xg[0, 0] = out_g[e]

    step = 32

    @pl.loop(0, D // step)
    def _(i):
        at = pl.ds(pl.multiple_of(i * step, step), step)
        win[c, at, :] = w_in[at, :].astype(half)

    @pl.loop(0, Fq // step)
    def _(i):
        at = pl.ds(pl.multiple_of(i * step, step), step)
        wdn[c, at, :] = w_dn[at, :].astype(half)

    win_copy = remote(win.at[c], win.at[c], send_w.at[0], recv_w.at[0], core_peer)
    wdn_copy = remote(wdn.at[c], wdn.at[c], send_w.at[1], recv_w.at[1], core_peer)
    win_copy.start()
    wdn_copy.start()

    def pass_on(g):
        @pl.loop(0, G)
        def _(i):
            k = g * G + i

            @pl.when(k > 0)
            def _():
                dispatch(k, 0).wait_recv()
                dispatch(k, 1).wait_recv()

            for d in range(1, X):
                forward(k, 0, d).start()
                forward(k, 1, d).start()

    def take(j, g):
        @pl.loop(0, G)
        def _(i):
            k = g * G + i
            forward(k, 0, X - j).wait_recv()
            forward(k, 1, X - j).wait_recv()

    def compute(j, g):
        slots = pl.ds(g * G, G)
        t = j * NG + g
        xh_g = xh[j, slots].reshape(rows, D)
        xg_g = xg[j, slots].reshape(rows, D)
        for q in range(2):
            before[...] = dot(xh_g, win[q])
            ga[...] = dot_cols(xg_g, wdn[q])

            @pl.loop(0, rows // step)
            def _(i):
                at = pl.ds(pl.multiple_of(i * step, step), step)
                v = before[at, :]
                cdf = 0.5 * (1.0 + lax.erf(v * (0.5 ** 0.5)))
                slope = cdf + v * (jnp.exp(-0.5 * v * v) * 0.3989422804014327)
                act[q, t, at, :] = (v * cdf).astype(half)
                gbef[q, t, at, :] = (slope * ga[at, :]).astype(half)

        out = dot(act[0, t], wdn[0]) + dot(act[1, t], wdn[1])
        gin = dot_cols(gbef[0, t], win[0]) + dot_cols(gbef[1, t], win[1])
        return out, gin

    def partial(j, g, part):
        src, dst = ((so, ro), (sg, rg))[part]
        return remote(
            src.at[j - 1, pl.ds(g * G, G)], dst.at[X - j - 1, pl.ds(g * G, G)],
            send_p.at[part, j - 1, g], recv_p.at[part, X - j - 1, g], x_peer(j),
        )

    def give_back(k, part):
        src, dst = ((to, ret_o), (tg, ret_g))[part]
        return remote(src.at[k], dst.at[e], send_r.at[part, k], recv_r.at[part, k], expert_peer(k))

    def finish(g):
        for j in range(1, X):
            for part in range(2):
                partial(X - j, g, part).wait_recv()

        @pl.loop(0, G)
        def _(i):
            k = g * G + i
            for part, own, got, total in ((0, po, ro, to), (1, pg, rg, tg)):
                value = own[k]
                for j in range(X - 1):
                    value = value + got[j, k].astype(single)
                total[k] = value.astype(half)

            @pl.when(k > 0)
            def _():
                give_back(k, 0).start()
                give_back(k, 1).start()

            @pl.when(k == 0)
            def _():
                ret_o[e] = to[0]
                ret_g[e] = tg[0]

    @pl.loop(0, NG * X)
    def _(t):
        g = lax.div(t, X)
        j = lax.rem(t, X)

        @pl.when(j == 0)
        def _():
            pass_on(g)

        for d in range(1, X):
            @pl.when(j == d)
            def _():
                take(d, g)

        @pl.when(t == 0)
        def _():
            win_copy.wait_recv()
            wdn_copy.wait_recv()

        out, gin = compute(j, g)
        slots = pl.ds(g * G, G)

        @pl.when(j == 0)
        def _():
            po[slots] = out.reshape(G, cap, D)
            pg[slots] = gin.reshape(G, cap, D)

        for d in range(1, X):
            @pl.when(j == d)
            def _():
                so[d - 1, slots] = out.astype(half).reshape(G, cap, D)
                sg[d - 1, slots] = gin.astype(half).reshape(G, cap, D)
                partial(d, g, 0).start()
                partial(d, g, 1).start()

        @pl.when((j == 0) & (g > 0))
        def _():
            finish(g - 1)

    finish(NG - 1)

    T = X * NG * rows
    tile = 256 if Fq % 256 == 0 else 128

    def grad_in(q, i):
        lhs = xh[:, :, :, pl.ds(pl.multiple_of(i * tile, tile), tile)].reshape(T, tile)
        return dot_rows(lhs, gbef[q].reshape(T, Fq))

    def grad_dn(q, i):
        lhs = act[q, :, :, pl.ds(pl.multiple_of(i * tile, tile), tile)].reshape(T, tile)
        return dot_rows(lhs, xg[...].reshape(T, D))

    @pl.loop(0, D // tile)
    def _(i):
        gs[0, pl.ds(pl.multiple_of(i * tile, tile), tile), :Fq] = grad_in(other, i)

    in_copy = remote(gs.at[0, :, :Fq], gr.at[0, :, :Fq], send_d.at[0], recv_d.at[0], core_peer)
    in_copy.start()

    @pl.loop(0, Fq // tile)
    def _(i):
        gs[1, pl.ds(pl.multiple_of(i * tile, tile), tile), :] = grad_dn(other, i)

    dn_copy = remote(gs.at[1, :Fq], gr.at[1, :Fq], send_d.at[1], recv_d.at[1], core_peer)
    dn_copy.start()

    @pl.loop(0, D // tile)
    def _(i):
        in_grad[pl.ds(pl.multiple_of(i * tile, tile), tile), :] = grad_in(c, i)

    @pl.loop(0, Fq // tile)
    def _(i):
        dn_grad[pl.ds(pl.multiple_of(i * tile, tile), tile), :] = grad_dn(c, i)

    in_copy.wait_recv()

    @pl.loop(0, D // step)
    def _(i):
        at = pl.ds(pl.multiple_of(i * step, step), step)
        in_grad[at, :] += gr[0, at, :Fq]

    dn_copy.wait_recv()

    @pl.loop(0, Fq // step)
    def _(i):
        at = pl.ds(pl.multiple_of(i * step, step), step)
        dn_grad[at, :] += gr[1, at, :]

    win_copy.wait_send()
    wdn_copy.wait_send()
    in_copy.wait_send()
    dn_copy.wait_send()

    @pl.loop(0, E)
    def _(k):
        for part in range(2):
            @pl.when(k > 0)
            def _():
                dispatch(k, part).wait_send()
                give_back(k, part).wait()

            for d in range(1, X):
                forward(k, part, d).wait_send()

    for g in range(NG):
        for part in range(2):
            for j in range(1, X):
                partial(j, g, part).wait_send()


def expert_call(out_h, out_g, w_in, w_dn, X):
    E, cap, D = out_h.shape
    Fq = w_in.shape[1]
    G = max(1, min(E, 256 // cap))
    NG = E // G
    rows = G * cap
    dma = pltpu.SemaphoreType.DMA
    token = jax.ShapeDtypeStruct((E, cap, D), half)
    vmem = pl.BlockSpec(memory_space=pltpu.VMEM)
    return pl.pallas_call(
        functools.partial(expert_kernel, E, X, G),
        out_shape=(
            token, token,
            jax.ShapeDtypeStruct((D, Fq), single), jax.ShapeDtypeStruct((Fq, D), single),
        ),
        in_specs=[vmem] * 4,
        out_specs=(vmem,) * 4,
        scratch_shapes=[
            pltpu.VMEM((X, E, cap, D), half), pltpu.VMEM((X, E, cap, D), half),
            pltpu.VMEM((2, D, Fq), half), pltpu.VMEM((2, Fq, D), half),
            pltpu.VMEM((2, X * NG, rows, Fq), half), pltpu.VMEM((2, X * NG, rows, Fq), half),
            pltpu.VMEM((E, cap, D), single), pltpu.VMEM((E, cap, D), single),
            pltpu.VMEM((X - 1, E, cap, D), half), pltpu.VMEM((X - 1, E, cap, D), half),
            pltpu.VMEM((X - 1, E, cap, D), half), pltpu.VMEM((X - 1, E, cap, D), half),
            pltpu.VMEM((E, cap, D), half), pltpu.VMEM((E, cap, D), half),
            pltpu.VMEM((2, D, D), single), pltpu.VMEM((2, D, D), single),
            pltpu.VMEM((rows, Fq), single), pltpu.VMEM((rows, Fq), single),
            dma((2, E)), dma((2, E)),
            dma((2, X - 1, E)), dma((2, X - 1, E)),
            dma((2, X - 1, NG)), dma((2, X - 1, NG)),
            dma((2, E)), dma((2, E)),
            dma((2,)), dma((2,)), dma((2,)), dma((2,)),
        ],
        compiler_params=pltpu.CompilerParams(
            collective_id=1, has_side_effects=True, vmem_limit_bytes=60 * 1024 * 1024,
        ),
        name="experts",
    )(out_h, out_g, w_in, w_dn)


HEAD_DIM = 64
LANES = 128


def norm_stats(values):
    average = jnp.mean(values, axis=-1, keepdims=True)
    centred = values - average
    spread = jnp.mean(centred * centred, axis=-1, keepdims=True)
    return centred, lax.rsqrt(spread + epsilon)


def norm_back(grad, values, gain):
    centred, rate = norm_stats(values)
    unit = centred * rate
    scaled = grad * gain
    toward = rate * (
        scaled
        - jnp.mean(scaled, axis=-1, keepdims=True)
        - unit * jnp.mean(scaled * unit, axis=-1, keepdims=True)
    )
    gain_grad = jnp.sum(grad * unit, axis=0, keepdims=True)
    shift_grad = jnp.sum(grad, axis=0, keepdims=True)
    return toward, gain_grad, shift_grad


def iota(shape, axis):
    return lax.broadcasted_iota(jnp.int32, shape, axis)


def slot_places(assign, capacity):
    T = assign.shape[1]
    down, across = iota((T, T), 0), iota((T, T), 1)
    column = jnp.sum(jnp.where(down == across, assign, 0.0), axis=1, keepdims=True)
    same = column == assign
    rank_column = jnp.sum(jnp.where(same & (across < down), 1.0, 0.0), axis=1, keepdims=True)
    rank_row = jnp.sum(jnp.where(same & (down < across), 1.0, 0.0), axis=0, keepdims=True)
    place_column = (column * capacity + rank_column).astype(jnp.int32)
    place_row = (assign * capacity + rank_row).astype(jnp.int32)
    return column.astype(jnp.int32), place_column, place_row


def head_probs(q_one, k_pair, allowed):
    scores = dot_cols(q_one, k_pair) * (HEAD_DIM ** -0.5)
    scores = jnp.where(allowed, scores, masked_score)
    powers = jnp.exp(scores - jnp.max(scores, axis=-1, keepdims=True))
    return powers * (1.0 / jnp.sum(powers, axis=-1, keepdims=True))


def head_masks(T):
    first = iota((T, LANES), 1) < HEAD_DIM
    low_lanes = jnp.where(first, 1.0, 0.0).astype(half)
    high_lanes = jnp.where(first, 0.0, 1.0).astype(half)
    return first, (low_lanes, high_lanes)


def forward_body(E, tokens, cotangent, assign, wts, small, hid_a, qkv, att, resid, hid_b, probs, out_h, out_g):
    T, D = tokens.shape
    cap = out_h.shape[1]
    small_t = small[...].astype(single).T
    inputs = tokens[...].astype(single)
    centred, rate = norm_stats(inputs)
    hid_a[...] = (centred * rate * small_t[E : E + 1] + small_t[E + 1 : E + 2]).astype(half)
    for m in range(3):
        qkv[m] = dot(hid_a[...], wts[m]).astype(half)
    allowed = iota((T, T), 1) <= iota((T, T), 0)
    first, masks = head_masks(T)

    @pl.loop(0, D // LANES)
    def _(p):
        at = pl.ds(pl.multiple_of(p * LANES, LANES), LANES)
        q_pair, k_pair, v_pair = qkv[0, :, at], qkv[1, :, at], qkv[2, :, at]
        mixed = [
            dot(head_probs(q_pair * mask, k_pair, allowed).astype(half), v_pair) for mask in masks
        ]
        att[:, at] = jnp.where(first, mixed[0], mixed[1]).astype(half)

    resid[...] = inputs + dot(att[...], wts[3])
    centred, rate = norm_stats(resid[...])
    hid_b[...] = (centred * rate * small_t[E + 2 : E + 3] + small_t[E + 3 : E + 4]).astype(half)
    lane = iota((T, LANES), 1)
    logits = jnp.where(lane < E, dot(hid_b[...], small[...]), -1e30)
    powers = jnp.exp(logits - jnp.max(logits, axis=-1, keepdims=True))
    chance = powers * (1.0 / jnp.sum(powers, axis=-1, keepdims=True))
    probs[...] = chance
    column, _, place_row = slot_places(assign[...], cap)
    gate = jnp.sum(jnp.where(lane == column, chance, 0.0), axis=1, keepdims=True)
    pick = jnp.where(iota((E * cap, T), 0) == place_row, 1.0, 0.0).astype(half)
    out_h[...] = dot(pick, hid_b[...]).astype(half).reshape(E, cap, D)
    grad_expert = (gate * cotangent[...].astype(single)).astype(half)
    out_g[...] = dot(pick, grad_expert).astype(half).reshape(E, cap, D)


def backward_body(
    E, total_tokens, tokens, cotangent, assign, small, counts, proj_w, resid, hid_b, probs, qkv, ret_o, ret_g,
    layer_out, grad_res, gall, gatt, router_grad,
):
    T, D = tokens.shape
    cap = ret_o.shape[1]
    small_t = small[...].astype(single).T
    cot = cotangent[...].astype(single)
    column, place_column, _ = slot_places(assign[...], cap)
    lane = iota((T, LANES), 1)
    chance = probs[...]
    mine = lane == column
    gate = jnp.sum(jnp.where(mine, chance, 0.0), axis=1, keepdims=True)
    pick = jnp.where(iota((T, E * cap), 1) == place_column, 1.0, 0.0).astype(half)
    expert_tok = dot(pick, ret_o[...].reshape(E * cap, D))
    layer_out[...] = (resid[...] + gate * expert_tok).astype(half)
    grad_gate = jnp.sum(cot * expert_tok, axis=1, keepdims=True)
    scale = counts * (balance_weight * E / total_tokens)
    grad_probs = jnp.where(mine, grad_gate, 0.0) + scale
    grad_logits = chance * (grad_probs - jnp.sum(chance * grad_probs, axis=1, keepdims=True))
    grad_logits = jnp.where(lane < E, grad_logits, 0.0).astype(half)
    router_grad[...] = dot_rows(hid_b[...], grad_logits)
    grad_hidden_b = dot(pick, ret_g[...].reshape(E * cap, D)) + dot_cols(grad_logits, small[...])
    toward, mid_gain, mid_shift = norm_back(grad_hidden_b, resid[...], small_t[E + 2 : E + 3])
    grad_res[...] = cot + toward
    gall[3] = grad_res[...].astype(half)
    gatt[...] = dot_cols(gall[3], proj_w).astype(half)
    allowed = iota((T, T), 1) <= iota((T, T), 0)
    first, masks = head_masks(T)

    @pl.loop(0, D // LANES)
    def _(p):
        at = pl.ds(pl.multiple_of(p * LANES, LANES), LANES)
        q_pair, k_pair, v_pair, g_pair = qkv[0, :, at], qkv[1, :, at], qkv[2, :, at], gatt[:, at]
        found = []
        for mask in masks:
            weights = head_probs(q_pair * mask, k_pair, allowed)
            grad_w = dot_cols(g_pair * mask, v_pair)
            grad_s = weights * (grad_w - jnp.sum(weights * grad_w, axis=-1, keepdims=True))
            grad_s = grad_s.astype(half)
            found.append(
                (
                    dot(grad_s, k_pair) * (HEAD_DIM ** -0.5),
                    dot_rows(grad_s, q_pair) * (HEAD_DIM ** -0.5),
                    dot_rows(weights.astype(half), g_pair),
                )
            )
        for m in range(3):
            gall[m, :, at] = jnp.where(first, found[0][m], found[1][m]).astype(half)

    return mid_gain, mid_shift


def input_body(E, tokens, small, wts, gall, grad_res, input_grad):
    small_t = small[...].astype(single).T
    grad_hidden_a = dot_cols(gall[0], wts[0]) + dot_cols(gall[1], wts[1]) + dot_cols(gall[2], wts[2])
    toward, pre_gain, pre_shift = norm_back(
        grad_hidden_a, tokens[...].astype(single), small_t[E : E + 1]
    )
    input_grad[...] = (grad_res[...] + toward).astype(half)
    return pre_gain, pre_shift


def small_grads(E, router, rows, chance_sum, block, D):
    lane = iota((D, LANES), 1)
    eight = iota((LANES, D), 0)
    stacked = jnp.zeros((LANES, D), single)
    for i, row in enumerate(rows):
        stacked = jnp.where(eight == E + i, row, stacked)
    packed = jnp.where(lane < E, router, stacked.T)
    if block:
        place = lax.rem(iota((D, LANES), 0), block)
        copy = jnp.sum(jnp.where(place == lane, chance_sum, 0.0), axis=1, keepdims=True)
        packed = jnp.where(lane == E + 4, copy, packed)
    return packed


class Place:
    def __init__(self, E):
        e, h = lax.axis_index("expert"), lax.axis_index("hid")
        self.Z = E // 2
        self.z, self.y = lax.div(e, 2), lax.rem(e, 2)
        self.x, self.c = lax.div(h, 2), lax.rem(h, 2)

    def device(self, z, y, x, c):
        return (z * 2 + y, x * 2 + c)

    def z_at(self, d):
        return lax.rem(self.z + d, self.Z)

    def z_peer(self, d):
        return self.device(self.z_at(d), self.y, self.x, self.c)

    def y_peer(self):
        return self.device(self.z, 1 - self.y, self.x, self.c)

    def x_peer(self):
        return self.device(self.z, self.y, 1 - self.x, self.c)

    def core_peer(self):
        return self.device(self.z, self.y, self.x, 1 - self.c)

    def z_steps(self):
        return sorted(range(1, self.Z), key=lambda d: min(d, self.Z - d))

    def greet(self):
        barrier = pltpu.get_barrier_semaphore()
        peers = [self.z_peer(d) for d in range(1, self.Z)]
        peers += [self.y_peer(), self.x_peer(), self.core_peer()]
        for peer in peers:
            pl.semaphore_signal(barrier, inc=1, device_id=peer, device_id_type=MESH)
        pl.semaphore_wait(barrier, len(peers))


def chip_index(z, y, x):
    return (z * 2 + y) * 2 + x


class Sends:
    def __init__(self, sems):
        self.sems, self.started = sems, []

    def start(self, src, dst, recv_sem, device):
        copy = remote(src, dst, self.sems.at[len(self.started)], recv_sem, device)
        copy.start()
        self.started.append(copy)

    def finish(self):
        for copy in self.started:
            copy.wait_send()


def arrive(dst, send_sem, recv_sem, device):
    remote(dst, dst, send_sem, recv_sem, device).wait_recv()


def gather_weights(at, sends, shard, small_shard, other, other_small, wts, small, recv, recv_own):
    Z, z, y, x, c = at.Z, at.z, at.y, at.x, at.c
    rows, D = shard.shape[1], shard.shape[2]
    core = at.core_peer()
    mine, theirs = 2 * c, 2 * (1 - c)
    for o in range(2):
        sends.start(shard.at[theirs + o], other.at[o], recv_own.at[o], core)
    sends.start(small_shard, other_small, recv_own.at[2], core)
    span = 2 * rows

    def rows_of(chip):
        return pl.ds(pl.multiple_of(chip * span, span), span)

    def block(o, chip):
        return small.at[rows_of(chip), :] if o == 2 else wts.at[mine + o, rows_of(chip), :]

    def send(o, chip, device):
        sends.start(block(o, chip), block(o, chip), recv.at[o, chip], device)

    def share(o, chip):
        if o < 2:
            sends.start(block(o, chip), block(o, chip), recv.at[3 + o, chip], core)

    def wait(o, chip):
        arrive(block(o, chip), sends.sems.at[0], recv.at[o, chip], core)

    own = chip_index(z, y, x)
    for o, there in ((2, other_small), (0, other.at[0]), (1, other.at[1])):
        arrive(there, sends.sems.at[0], recv_own.at[o], core)
        here = small_shard[...] if o == 2 else shard[mine + o]
        got = there[...]
        low = jnp.where(c == 0, here, got)
        high = jnp.where(c == 0, got, here)
        both = jnp.concatenate([low, high], axis=0).astype(half)
        if o == 2:
            small[rows_of(own), :] = both
        else:
            wts[mine + o, rows_of(own), :] = both
        if o == 1:
            send(o, own, at.x_peer())
        for d in at.z_steps():
            send(o, own, at.z_peer(d))
        send(o, own, at.y_peer())
        if o != 1:
            send(o, own, at.x_peer())
    share(0, own)
    share(1, own)
    wait(1, chip_index(z, y, 1 - x))
    for d in at.z_steps():
        send(1, chip_index(z, y, 1 - x), at.z_peer(d))
    send(1, chip_index(z, y, 1 - x), at.y_peer())
    share(1, chip_index(z, y, 1 - x))
    for d in at.z_steps():
        for o in (2, 0):
            chip = chip_index(at.z_at(d), y, x)
            wait(o, chip)
            send(o, chip, at.y_peer())
            send(o, chip, at.x_peer())
            share(o, chip)
        for there in (x, 1 - x):
            chip = chip_index(at.z_at(d), y, there)
            wait(1, chip)
            send(1, chip, at.y_peer())
            share(1, chip)
    for d in [0] + at.z_steps():
        for o in (2, 0):
            chip = chip_index(at.z_at(d), 1 - y, x)
            wait(o, chip)
            send(o, chip, at.x_peer())
            share(o, chip)
        for there in (x, 1 - x):
            chip = chip_index(at.z_at(d), 1 - y, there)
            wait(1, chip)
            share(1, chip)
    for d in [0] + at.z_steps():
        for there in (y, 1 - y):
            for o in (2, 0):
                chip = chip_index(at.z_at(d), there, 1 - x)
                wait(o, chip)
                share(o, chip)

    def wait_shared():
        for o in range(2):
            for chip in range(4 * Z):
                theirs_block = wts.at[theirs + o, rows_of(chip), :]
                arrive(theirs_block, sends.sems.at[0], recv.at[3 + o, chip], core)

    return wait_shared


class SumScatter:
    def __init__(self, at, sends, acc, give, got, sent, came, final, other, recv):
        self.at, self.sends = at, sends
        self.acc, self.give, self.got, self.sent, self.came = acc, give, got, sent, came
        self.final, self.other, self.recv = final, other, recv
        self.span = final.shape[1]

    def rows_of(self, chip):
        return pl.ds(pl.multiple_of(chip * self.span, self.span), self.span)

    def swap(self, o):
        self.sends.start(self.give.at[o], self.got.at[o], self.recv.at[o, 0], self.at.core_peer())

    def wait_swap(self, o):
        arrive(self.got.at[o], self.sends.sems.at[0], self.recv.at[o, 0], self.at.core_peer())

    def send(self, o, slot, value, device):
        self.sent[o, slot] = value.astype(half)
        self.sends.start(self.sent.at[o, slot], self.came.at[o, slot], self.recv.at[o, 1 + slot], device)

    def take(self, o, slot):
        arrive(
            self.came.at[o, slot], self.sends.sems.at[0], self.recv.at[o, 1 + slot], self.at.core_peer()
        )
        return self.came[o, slot].astype(single)

    def base(self, o, chip):
        rows = self.rows_of(chip)
        return self.acc[o, rows, :] + self.got[o, rows, :].astype(single)

    def one(self, o):
        at = self.at
        for dz in range(at.Z):
            for b in range(2):
                z = at.z_at(dz)
                if o == 0:
                    chip, device = chip_index(z, b, 1 - at.x), at.x_peer()
                else:
                    chip, device = chip_index(z, 1 - at.y, b), at.y_peer()
                self.send(o, dz * 2 + b, self.base(o, chip), device)

    def two(self, o):
        at = self.at
        first = 2 * at.Z
        if o == 0:
            for dz in range(at.Z):
                for flip in (1, 0):
                    y = 1 - at.y if flip else at.y
                    chip = chip_index(at.z_at(dz), y, at.x)
                    value = self.base(o, chip)
                    value = value + self.pick(o, dz * 2, y)
                    if flip:
                        self.send(o, first + dz, value, at.y_peer())
                    else:
                        self.acc[o, self.rows_of(chip), :] = value
        else:
            for dz in at.z_steps() + [0]:
                for b in range(2):
                    chip = chip_index(at.z_at(dz), at.y, b)
                    value = self.base(o, chip) + self.take(o, dz * 2 + b)
                    if dz:
                        self.send(o, first + dz * 2 + b, value, at.z_peer(dz))
                    else:
                        self.acc[o, self.rows_of(chip), :] = value

    def pick(self, o, slot, index):
        place = slot + index
        arrive(
            self.came.at[o, place], self.sends.sems.at[0], self.recv.at[o, 1 + place], self.at.core_peer()
        )
        return self.came[o, place].astype(single)

    def three(self, o):
        at = self.at
        first = 2 * at.Z
        if o == 0:
            second = first + at.Z
            for dz in at.z_steps() + [0]:
                rows = self.rows_of(chip_index(at.z_at(dz), at.y, at.x))
                value = self.acc[o, rows, :] + self.take(o, first + dz)
                if dz:
                    self.send(o, second + dz, value, at.z_peer(dz))
                else:
                    self.final[o] = value
        else:
            second = first + 2 * at.Z
            for flip in (1, 0):
                x = 1 - at.x if flip else at.x
                value = self.acc[o, self.rows_of(chip_index(at.z, at.y, x)), :]
                for dz in range(1, at.Z):
                    value = value + self.pick(o, first + dz * 2, x)
                if flip:
                    self.send(o, second, value, at.x_peer())
                else:
                    self.final[o] = value

    def four(self, o):
        at = self.at
        if o == 0:
            second = 2 * at.Z + at.Z
            for dz in range(1, at.Z):
                self.final[o] += self.take(o, second + dz)
        else:
            self.final[o] += self.take(o, 2 * at.Z + 2 * at.Z)
        rows = self.span // 2
        last = self.recv.shape[1] - 1
        there = self.final.at[o, pl.ds(pl.multiple_of((1 - at.c) * rows, rows), rows), :]
        self.sends.start(there, self.other.at[o], self.recv.at[o, last], at.core_peer())

    def end(self, o):
        last = self.recv.shape[1] - 1
        arrive(self.other.at[o], self.sends.sems.at[0], self.recv.at[o, last], self.at.core_peer())


def start_kernel(E, fused, *refs):
    if fused:
        (tokens, cotangent, assign, qkv_shard, proj_shard, small_in,
         out_h, out_g, wts, small, counts, hid_a, qkv, att, resid, hid_b, probs,
         shard, small_shard, other, other_small, send, recv, recv_own) = refs
        rows, D = proj_shard.shape
        at = Place(E)
        at.greet()
        for m in range(3):
            shard[m] = qkv_shard[:, m * D : (m + 1) * D]
        shard[3] = proj_shard[...]
        numbers = iota((rows, tokens.shape[0]), 0).astype(single)
        count = jnp.sum(jnp.where(assign[...] == numbers, 1.0, 0.0), axis=1, keepdims=True)
        small_shard[...] = jnp.where(iota((rows, LANES), 1) == E + 4, count, small_in[...])
        sends = Sends(send)
        wait_shared = gather_weights(
            at, sends, shard, small_shard, other, other_small, wts, small, recv, recv_own
        )
        wait_shared()
        place = lax.rem(iota((D, LANES), 0), rows)
        column = small[:, E + 4 : E + 5].astype(single)
        total = jnp.sum(jnp.where(place == iota((D, LANES), 1), column, 0.0), axis=0, keepdims=True)
        counts[...] = jnp.broadcast_to(total, counts.shape)
    else:
        (tokens, cotangent, assign, wts, small, out_h, out_g, hid_a, qkv, att, resid, hid_b, probs) = refs
    forward_body(
        E, tokens, cotangent, assign, wts, small, hid_a, qkv, att, resid, hid_b, probs, out_h, out_g
    )
    if fused:
        sends.finish()


def end_kernel(E, total_tokens, fused, *refs):
    (tokens, cotangent, assign, wts, small, counts, hid_a, qkv, att, resid, hid_b, probs, ret_o, ret_g,
     layer_out, input_grad) = refs[:16]
    T, D = tokens.shape
    if fused:
        (qkv_grad, proj_grad, small_out, gall, gatt, grad_res, router_grad,
         acc, give, got, sent, came, final, other,
         pack, pack_other, pack_sent, pack_came, send, recv, pack_recv) = refs[16:]
        at = Place(E)
        at.greet()
    else:
        weight_grads, small_out, gall, gatt, grad_res, router_grad = refs[16:]
    mid_gain, mid_shift = backward_body(
        E, total_tokens, tokens, cotangent, assign, small, counts[0:1], wts[3], resid, hid_b, probs, qkv,
        ret_o, ret_g, layer_out, grad_res, gall, gatt, router_grad,
    )
    tile = 256 if D % 256 == 0 else LANES

    def fill(write, m):
        @pl.loop(0, D // tile)
        def _(i):
            cols = pl.ds(pl.multiple_of(i * tile, tile), tile)
            if isinstance(m, int):
                left = att[:, cols] if m == 3 else hid_a[:, cols]
            else:
                left = jnp.where(m == 3, att[:, cols].astype(single), hid_a[:, cols].astype(single))
                left = left.astype(half)
            write(cols, dot_rows(left, gall[m]))

    chance_sum = jnp.sum(probs[...], axis=0, keepdims=True)
    if not fused:
        for m in range(4):
            def write(cols, value):
                weight_grads[m, cols, :] = value
            fill(write, m)
        pre_gain, pre_shift = input_body(E, tokens, small, wts, gall, grad_res, input_grad)
        small_out[...] = small_grads(
            E, router_grad[...], (pre_gain, pre_shift, mid_gain, mid_shift), chance_sum, 0, D
        )
        return

    rows = proj_grad.shape[0]
    sends = Sends(send)
    sums = SumScatter(at, sends, acc, give, got, sent, came, final, other, recv)
    mine, theirs = 2 * at.c, 2 * (1 - at.c)
    for o in (1, 0):
        def write(cols, value):
            give[o, cols, :] = value.astype(half)
        fill(write, theirs + o)
        sums.swap(o)
    for o in (1, 0):
        def write(cols, value):
            acc[o, cols, :] = value
        fill(write, mine + o)
    for o in (1, 0):
        sums.wait_swap(o)
        sums.one(o)
    pre_gain, pre_shift = input_body(E, tokens, small, wts, gall, grad_res, input_grad)
    pack[...] = small_grads(
        E, router_grad[...], (pre_gain, pre_shift, mid_gain, mid_shift), chance_sum, rows, D
    )
    sends.start(pack, pack_other, pack_recv.at[0], at.core_peer())
    sums.two(1)
    sums.two(0)
    arrive(pack_other, send.at[0], pack_recv.at[0], at.core_peer())
    pack_other[...] += pack[...]

    def pack_rows(z, y, x):
        first = chip_index(z, y, x) * 2 * rows + at.c * rows
        return pl.ds(pl.multiple_of(first, rows), rows)

    def pack_send(slot, value, device):
        pack_sent[slot] = value
        sends.start(pack_sent.at[slot], pack_came.at[slot], pack_recv.at[1 + slot], device)

    def pack_take(slot):
        arrive(pack_came.at[slot], send.at[0], pack_recv.at[1 + slot], at.core_peer())
        return pack_came[slot]

    Z = at.Z
    for dz in range(Z):
        for y in range(2):
            pack_send(dz * 2 + y, pack_other[pack_rows(at.z_at(dz), y, 1 - at.x), :], at.x_peer())
    sums.three(1)
    sums.three(0)
    for dz in range(Z):
        for flip in (1, 0):
            y = 1 - at.y if flip else at.y
            here = pack_rows(at.z_at(dz), y, at.x)
            value = pack_other[here, :] + pack_take(dz * 2 + y)
            if flip:
                pack_send(2 * Z + dz, value, at.y_peer())
            else:
                pack_other[here, :] = value
    sums.four(1)
    sums.four(0)
    for dz in at.z_steps() + [0]:
        value = pack_other[pack_rows(at.z_at(dz), at.y, at.x), :] + pack_take(2 * Z + dz)
        if dz:
            pack_send(3 * Z + dz, value, at.z_peer(dz))
        else:
            total = value
    for dz in range(1, Z):
        total = total + pack_take(3 * Z + dz)
    lane = iota((rows, LANES), 1)
    scale = counts[0:1] * (balance_weight * E / total_tokens)
    chance = jnp.sum(jnp.where(lane == E + 4, total, 0.0), axis=1, keepdims=True)
    chosen = jnp.where((lane == iota((rows, LANES), 0)) & (lane < E), chance * scale, 0.0)
    loss = jnp.sum(jnp.sum(chosen, axis=1, keepdims=True), axis=0, keepdims=True) / total_tokens
    small_out[...] = jnp.where(lane == E + 5, loss, total)
    sums.end(1)
    sums.end(0)
    half_rows = pl.ds(pl.multiple_of(at.c * rows, rows), rows)

    def put(o_mine, o_other):
        for m, value in o_mine + o_other:
            if m == 3:
                proj_grad[...] = value
            else:
                qkv_grad[:, m * D : (m + 1) * D] = value

    @pl.when(at.c == 0)
    def _():
        put([(o, final[o, half_rows, :]) for o in range(2)], [(2 + o, other[o]) for o in range(2)])

    @pl.when(at.c == 1)
    def _():
        put([(2 + o, final[o, half_rows, :]) for o in range(2)], [(o, other[o]) for o in range(2)])

    sends.finish()


DMA = pltpu.SemaphoreType.DMA
VMEM_SPEC = pl.BlockSpec(memory_space=pltpu.VMEM)


def call(kernel, outs, scratch, collective, name, *args):
    if collective is None:
        params = pltpu.CompilerParams(vmem_limit_bytes=60 * 1024 * 1024)
    else:
        params = pltpu.CompilerParams(
            collective_id=collective, has_side_effects=True, vmem_limit_bytes=60 * 1024 * 1024
        )
    return pl.pallas_call(
        kernel,
        out_shape=tuple(jax.ShapeDtypeStruct(shape, kind) for shape, kind in outs),
        in_specs=[VMEM_SPEC] * len(args),
        out_specs=(VMEM_SPEC,) * len(outs),
        scratch_shapes=scratch,
        compiler_params=params,
        name=name,
    )(*args)


def on_device(
    tokens_in, out_cotangent, qkv_weight, proj_weight, router_weight, pre_gain, pre_shift, mid_gain, mid_shift,
    expert_in, expert_down, assignment,
):
    T, D = tokens_in.shape
    E, H = lax.axis_size("expert"), lax.axis_size("hid")
    X = H // 2
    Z = E // 2
    cap = 2 * T // E
    total_tokens = T * E * H
    rows = proj_weight.shape[0]
    both = ("expert", "hid")
    fused = X == 2 and E % 2 == 0 and rows % 8 == 0 and rows >= E
    assign = assignment.astype(single).reshape(1, T)
    columns = [v[:, None] for v in (pre_gain, pre_shift, mid_gain, mid_shift)]
    small_in = jnp.concatenate([router_weight] + columns, axis=1)
    small_in = jnp.pad(small_in, ((0, 0), (0, LANES - small_in.shape[1])))
    kept = [
        ((E, cap, D), half), ((E, cap, D), half),
    ]
    saved = [
        ((T, D), half), ((3, T, D), half), ((T, D), half), ((T, D), single), ((T, D), half), ((T, LANES), single),
    ]
    if fused:
        out_h, out_g, wts, small, counts, *rest = call(
            functools.partial(start_kernel, E, True),
            kept + [((4, D, D), half), ((D, LANES), half), ((8, LANES), single)] + saved,
            [
                pltpu.VMEM((4, rows, D), single), pltpu.VMEM((rows, LANES), single),
                pltpu.VMEM((2, rows, D), single), pltpu.VMEM((rows, LANES), single),
                DMA((20 * Z + 8,)), DMA((5, 4 * Z)), DMA((3,)),
            ],
            2, "start", tokens_in, out_cotangent, assign, qkv_weight, proj_weight, small_in,
        )
    else:
        shard = jnp.concatenate([qkv_weight, proj_weight], axis=1).astype(half)
        wts = lax.all_gather(shard, both, axis=0, tiled=True).reshape(D, 4, D).transpose(1, 0, 2)
        small = lax.all_gather(small_in.astype(half), both, axis=0, tiled=True)
        onehot = assignment[:, None] == jnp.arange(LANES, dtype=jnp.int32)[None, :]
        counts = lax.psum(jnp.sum(onehot.astype(single), axis=0), both)
        counts = jnp.broadcast_to(counts[None, :], (8, LANES))
        out_h, out_g, *rest = call(
            functools.partial(start_kernel, E, False), kept + saved, [], None, "start",
            tokens_in, out_cotangent, assign, wts, small,
        )
    hid_a, qkv, att, resid, hid_b, probs = rest
    ret_o, ret_g, in_grad, down_grad = expert_call(out_h, out_g, expert_in[0], expert_down[0], X)
    given = (
        tokens_in, out_cotangent, assign, wts, small, counts, hid_a, qkv, att, resid, hid_b, probs, ret_o, ret_g,
    )
    outs = [((T, D), half), ((T, D), half)]
    working = [
        pltpu.VMEM((4, T, D), half), pltpu.VMEM((T, D), half), pltpu.VMEM((T, D), single),
        pltpu.VMEM((D, LANES), single),
    ]
    if fused:
        slots = 4 * Z + 1
        layer_out, input_grad, qkv_grad, proj_grad, small_out = call(
            functools.partial(end_kernel, E, total_tokens, True),
            outs + [((rows, 3 * D), single), ((rows, D), single), ((rows, LANES), single)],
            working + [
                pltpu.VMEM((2, D, D), single), pltpu.VMEM((2, D, D), half), pltpu.VMEM((2, D, D), half),
                pltpu.VMEM((2, slots, 2 * rows, D), half), pltpu.VMEM((2, slots, 2 * rows, D), half),
                pltpu.VMEM((2, 2 * rows, D), single), pltpu.VMEM((2, rows, D), single),
                pltpu.VMEM((D, LANES), single), pltpu.VMEM((D, LANES), single),
                pltpu.VMEM((4 * Z, rows, LANES), single), pltpu.VMEM((4 * Z, rows, LANES), single),
                DMA((12 * Z + 8,)), DMA((2, slots + 2)), DMA((4 * Z + 1,)),
            ],
            3, "end", *given,
        )
        balance_loss = small_out[0, E + 5]
    else:
        layer_out, input_grad, weight_grads, packed = call(
            functools.partial(end_kernel, E, total_tokens, False),
            outs + [((4, D, D), single), ((D, LANES), single)], working, None, "end", *given,
        )
        gathered = weight_grads.transpose(1, 0, 2).reshape(D, 4 * D)
        gathered = lax.psum_scatter(gathered, both, scatter_dimension=0, tiled=True)
        qkv_grad, proj_grad = gathered[:, : 3 * D], gathered[:, 3 * D :]
        small_out = lax.psum_scatter(packed, both, scatter_dimension=0, tiled=True)
        chance = lax.psum(jnp.sum(probs, axis=0), both)
        balance_loss = jnp.sum(chance * counts[0]) * (balance_weight * E / total_tokens) / total_tokens
    grads = [small_out[:, E + i] for i in range(4)]
    return (
        layer_out, balance_loss, input_grad, qkv_grad, proj_grad, small_out[:, :E], *grads,
        in_grad[None], down_grad[None],
    )


def solution(mesh):
    in_specs = (
        P(("expert", "hid"), None),
        P(("expert", "hid"), None),
        P(("expert", "hid"), None),
        P(("expert", "hid"), None),
        P(("expert", "hid"), None),
        P(("expert", "hid")),
        P(("expert", "hid")),
        P(("expert", "hid")),
        P(("expert", "hid")),
        P("expert", None, "hid"),
        P("expert", "hid", None),
        P(("expert", "hid")),
    )
    out_specs = (
        P(("expert", "hid"), None),
        P(),
        P(("expert", "hid"), None),
        P(("expert", "hid"), None),
        P(("expert", "hid"), None),
        P(("expert", "hid"), None),
        P(("expert", "hid")),
        P(("expert", "hid")),
        P(("expert", "hid")),
        P(("expert", "hid")),
        P("expert", None, "hid"),
        P("expert", "hid", None),
    )
    return jax.shard_map(
        on_device, mesh=mesh, in_specs=in_specs, out_specs=out_specs, check_vma=False
    )
```

```python
import functools

import jax
import jax.numpy as jnp
from jax import lax
from jax.experimental import pallas as pl
from jax.experimental.pallas import tpu as pltpu
from jax.sharding import PartitionSpec as P

epsilon = 1e-05
balance_weight = 3.0
masked_score = -1000000000.0


MESH = pl.DeviceIdType.MESH
DMA = pltpu.SemaphoreType.DMA
VMEM_SPEC = pl.BlockSpec(memory_space=pltpu.VMEM)
ANY_SPEC = pl.BlockSpec(memory_space=pl.ANY)
half = jnp.bfloat16
single = jnp.float32
STEP = 32


def remote(src, dst, send_sem, recv_sem, device):
    return pltpu.make_async_remote_copy(
        src_ref=src, dst_ref=dst, send_sem=send_sem, recv_sem=recv_sem,
        device_id=device, device_id_type=MESH,
    )


def dot(a, b):
    return jnp.dot(a, b, preferred_element_type=single)


def dot_cols(a, b):
    return lax.dot_general(a, b, (((1,), (1,)), ((), ())), preferred_element_type=single)


def dot_rows(a, b):
    return lax.dot_general(a, b, (((0,), (0,)), ((), ())), preferred_element_type=single)


def steps(count, step):
    def run(body):
        @pl.loop(0, count // step)
        def _(i):
            body(pl.ds(pl.multiple_of(i * step, step), step))
    return run


class Named:
    def __init__(self, names, refs):
        self.__dict__.update(zip(names, refs, strict=True))


def expert_scratch(E, X, cap, D, Fq):
    P, token = 2 * X, (E, cap, D)
    return dict(
        xh=pltpu.VMEM(token, half), xg=pltpu.VMEM(token, half),
        win=pltpu.VMEM((P, D, Fq), half), wdn=pltpu.VMEM((P, Fq, D), half),
        act=pltpu.VMEM((P, E * cap, Fq), half), gbef=pltpu.VMEM((P, E * cap, Fq), half),
        to=pltpu.VMEM(token, half), tg=pltpu.VMEM(token, half), xh_t=pltpu.VMEM((D, E * cap), half),
        core_in=pltpu.VMEM((X, D, Fq), half), core_dn=pltpu.VMEM((X, Fq, D), half),
        xgate=pltpu.VMEM((E, 8, E * cap), single),
        send_a=DMA((3, E)), recv_a=DMA((3, E)), send_r=DMA((2, E)), recv_r=DMA((2, E)),
        send_w=DMA((2, X)), recv_w=DMA((2, X)), send_f=DMA((2, X)), recv_f=DMA((2, X)),
        send_d=DMA((2, X)), recv_d=DMA((2, X)), send_s=DMA((2, X)), recv_s=DMA((2, X)),
    )


class Experts:
    def __init__(self, E, X, G, r, gated):
        self.E, self.X, self.G, self.r, self.gated = E, X, G, r, gated
        self.e, self.h = lax.axis_index("expert"), lax.axis_index("hid")
        self.x, self.c = lax.div(self.h, 2), lax.rem(self.h, 2)
        self.cap, self.D = r.out_h.shape[1], r.out_h.shape[2]
        self.Fq = r.win.shape[2]
        self.NG, self.rows = E // G, G * self.cap
        self.core_peer = (self.e, self.x * 2 + 1 - self.c)

    def expert_at(self, k):
        found, bit = 0, 1
        while bit < self.E:
            a, b = lax.rem(lax.div(self.e, bit), 2), lax.rem(lax.div(k, bit), 2)
            found = found + bit * (a + b - 2 * a * b)
            bit *= 2
        return found

    def x_peer(self, d):
        return (self.e, lax.rem(self.x + d, self.X) * 2 + self.c)

    def part(self, j, core):
        return lax.rem(self.x + j, self.X) * 2 + core

    def greet(self):
        barrier = pltpu.get_barrier_semaphore()

        @pl.loop(1, self.E)
        def _(k):
            pl.semaphore_signal(
                barrier, inc=1, device_id=(self.expert_at(k), self.h), device_id_type=MESH
            )

        for d in range(1, self.X):
            pl.semaphore_signal(barrier, inc=1, device_id=self.x_peer(d), device_id_type=MESH)
        pl.semaphore_signal(barrier, inc=1, device_id=self.core_peer, device_id_type=MESH)
        pl.semaphore_wait(barrier, self.E - 1 + self.X - 1 + 1)

    def weight_to_x(self, i, d):
        r, w, q = self.r, (self.r.win, self.r.wdn)[i], self.part(0, self.c)
        return remote(
            w.at[q], w.at[q], r.send_w.at[i, d], r.recv_w.at[i, self.X - d], self.x_peer(d)
        )

    def weight_to_core(self, i, j, core):
        r, w, q = self.r, (self.r.win, self.r.wdn)[i], self.part(j, core)
        return remote(w.at[q], w.at[q], r.send_f.at[i, j], r.recv_f.at[i, j], self.core_peer)

    def share_weights(self, w_in, w_dn):
        r, q = self.r, self.part(0, self.c)

        @steps(self.D, STEP)
        def _(at):
            r.win[q, at, :] = w_in[at, :].astype(half)

        for d in range(1, self.X):
            self.weight_to_x(0, d).start()

        @steps(self.Fq, STEP)
        def _(at):
            r.wdn[q, at, :] = w_dn[at, :].astype(half)

        for d in range(1, self.X):
            self.weight_to_x(1, d).start()
        for i in range(2):
            self.weight_to_core(i, 0, self.c).start()

    def wait_weights(self, j, core):
        for i in range(2):
            if core == 0:
                if j:
                    self.weight_to_x(i, self.X - j).wait_recv()
                    self.weight_to_core(i, j, self.c).start()
            else:
                self.weight_to_core(i, j, 1 - self.c).wait_recv()

    def end_weights(self):
        for i in range(2):
            for j in range(self.X):
                self.weight_to_core(i, j, self.c).wait_send()
                if j:
                    self.weight_to_x(i, j).wait_send()

    def dispatch(self, k, part):
        r = self.r
        peer = self.expert_at(k)
        if part == 2:
            src, dst = r.gates, r.xgate
        else:
            src, dst = ((r.out_h.at[peer], r.xh), (r.out_g.at[peer], r.xg))[part]
        return remote(src, dst.at[k], r.send_a.at[part, k], r.recv_a.at[part, k], (peer, self.h))

    def send_out(self, *parts):
        r = self.r

        @pl.loop(1, self.E)
        def _(k):
            for part in parts:
                self.dispatch(k, part).start()

        for part in parts:
            if part == 2:
                r.xgate[0] = r.gates[...]
            else:
                src, dst = ((r.out_h, r.xh), (r.out_g, r.xg))[part]
                dst[0] = src[self.e]

    def take(self, g):
        r, cap = self.r, self.cap

        @pl.loop(0, self.G)
        def _(i):
            k = g * self.G + i

            @pl.when(k > 0)
            def _():
                for part in (1, 2, 0) if self.gated else (1, 0):
                    self.dispatch(k, part).wait_recv()

            if self.gated:
                lane = iota((cap, self.E * cap), 1)
                wanted = iota((cap, self.E * cap), 0) + self.e * cap
                gate = jnp.where(lane == wanted, r.xgate[k, 0:1, :], 0.0)
                gate = jnp.sum(gate, axis=1, keepdims=True)
                r.xg[k] = (gate * r.xg[k].astype(single)).astype(half)

    def compute(self, g):
        r = self.r
        slots = pl.ds(g * self.G, self.G)
        at = pl.ds(pl.multiple_of(g * self.rows, self.rows), self.rows)
        xh_g = r.xh[slots].reshape(self.rows, self.D)
        xg_g = r.xg[slots].reshape(self.rows, self.D)
        parts = []
        for n in range(2 * self.X):
            j, core = n // 2, n % 2
            q = self.part(j, self.c if core == 0 else 1 - self.c)
            parts.append(q)

            @pl.when(g == 0)
            def _():
                self.wait_weights(j, core)

            v = dot(xh_g, r.win[q])
            ga = dot_cols(xg_g, r.wdn[q])
            cdf = 0.5 * (1.0 + lax.erf(v * (0.5 ** 0.5)))
            slope = cdf + v * (jnp.exp(-0.5 * v * v) * 0.3989422804014327)
            r.act[q, at, :] = (v * cdf).astype(half)
            r.gbef[q, at, :] = (slope * ga).astype(half)
        out = sum(dot(r.act[q, at, :], r.wdn[q]) for q in parts)
        gin = sum(dot_cols(r.gbef[q, at, :], r.win[q]) for q in parts)
        shape = (self.G, self.cap, self.D)
        r.to[slots] = out.astype(half).reshape(shape)
        r.tg[slots] = gin.astype(half).reshape(shape)

    def give_back(self, k, part):
        r = self.r
        src, dst = ((r.to, r.ret_o), (r.tg, r.ret_g))[part]
        return remote(
            src.at[k], dst.at[self.e], r.send_r.at[part, k], r.recv_r.at[part, k],
            (self.expert_at(k), self.h),
        )

    def run(self):
        r = self.r

        @pl.loop(0, self.NG)
        def _(g):
            self.take(g)
            self.compute(g)

            @pl.loop(0, self.G)
            def _(i):
                k = g * self.G + i

                @pl.when(k > 0)
                def _():
                    self.give_back(k, 0).start()
                    self.give_back(k, 1).start()

                @pl.when(k == 0)
                def _():
                    r.ret_o[self.e] = r.to[0]
                    r.ret_g[self.e] = r.tg[0]

    def grad_to_core(self, i, j):
        r, w, came = self.r, (self.r.win, self.r.wdn)[i], (self.r.core_in, self.r.core_dn)[i]
        return remote(w.at[j], came.at[j], r.send_d.at[i, j], r.recv_d.at[i, j], self.core_peer)

    def grad_to_x(self, i, j):
        r, w, came = self.r, (self.r.win, self.r.wdn)[i], (self.r.in_came, self.r.dn_came)[i]
        return remote(
            w.at[self.X + j], came.at[self.X - j - 1], r.send_s.at[i, j], r.recv_s.at[i, self.X - j],
            self.x_peer(j),
        )

    def weight_grads(self, in_grad, dn_grad):
        r, D, Fq = self.r, self.D, self.Fq
        T = self.E * self.cap
        tile = 256 if Fq % 256 == 0 else 128
        r.xh_t[...] = r.xh[...].reshape(T, D).T

        def grad(i, q, at):
            if i == 0:
                return dot(r.xh_t[at, :], r.gbef[q])
            return dot_rows(r.act[q, :, at], r.xg[...].reshape(T, D))

        for j in list(range(1, self.X)) + [0]:
            for i, (w, size) in enumerate(((r.win, D), (r.wdn, Fq))):
                @steps(size, tile)
                def _(at):
                    w[j, at, :] = grad(i, self.part(j, 1 - self.c), at).astype(half)

                self.grad_to_core(i, j).start()
            for i, (w, came, size) in enumerate(((r.win, r.core_in, D), (r.wdn, r.core_dn, Fq))):
                self.grad_to_core(i, j).wait_recv()

                @steps(size, tile)
                def _(at):
                    total = grad(i, self.part(j, self.c), at) + came[j, at, :].astype(single)
                    if j:
                        w[self.X + j, at, :] = total.astype(half)
                    else:
                        (in_grad, dn_grad)[i][at, :] = total

                if j:
                    self.grad_to_x(i, j).start()

    def wait_returns(self):
        @pl.loop(1, self.E)
        def _(k):
            self.give_back(k, 0).wait_recv()
            self.give_back(k, 1).wait_recv()

    def end(self):
        for i in range(2):
            for j in range(self.X):
                self.grad_to_core(i, j).wait_send()
                if j:
                    self.grad_to_x(i, j).wait()

        @pl.loop(1, self.E)
        def _(k):
            for part in range(3 if self.gated else 2):
                self.dispatch(k, part).wait_send()
                if part < 2:
                    self.give_back(k, part).wait_send()


def expert_kernel(E, X, G, names, *refs):
    r = Named(names, refs)
    experts = Experts(E, X, G, r, False)
    experts.greet()
    experts.send_out(0, 1)
    experts.share_weights(r.w_in, r.w_dn)
    experts.run()
    experts.end_weights()
    experts.weight_grads(r.in_grad, r.dn_grad)
    experts.wait_returns()
    experts.end()


def group_size(E, cap):
    return max(1, min(E, GROUP_ROWS // cap))


def call(kernel, ins, outs, scratch, collective, name):
    names = list(ins) + list(outs) + list(scratch)
    extra = dict() if collective is None else dict(collective_id=collective, has_side_effects=True)
    pairs = [value if isinstance(value, tuple) else (value, VMEM_SPEC) for value in ins.values()]
    return pl.pallas_call(
        functools.partial(kernel, names),
        out_shape=tuple(jax.ShapeDtypeStruct(value[0], value[1]) for value in outs.values()),
        in_specs=[spec for _, spec in pairs],
        out_specs=tuple(value[2] if len(value) > 2 else VMEM_SPEC for value in outs.values()),
        scratch_shapes=list(scratch.values()),
        compiler_params=pltpu.CompilerParams(vmem_limit_bytes=VMEM_LIMIT, **extra),
        name=name,
    )(*[array for array, _ in pairs])


HEAD_DIM = 64
LANES = 128


def norm_stats(values):
    average = jnp.mean(values, axis=-1, keepdims=True)
    centred = values - average
    spread = jnp.mean(centred * centred, axis=-1, keepdims=True)
    return centred, lax.rsqrt(spread + epsilon)


def norm_back(grad, values, gain):
    centred, rate = norm_stats(values)
    unit = centred * rate
    scaled = grad * gain
    toward = rate * (
        scaled
        - jnp.mean(scaled, axis=-1, keepdims=True)
        - unit * jnp.mean(scaled * unit, axis=-1, keepdims=True)
    )
    gain_grad = jnp.sum(grad * unit, axis=0, keepdims=True)
    shift_grad = jnp.sum(grad, axis=0, keepdims=True)
    return toward, gain_grad, shift_grad


def iota(shape, axis):
    return lax.broadcasted_iota(jnp.int32, shape, axis)


def slot_places(assign, capacity):
    T = assign.shape[1]
    down, across = iota((T, T), 0), iota((T, T), 1)
    column = jnp.sum(jnp.where(down == across, assign, 0.0), axis=1, keepdims=True)
    same = column == assign
    rank_column = jnp.sum(jnp.where(same & (across < down), 1.0, 0.0), axis=1, keepdims=True)
    rank_row = jnp.sum(jnp.where(same & (down < across), 1.0, 0.0), axis=0, keepdims=True)
    place_column = (column * capacity + rank_column).astype(jnp.int32)
    place_row = (assign * capacity + rank_row).astype(jnp.int32)
    return column.astype(jnp.int32), place_column, place_row


def head_probs(q_one, k_pair, allowed):
    scores = dot_cols(q_one, k_pair) * (HEAD_DIM ** -0.5)
    scores = jnp.where(allowed, scores, masked_score)
    powers = jnp.exp(scores - jnp.max(scores, axis=-1, keepdims=True))
    return powers * (1.0 / jnp.sum(powers, axis=-1, keepdims=True))


def head_masks(T):
    first = iota((T, LANES), 1) < HEAD_DIM
    low_lanes = jnp.where(first, 1.0, 0.0).astype(half)
    high_lanes = jnp.where(first, 0.0, 1.0).astype(half)
    return first, (low_lanes, high_lanes)


def columns_of(D):
    return pl.ds(0, 3 * D // 2), pl.ds(3 * D // 2, D // 2)


def pair_columns(D, m, p):
    return pl.ds(pl.multiple_of(m * (D // 2) + p * LANES, LANES), LANES)


def attend(E, r, wts, small, between=lambda: None, then=lambda: None):
    T, D = r.tokens.shape
    first_cols, last_cols = columns_of(D)
    small_t = small[...].astype(single).T
    inputs = r.tokens[...].astype(single)
    centred, rate = norm_stats(inputs)
    r.hid_a[...] = (centred * rate * small_t[E : E + 1] + small_t[E + 1 : E + 2]).astype(half)
    for part in range(2):
        r.qkv[part] = dot(r.hid_a[...], wts[part, :, first_cols]).astype(half)
    between()
    allowed = iota((T, T), 1) <= iota((T, T), 0)
    first, masks = head_masks(T)
    count = D // LANES // 2

    @pl.loop(0, 2 * count)
    def _(i):
        part, p = lax.div(i, count), lax.rem(i, count)
        q_pair, k_pair, v_pair = (r.qkv[part, :, pair_columns(D, m, p)] for m in range(3))
        mixed = [
            dot(head_probs(q_pair * mask, k_pair, allowed).astype(half), v_pair) for mask in masks
        ]
        at = pl.ds(pl.multiple_of(i * LANES, LANES), LANES)
        r.att[:, at] = jnp.where(first, mixed[0], mixed[1]).astype(half)

    then()
    for part in range(2):
        at = pl.ds(part * (D // 2), D // 2)
        r.resid[:, at] = r.tokens[:, at].astype(single) + dot(r.att[...], wts[part, :, last_cols])
    centred, rate = norm_stats(r.resid[...])
    r.hid_b[...] = (centred * rate * small_t[E + 2 : E + 3] + small_t[E + 3 : E + 4]).astype(half)
    lane = iota((T, LANES), 1)
    logits = jnp.where(lane < E, dot(r.hid_b[...], small[...]), -1e30)
    powers = jnp.exp(logits - jnp.max(logits, axis=-1, keepdims=True))
    chance = powers * (1.0 / jnp.sum(powers, axis=-1, keepdims=True))
    r.probs[...] = chance
    return jnp.sum(jnp.where(r.mine[...] > 0.0, chance, 0.0), axis=1, keepdims=True)


def set_places(E, cap, r):
    T = r.tokens.shape[0]
    column, place_column, place_row = slot_places(r.assign[...].astype(single), cap)
    r.pick[...] = jnp.where(iota((E * cap, T), 0) == place_row, 1.0, 0.0).astype(half)
    r.place[...] = jnp.where(iota((T, E * cap), 1) == place_column, 1.0, 0.0).astype(half)
    r.mine[...] = jnp.where(iota((T, LANES), 1) == column, 1.0, 0.0)


def to_slots(r, rows, out):
    out[...] = dot(r.pick[...], rows).astype(half).reshape(out.shape)


def backward_body(E, total_tokens, r, wts, small, counts):
    T, D = r.tokens.shape
    slots = r.place.shape[1]
    small_t = small[...].astype(single).T
    cot = r.cotangent[...].astype(single)
    lane = iota((T, LANES), 1)
    chance = r.probs[...]
    mine = r.mine[...]
    gate = jnp.sum(mine * chance, axis=1, keepdims=True)
    expert_tok = dot(r.place[...], r.ret_o[...].reshape(slots, D))
    r.layer_out[...] = (r.resid[...] + gate * expert_tok).astype(half)
    grad_gate = jnp.sum(cot * expert_tok, axis=1, keepdims=True)
    scale = counts * (balance_weight * E / total_tokens)
    grad_probs = mine * grad_gate + scale
    grad_logits = chance * (grad_probs - jnp.sum(chance * grad_probs, axis=1, keepdims=True))
    grad_logits = jnp.where(lane < E, grad_logits, 0.0).astype(half)
    r.router_sum[...] = dot_rows(r.hid_b[...], grad_logits)
    grad_hidden_b = dot(r.place[...], r.ret_g[...].reshape(slots, D)) + dot_cols(grad_logits, small[...])
    toward, mid_gain, mid_shift = norm_back(grad_hidden_b, r.resid[...], small_t[E + 2 : E + 3])
    r.grad_res[...] = cot + toward
    r.gproj[...] = r.grad_res[...].astype(half)
    _, last_cols = columns_of(D)
    r.gatt[...] = sum(
        dot_cols(r.gproj[:, part * (D // 2) : (part + 1) * (D // 2)], wts[part, :, last_cols])
        for part in range(2)
    ).astype(half)
    return mid_gain, mid_shift


def attend_back(r, part):
    T, D = r.tokens.shape
    allowed = iota((T, T), 1) <= iota((T, T), 0)
    first, masks = head_masks(T)

    @pl.loop(0, D // LANES // 2)
    def _(p):
        q_pair, k_pair, v_pair = (r.qkv[part, :, pair_columns(D, m, p)] for m in range(3))
        g_pair = r.gatt[:, pl.ds(pl.multiple_of(part * (D // 2) + p * LANES, LANES), LANES)]
        found = []
        for mask in masks:
            weights = head_probs(q_pair * mask, k_pair, allowed)
            grad_w = dot_cols(g_pair * mask, v_pair)
            grad_s = weights * (grad_w - jnp.sum(weights * grad_w, axis=-1, keepdims=True))
            grad_s = grad_s.astype(half)
            found.append(
                (
                    dot(grad_s, k_pair) * (HEAD_DIM ** -0.5),
                    dot_rows(grad_s, q_pair) * (HEAD_DIM ** -0.5),
                    dot_rows(weights.astype(half), g_pair),
                )
            )
        for m in range(3):
            r.gqkv[part, :, pair_columns(D, m, p)] = jnp.where(first, found[0][m], found[1][m]).astype(half)


def transposes(r):
    r.hid_a_t[...] = r.hid_a[...].T
    r.att_t[...] = r.att[...].T


def qkv_weight_grad(r, part, write):
    D = r.hid_a_t.shape[0]

    @steps(D, 256 if D % 256 == 0 else LANES)
    def _(rows):
        write(rows, dot(r.hid_a_t[rows, :], r.gqkv[part]))


def proj_weight_grad(r, part, write):
    D = r.att_t.shape[0]
    cols = pl.ds(pl.multiple_of(part * (D // 2), D // 2), D // 2)

    @steps(D, 256 if D % 256 == 0 else LANES)
    def _(rows):
        write(rows, dot(r.att_t[rows, :], r.gproj[:, cols]))


def input_body(E, r, wts, small):
    small_t = small[...].astype(single).T
    first_cols, _ = columns_of(r.tokens.shape[1])
    grad_hidden_a = sum(dot_cols(r.gqkv[part], wts[part, :, first_cols]) for part in range(2))
    toward, pre_gain, pre_shift = norm_back(
        grad_hidden_a, r.tokens[...].astype(single), small_t[E : E + 1]
    )
    r.input_grad[...] = (r.grad_res[...] + toward).astype(half)
    return pre_gain, pre_shift


def small_grads(E, router, rows, chance_sum, block, D):
    lane = iota((D, LANES), 1)
    eight = iota((LANES, D), 0)
    stacked = jnp.zeros((LANES, D), single)
    for i, row in enumerate(rows):
        stacked = jnp.where(eight == E + i, row, stacked)
    packed = jnp.where(lane < E, router, stacked.T)
    if block:
        place = lax.rem(iota((D, LANES), 0), block)
        copy = jnp.sum(jnp.where(place == lane, chance_sum, 0.0), axis=1, keepdims=True)
        packed = jnp.where(lane == E + 4, copy, packed)
    return packed


class Place:
    def __init__(self, E):
        e, h = lax.axis_index("expert"), lax.axis_index("hid")
        self.Z = E // 2
        self.z, self.y = lax.div(e, 2), lax.rem(e, 2)
        self.x, self.c = lax.div(h, 2), lax.rem(h, 2)

    def device(self, z, y, x, c):
        return (z * 2 + y, x * 2 + c)

    def z_at(self, d):
        return lax.rem(self.z + d, self.Z)

    def z_peer(self, d):
        return self.device(self.z_at(d), self.y, self.x, self.c)

    def y_peer(self):
        return self.device(self.z, 1 - self.y, self.x, self.c)

    def x_peer(self):
        return self.device(self.z, self.y, 1 - self.x, self.c)

    def core_peer(self):
        return self.device(self.z, self.y, self.x, 1 - self.c)

    def z_steps(self):
        return sorted(range(1, self.Z), key=lambda d: min(d, self.Z - d))

    def greet(self):
        barrier = pltpu.get_barrier_semaphore()
        peers = [self.z_peer(d) for d in range(1, self.Z)]
        peers += [self.y_peer(), self.x_peer(), self.core_peer()]
        for peer in peers:
            pl.semaphore_signal(barrier, inc=1, device_id=peer, device_id_type=MESH)
        pl.semaphore_wait(barrier, len(peers))


def chip_index(z, y, x):
    return (z * 2 + y) * 2 + x


class Sends:
    def __init__(self, sems):
        self.sems, self.started = sems, []

    def start(self, src, dst, recv_sem, device):
        copy = remote(src, dst, self.sems.at[len(self.started)], recv_sem, device)
        copy.start()
        self.started.append(copy)

    def finish(self):
        for copy in self.started:
            copy.wait_send()


def arrive(dst, send_sem, recv_sem, device):
    remote(dst, dst, send_sem, recv_sem, device).wait_recv()


class Gather:
    def __init__(self, at, sends, wts, small, spans, recv, rows):
        self.at, self.sends, self.wts, self.small, self.spans = at, sends, wts, small, spans
        self.recv, self.span = recv, 2 * rows

    def rows_of(self, chip):
        return pl.ds(pl.multiple_of(chip * self.span, self.span), self.span)

    def block(self, o, chip, core):
        if o == len(self.spans):
            return self.small.at[self.rows_of(chip), :]
        return self.wts.at[core, self.rows_of(chip), self.spans[o]]

    def send(self, o, chip, device):
        block = self.block(o, chip, self.at.c)
        self.sends.start(block, block, self.recv.at[0, o, chip], device)

    def share(self, o, chip):
        if o < len(self.spans):
            block = self.block(o, chip, self.at.c)
            self.sends.start(block, block, self.recv.at[1, o, chip], self.at.core_peer())

    def wait(self, o, chip):
        block = self.block(o, chip, self.at.c)
        arrive(block, self.sends.sems.at[0], self.recv.at[0, o, chip], self.at.core_peer())

    def spread(self, o, chip):
        for d in self.at.z_steps():
            self.send(o, chip, self.at.z_peer(d))
        self.send(o, chip, self.at.y_peer())
        self.share(o, chip)

    def along_x(self, o):
        at = self.at
        self.send(o, chip_index(at.z, at.y, at.x), at.x_peer())

    def own(self, o):
        at = self.at
        self.spread(o, chip_index(at.z, at.y, at.x))

    def second(self, o):
        at = self.at
        chip = chip_index(at.z, at.y, 1 - at.x)
        self.wait(o, chip)
        self.spread(o, chip)

    def third(self, o):
        at = self.at
        for x in (at.x, 1 - at.x):
            for d in at.z_steps():
                chip = chip_index(at.z_at(d), at.y, x)
                self.wait(o, chip)
                self.send(o, chip, at.y_peer())
                self.share(o, chip)

    def fourth(self, o):
        at = self.at
        for x in (at.x, 1 - at.x):
            for d in [0] + at.z_steps():
                chip = chip_index(at.z_at(d), 1 - at.y, x)
                self.wait(o, chip)
                self.share(o, chip)

    def finish(self, o):
        if o < len(self.spans):
            @pl.loop(0, 4 * self.at.Z)
            def _(chip):
                block = self.block(o, chip, 1 - self.at.c)
                arrive(block, self.sends.sems.at[0], self.recv.at[1, o, chip], self.at.core_peer())


class SumScatter:
    def __init__(self, at, sends, cols, r, recv):
        self.at, self.sends, self.cols, self.r, self.recv = at, sends, cols, r, recv
        self.span = r.final.shape[0]

    def rows_of(self, chip):
        return pl.ds(pl.multiple_of(chip * self.span, self.span), self.span)

    def swap(self):
        r = self.r
        self.sends.start(r.give.at[:, self.cols], r.got.at[:, self.cols], self.recv.at[0], self.at.core_peer())

    def wait_swap(self):
        there = self.r.got.at[:, self.cols]
        arrive(there, self.sends.sems.at[0], self.recv.at[0], self.at.core_peer())

    def send(self, slot, value, device):
        r = self.r
        r.sent[slot, :, self.cols] = value.astype(half)
        self.sends.start(
            r.sent.at[slot, :, self.cols], r.came.at[slot, :, self.cols], self.recv.at[1 + slot], device
        )

    def take(self, slot):
        there = self.r.came.at[slot, :, self.cols]
        arrive(there, self.sends.sems.at[0], self.recv.at[1 + slot], self.at.core_peer())
        return there[...].astype(single)

    def base(self, chip):
        rows = self.rows_of(chip)
        return self.r.acc[rows, self.cols] + self.r.got[rows, self.cols].astype(single)

    def one(self):
        at = self.at
        for dz in at.z_steps() + [0]:
            for x in range(2):
                chip = chip_index(at.z_at(dz), 1 - at.y, x)
                self.send(dz * 2 + x, self.base(chip), at.y_peer())

    def two(self):
        at = self.at
        for dz in at.z_steps() + [0]:
            for x in range(2):
                chip = chip_index(at.z_at(dz), at.y, x)
                value = self.base(chip) + self.take(dz * 2 + x)
                if dz:
                    self.send(2 * at.Z + dz * 2 + x, value, at.z_peer(dz))
                else:
                    self.r.acc[self.rows_of(chip), self.cols] = value

    def three(self):
        at = self.at
        for flip in (1, 0):
            x = 1 - at.x if flip else at.x
            value = self.r.acc[self.rows_of(chip_index(at.z, at.y, x)), self.cols]
            for dz in range(1, at.Z):
                value = value + self.take(2 * at.Z + dz * 2 + x)
            if flip:
                self.send(4 * at.Z, value, at.x_peer())
            else:
                self.r.final[:, self.cols] = value

    def four(self):
        at, r = self.at, self.r
        r.final[:, self.cols] += self.take(4 * at.Z)
        rows = self.span // 2
        there = r.final.at[pl.ds(pl.multiple_of((1 - at.c) * rows, rows), rows), self.cols]
        last = self.recv.shape[0] - 1
        self.sends.start(there, r.final_other.at[:, self.cols], self.recv.at[last], at.core_peer())

    def end(self):
        there = self.r.final_other.at[:, self.cols]
        arrive(there, self.sends.sems.at[0], self.recv.at[self.recv.shape[0] - 1], self.at.core_peer())


VMEM_LIMIT = 62 * 1024 * 1024
GROUP_ROWS = 128


def model_scratch(E, T, D, cap):
    slots = E * cap
    return dict(
        pick=pltpu.VMEM((slots, T), half), place=pltpu.VMEM((T, slots), half),
        mine=pltpu.VMEM((T, LANES), single),
    )


def end_scratch(T, D):
    return dict(
        gqkv=pltpu.VMEM((2, T, 3 * D // 2), half), gproj=pltpu.VMEM((T, D), half), gatt=pltpu.VMEM((T, D), half),
        grad_res=pltpu.VMEM((T, D), single), router_sum=pltpu.VMEM((D, LANES), single),
        hid_a_t=pltpu.VMEM((D, T), half), att_t=pltpu.VMEM((D, T), half),
    )


def start_kernel(E, names, *refs):
    r = Named(names, refs)
    cap = r.out_h.shape[1]
    set_places(E, cap, r)
    gate = attend(E, r, r.wts, r.small)
    to_slots(r, r.hid_b[...], r.out_h)
    to_slots(r, (gate * r.cotangent[...].astype(single)).astype(half), r.out_g)


def end_kernel(E, total_tokens, names, *refs):
    r = Named(names, refs)
    D = r.tokens.shape[1]
    set_places(E, r.ret_o.shape[1], r)
    transposes(r)
    mid_gain, mid_shift = backward_body(E, total_tokens, r, r.wts, r.small, r.counts[0:1])
    first_cols, last_cols = columns_of(D)
    for part in range(2):
        attend_back(r, part)

        def write_first(rows, value):
            r.weight_grads[part, rows, first_cols] = value

        def write_last(rows, value):
            r.weight_grads[part, rows, last_cols] = value

        qkv_weight_grad(r, part, write_first)
        proj_weight_grad(r, part, write_last)
    pre_gain, pre_shift = input_body(E, r, r.wts, r.small)
    chance_sum = jnp.sum(r.probs[...], axis=0, keepdims=True)
    r.small_out[...] = small_grads(
        E, r.router_sum[...], (pre_gain, pre_shift, mid_gain, mid_shift), chance_sum, 0, D
    )


class SmallSum:
    def __init__(self, at, sends, r, rows):
        self.at, self.sends, self.r, self.rows = at, sends, r, rows

    def rows_of(self, z, y, x):
        first = chip_index(z, y, x) * 2 * self.rows + self.at.c * self.rows
        return pl.ds(pl.multiple_of(first, self.rows), self.rows)

    def send(self, slot, value, device):
        r = self.r
        r.pack_sent[slot] = value
        self.sends.start(r.pack_sent.at[slot], r.pack_came.at[slot], r.pack_recv.at[1 + slot], device)

    def take(self, slot):
        r = self.r
        arrive(r.pack_came.at[slot], r.send.at[0], r.pack_recv.at[1 + slot], self.at.core_peer())
        return r.pack_came[slot]

    def zero(self):
        r = self.r
        self.sends.start(r.pack, r.pack_other, r.pack_recv.at[0], self.at.core_peer())

    def one(self):
        r, at = self.r, self.at
        arrive(r.pack_other, r.send.at[0], r.pack_recv.at[0], at.core_peer())
        r.pack_other[...] += r.pack[...]
        for dz in range(at.Z):
            for y in range(2):
                self.send(dz * 2 + y, r.pack_other[self.rows_of(at.z_at(dz), y, 1 - at.x), :], at.x_peer())

    def two(self):
        r, at = self.r, self.at
        for dz in range(at.Z):
            for flip in (1, 0):
                y = 1 - at.y if flip else at.y
                here = self.rows_of(at.z_at(dz), y, at.x)
                value = r.pack_other[here, :] + self.take(dz * 2 + y)
                if flip:
                    self.send(2 * at.Z + dz, value, at.y_peer())
                else:
                    r.pack_other[here, :] = value

    def three(self):
        r, at = self.r, self.at
        for dz in at.z_steps() + [0]:
            value = r.pack_other[self.rows_of(at.z_at(dz), at.y, at.x), :] + self.take(2 * at.Z + dz)
            if dz:
                self.send(3 * at.Z + dz, value, at.z_peer(dz))
        return value

    def four(self, total):
        for dz in range(1, self.at.Z):
            total = total + self.take(3 * self.at.Z + dz)
        return total


def whole_scratch(E, T, D, cap, rows):
    Z = E // 2
    slots = 4 * Z + 1
    token = (E, cap, D)
    return dict(
        wts=pltpu.VMEM((2, D, 2 * D), half), small=pltpu.VMEM((D, LANES), half),
        shard=pltpu.VMEM((2, rows, 2 * D), single), small_shard=pltpu.VMEM((rows, LANES), single),
        other=pltpu.VMEM((rows, 2 * D), single), other_small=pltpu.VMEM((rows, LANES), single),
        square=pltpu.VMEM((LANES, LANES), single), counts=pltpu.VMEM((8, LANES), single),
        hid_a=pltpu.VMEM((T, D), half), qkv=pltpu.VMEM((2, T, 3 * D // 2), half), att=pltpu.VMEM((T, D), half),
        resid=pltpu.VMEM((T, D), single), hid_b=pltpu.VMEM((T, D), half),
        probs=pltpu.VMEM((T, LANES), single), gates=pltpu.VMEM((8, E * cap), single),
        out_h=pltpu.VMEM(token, half), out_g=pltpu.VMEM(token, half),
        ret_o=pltpu.VMEM(token, half), ret_g=pltpu.VMEM(token, half),
        acc=pltpu.VMEM((D, 2 * D), single), give=pltpu.VMEM((D, 2 * D), half), got=pltpu.VMEM((D, 2 * D), half),
        sent=pltpu.VMEM((slots, 2 * rows, 2 * D), half), came=pltpu.VMEM((slots, 2 * rows, 2 * D), half),
        final=pltpu.VMEM((2 * rows, 2 * D), single), final_other=pltpu.VMEM((rows, 2 * D), single),
        pack=pltpu.VMEM((D, LANES), single), pack_other=pltpu.VMEM((D, LANES), single),
        pack_sent=pltpu.VMEM((4 * Z, rows, LANES), single),
        pack_came=pltpu.VMEM((4 * Z, rows, LANES), single),
        local=DMA((4,)), send=DMA((40 * Z + 16,)), gather_recv=DMA((2, 3, 4 * Z)), own_recv=DMA((2,)),
        sum_recv=DMA((2, slots + 2)), pack_recv=DMA((4 * Z + 1,)),
    )


def whole_kernel(E, total_tokens, G, names, *refs):
    r = Named(names, refs)
    rows, D = r.proj_shard.shape
    T = r.tokens.shape[0]
    cap = r.out_h.shape[1]
    at = Place(E)
    experts = Experts(E, 2, G, r, True)
    sends = Sends(r.send)
    width = D // 2
    first_cols, last_cols = columns_of(D)
    through = r.acc.at[:, 0:D], r.acc.at[:, D : 2 * D]
    loads = [
        pltpu.make_async_copy(w.at[0], there, r.local.at[i])
        for i, (w, there) in enumerate(zip((r.w_in, r.w_dn), through))
    ]
    for load in loads:
        load.start()
    for part in range(2):
        for m in range(3):
            first = m * D + part * width
            r.shard[part, :, m * width : (m + 1) * width] = r.qkv_shard[:, first : first + width]
        r.shard[part, :, 3 * width :] = r.proj_shard[:, part * width : (part + 1) * width]
    assign = r.assign[...].astype(single)
    r.square[...] = jnp.zeros_like(r.square)
    r.square[0:E, 0:rows] = r.router[...]
    for i, gain in enumerate((r.pre_gain, r.pre_shift, r.mid_gain, r.mid_shift)):
        r.square[E + i : E + i + 1, 0:rows] = gain[...]
    numbers = iota((rows, T), 0).astype(single)
    count = jnp.sum(jnp.where(assign == numbers, 1.0, 0.0), axis=1, keepdims=True)
    lane = iota((rows, LANES), 1)
    r.small_shard[...] = jnp.where(lane == E + 4, count, r.square[...].T[0:rows, :])

    experts.greet()
    core = at.core_peer()
    sends.start(r.shard.at[1 - at.c], r.other, r.own_recv.at[0], core)
    sends.start(r.small_shard, r.other_small, r.own_recv.at[1], core)
    gather = Gather(at, sends, r.wts, r.small, (first_cols, last_cols), r.gather_recv, rows)
    own_rows = gather.rows_of(chip_index(at.z, at.y, at.x))

    def both(here, there):
        low, high = jnp.where(at.c == 0, here, there), jnp.where(at.c == 0, there, here)
        return jnp.concatenate([low, high], axis=0).astype(half)

    arrive(r.other, r.send.at[0], r.own_recv.at[0], core)
    r.wts[at.c, own_rows, :] = both(r.shard[at.c], r.other[...])
    gather.along_x(0)
    gather.own(0)
    arrive(r.other_small, r.send.at[0], r.own_recv.at[1], core)
    r.small[own_rows, :] = both(r.small_shard[...], r.other_small[...])
    gather.along_x(2)
    gather.along_x(1)
    gather.own(2)
    for load in loads:
        load.wait()
    experts.share_weights(*through)
    gather.second(0)
    gather.second(2)
    gather.third(0)
    gather.third(2)
    set_places(E, cap, r)
    to_slots(r, r.cotangent[...], r.out_g)
    gather.own(1)
    gather.fourth(0)
    gather.fourth(2)
    gather.second(1)
    experts.send_out(1)
    gather.finish(0)
    place = lax.rem(iota((D, LANES), 0), rows)
    column = r.small[:, E + 4 : E + 5].astype(single)
    total = jnp.sum(jnp.where(place == iota((D, LANES), 1), column, 0.0), axis=0, keepdims=True)
    r.counts[...] = jnp.broadcast_to(total, r.counts.shape)

    def between():
        gather.third(1)

    def then():
        gather.fourth(1)
        gather.finish(1)

    gate = attend(E, r, r.wts, r.small, between, then)
    to_slots(r, r.hid_b[...], r.out_h)
    gates = jnp.sum(r.place[...].astype(single) * gate, axis=0, keepdims=True)
    r.gates[...] = jnp.broadcast_to(gates, r.gates.shape)
    experts.send_out(2, 0)
    experts.run()
    experts.end_weights()
    experts.weight_grads(*through)
    stores = [
        pltpu.make_async_copy(there, w.at[0], r.local.at[2 + i])
        for i, (w, there) in enumerate(zip((r.in_own, r.dn_own), through))
    ]
    for store in stores:
        store.start()
    transposes(r)
    experts.wait_returns()

    mid_gain, mid_shift = backward_body(E, total_tokens, r, r.wts, r.small, r.counts[0:1])
    for store in stores:
        store.wait()
    first = SumScatter(at, sends, first_cols, r, r.sum_recv.at[0])
    last = SumScatter(at, sends, last_cols, r, r.sum_recv.at[1])
    smalls = SmallSum(at, sends, r, rows)

    def give_last(here, value):
        r.give[here, last_cols] = value.astype(half)

    def keep_last(here, value):
        r.acc[here, last_cols] = value

    def give_first(here, value):
        r.give[here, first_cols] = value.astype(half)

    def keep_first(here, value):
        r.acc[here, first_cols] = value

    proj_weight_grad(r, 1 - at.c, give_last)
    last.swap()
    proj_weight_grad(r, at.c, keep_last)
    attend_back(r, 1 - at.c)
    qkv_weight_grad(r, 1 - at.c, give_first)
    first.swap()
    last.wait_swap()
    last.one()
    attend_back(r, at.c)
    qkv_weight_grad(r, at.c, keep_first)
    first.wait_swap()
    first.one()
    last.two()
    pre_gain, pre_shift = input_body(E, r, r.wts, r.small)
    chance_sum = jnp.sum(r.probs[...], axis=0, keepdims=True)
    r.pack[...] = small_grads(
        E, r.router_sum[...], (pre_gain, pre_shift, mid_gain, mid_shift), chance_sum, rows, D
    )
    smalls.zero()
    last.three()
    first.two()
    smalls.one()
    last.four()
    smalls.two()
    first.three()
    total = smalls.three()
    first.four()
    total = smalls.four(total)
    scale = r.counts[0:1] * (balance_weight * E / total_tokens)
    chance = jnp.sum(jnp.where(lane == E + 4, total, 0.0), axis=1, keepdims=True)
    chosen = jnp.where((lane == iota((rows, LANES), 0)) & (lane < E), chance * scale, 0.0)
    loss = jnp.sum(jnp.sum(chosen, axis=1, keepdims=True), axis=0, keepdims=True) / total_tokens
    r.square[0:rows, :] = jnp.where(lane == E + 5, loss, total)
    r.small_out[...] = r.square[...].T[0 : r.small_out.shape[0], :]
    last.end()
    first.end()
    half_rows = pl.ds(pl.multiple_of(at.c * rows, rows), rows)
    mine, theirs = r.final[half_rows, :], r.final_other[...]
    for part, value in enumerate((jnp.where(at.c == 0, mine, theirs), jnp.where(at.c == 0, theirs, mine))):
        for m in range(3):
            begin = m * D + part * width
            r.qkv_grad[:, begin : begin + width] = value[:, m * width : (m + 1) * width]
        r.proj_grad[:, part * width : (part + 1) * width] = value[:, 3 * width :]
    experts.end()
    sends.finish()


def out_kernel(E, names, *refs):
    r = Named(names, refs)
    pairs = [
        (r.in_own, r.h0), (r.in_came, r.h1), (r.dn_own, r.h2), (r.dn_came, r.h3),
        (r.layer_in, r.h4), (r.input_in, r.h5), (r.qkv_in, r.h6), (r.proj_in, r.h7),
    ]
    loads = [pltpu.make_async_copy(src, there, r.sems.at[0, i]) for i, (src, there) in enumerate(pairs)]
    outs = [
        (r.h0, r.in_grad), (r.h2, r.dn_grad), (r.h4, r.layer_out), (r.h5, r.input_grad), (r.h6, r.qkv_grad),
        (r.h7, r.proj_grad),
    ]
    stores = [pltpu.make_async_copy(there, dst, r.sems.at[1, i]) for i, (there, dst) in enumerate(outs)]
    for load in loads:
        load.start()
    rows = r.proj_in.shape[0]
    r.router[...] = r.small_in[0:E, 0:rows]
    for i, gain in enumerate((r.pre_gain, r.pre_shift, r.mid_gain, r.mid_shift)):
        gain[...] = r.small_in[E + i : E + i + 1, 0:rows]
    r.loss[...] = r.small_in[E + 5 : E + 6, 0:1]
    for i, (own, came) in enumerate(((r.h0, r.h1), (r.h2, r.h3))):
        loads[2 * i].wait()
        loads[2 * i + 1].wait()

        @steps(own.shape[1], STEP)
        def _(at):
            own[0, at, :] += sum(came[j, at, :].astype(single) for j in range(came.shape[0]))

        stores[i].start()
    for load, store in zip(loads[4:], stores[2:]):
        load.wait()
        store.start()
    for store in stores:
        store.wait()


def on_device(
    tokens_in, out_cotangent, qkv_weight, proj_weight, router_weight, pre_gain, pre_shift, mid_gain, mid_shift,
    expert_in, expert_down, assignment,
):
    T, D = tokens_in.shape
    E, H = lax.axis_size("expert"), lax.axis_size("hid")
    X = H // 2
    Z = E // 2
    cap = 2 * T // E
    G = group_size(E, cap)
    Fq = expert_in.shape[2]
    total_tokens = T * E * H
    rows = proj_weight.shape[0]
    both = ("expert", "hid")
    assign = assignment.reshape(1, T)
    token = ((T, D), half)
    slot = ((E, cap, D), half)
    vectors = dict(pre_gain=pre_gain, pre_shift=pre_shift, mid_gain=mid_gain, mid_shift=mid_shift)
    if X == 2 and E % 2 == 0 and rows % 8 == 0 and E <= rows <= LANES and Fq == D and D % 256 == 0:
        small_rows = E + 8
        found = call(
            functools.partial(whole_kernel, E, total_tokens, G),
            dict(
                tokens=tokens_in, cotangent=out_cotangent, assign=assign,
                qkv_shard=qkv_weight, proj_shard=proj_weight, router=router_weight.T,
                **dict((name, value.reshape(1, rows)) for name, value in vectors.items()),
                w_in=(expert_in, ANY_SPEC), w_dn=(expert_down, ANY_SPEC),
            ),
            dict(
                layer_out=token, input_grad=token, qkv_grad=((rows, 3 * D), single),
                proj_grad=((rows, D), single), small_out=((small_rows, LANES), single),
                in_own=((1, D, Fq), single, ANY_SPEC), dn_own=((1, Fq, D), single, ANY_SPEC),
                in_came=((X - 1, D, Fq), half, ANY_SPEC), dn_came=((X - 1, Fq, D), half, ANY_SPEC),
            ),
            dict(
                **whole_scratch(E, T, D, cap, rows), **model_scratch(E, T, D, cap), **end_scratch(T, D),
                **expert_scratch(E, X, cap, D, Fq),
            ),
            1, "layer",
        )
        layer_out, input_grad, qkv_grad, proj_grad, small_out, in_own, dn_own, in_came, dn_came = found
        vector = ((1, rows), single)
        found = call(
            functools.partial(out_kernel, E),
            dict(
                layer_in=(layer_out, ANY_SPEC), input_in=(input_grad, ANY_SPEC),
                qkv_in=(qkv_grad, ANY_SPEC), proj_in=(proj_grad, ANY_SPEC),
                in_own=(in_own, ANY_SPEC), dn_own=(dn_own, ANY_SPEC),
                in_came=(in_came, ANY_SPEC), dn_came=(dn_came, ANY_SPEC), small_in=small_out,
            ),
            dict(
                layer_out=token + (ANY_SPEC,), input_grad=token + (ANY_SPEC,),
                qkv_grad=((rows, 3 * D), single, ANY_SPEC), proj_grad=((rows, D), single, ANY_SPEC),
                in_grad=((1, D, Fq), single, ANY_SPEC), dn_grad=((1, Fq, D), single, ANY_SPEC),
                router=((E, rows), single), pre_gain=vector, pre_shift=vector, mid_gain=vector,
                mid_shift=vector, loss=((1, 1), single),
            ),
            dict(
                h0=pltpu.VMEM((1, D, Fq), single), h1=pltpu.VMEM((X - 1, D, Fq), half),
                h2=pltpu.VMEM((1, Fq, D), single), h3=pltpu.VMEM((X - 1, Fq, D), half),
                h4=pltpu.VMEM(*token), h5=pltpu.VMEM(*token), h6=pltpu.VMEM((rows, 3 * D), single),
                h7=pltpu.VMEM((rows, D), single), sems=DMA((2, 8)),
            ),
            None, "results",
        )
        layer_out, input_grad, qkv_grad, proj_grad, in_grad, dn_grad, router, *grads, loss = found
        return (
            layer_out, loss.reshape(()), input_grad, qkv_grad, proj_grad, router.T,
            *[value.reshape(rows) for value in grads], in_grad, dn_grad,
        )

    small_in = jnp.concatenate([router_weight] + [value[:, None] for value in vectors.values()], axis=1)
    small_in = jnp.pad(small_in, ((0, 0), (0, LANES - small_in.shape[1])))
    shard = jnp.concatenate([qkv_weight, proj_weight], axis=1).astype(half)
    wts = lax.all_gather(shard, both, axis=0, tiled=True).reshape(D, 4, 2, D // 2)
    wts = wts.transpose(2, 0, 1, 3).reshape(2, D, 2 * D)
    small = lax.all_gather(small_in.astype(half), both, axis=0, tiled=True)
    onehot = assignment[:, None] == jnp.arange(LANES, dtype=jnp.int32)[None, :]
    counts = lax.psum(jnp.sum(onehot.astype(single), axis=0), both)
    saved = dict(
        hid_a=token, qkv=((2, T, 3 * D // 2), half), att=token, resid=((T, D), single), hid_b=token,
        probs=((T, LANES), single),
    )
    given = dict(tokens=tokens_in, cotangent=out_cotangent, assign=assign, wts=wts, small=small)
    out_h, out_g, *rest = call(
        functools.partial(start_kernel, E), given, dict(out_h=slot, out_g=slot, **saved),
        model_scratch(E, T, D, cap), None, "start",
    )
    ret_o, ret_g, in_own, dn_own, in_came, dn_came = call(
        functools.partial(expert_kernel, E, X, G),
        dict(out_h=out_h, out_g=out_g, w_in=expert_in[0], w_dn=expert_down[0]),
        dict(
            ret_o=slot, ret_g=slot, in_grad=((D, Fq), single), dn_grad=((Fq, D), single),
            in_came=((X - 1, D, Fq), half), dn_came=((X - 1, Fq, D), half),
        ),
        expert_scratch(E, X, cap, D, Fq), 1, "experts",
    )
    in_grad = in_own + jnp.sum(in_came.astype(single), axis=0)
    dn_grad = dn_own + jnp.sum(dn_came.astype(single), axis=0)
    layer_out, input_grad, weight_grads, packed = call(
        functools.partial(end_kernel, E, total_tokens),
        dict(
            **given, counts=jnp.broadcast_to(counts[None, :], (8, LANES)), **dict(zip(saved, rest)),
            ret_o=ret_o, ret_g=ret_g,
        ),
        dict(
            layer_out=token, input_grad=token, weight_grads=((2, D, 2 * D), single),
            small_out=((D, LANES), single),
        ),
        dict(**model_scratch(E, T, D, cap), **end_scratch(T, D)), None, "end",
    )
    gathered = weight_grads.reshape(2, D, 4, D // 2).transpose(1, 2, 0, 3).reshape(D, 4 * D)
    gathered = lax.psum_scatter(gathered, both, scatter_dimension=0, tiled=True)
    small_out = lax.psum_scatter(packed, both, scatter_dimension=0, tiled=True)
    chance = lax.psum(jnp.sum(rest[-1], axis=0), both)
    balance_loss = jnp.sum(chance * counts) * (balance_weight * E / total_tokens) / total_tokens
    return (
        layer_out, balance_loss, input_grad, gathered[:, : 3 * D], gathered[:, 3 * D :], small_out[:, :E],
        *[small_out[:, E + i] for i in range(4)], in_grad[None], dn_grad[None],
    )


def solution(mesh):
    in_specs = (
        P(("expert", "hid"), None),
        P(("expert", "hid"), None),
        P(("expert", "hid"), None),
        P(("expert", "hid"), None),
        P(("expert", "hid"), None),
        P(("expert", "hid")),
        P(("expert", "hid")),
        P(("expert", "hid")),
        P(("expert", "hid")),
        P("expert", None, "hid"),
        P("expert", "hid", None),
        P(("expert", "hid")),
    )
    out_specs = (
        P(("expert", "hid"), None),
        P(),
        P(("expert", "hid"), None),
        P(("expert", "hid"), None),
        P(("expert", "hid"), None),
        P(("expert", "hid"), None),
        P(("expert", "hid")),
        P(("expert", "hid")),
        P(("expert", "hid")),
        P(("expert", "hid")),
        P("expert", None, "hid"),
        P("expert", "hid", None),
    )
    return jax.shard_map(
        on_device, mesh=mesh, in_specs=in_specs, out_specs=out_specs, check_vma=False
    )
```

```python
import functools

import jax
import jax.numpy as jnp
from jax import lax
from jax.experimental import pallas as pl
from jax.experimental.pallas import tpu as pltpu
from jax.sharding import PartitionSpec as P

epsilon = 1e-05
balance_weight = 3.0
masked_score = -1000000000.0


MESH = pl.DeviceIdType.MESH
DMA = pltpu.SemaphoreType.DMA
VMEM_SPEC = pl.BlockSpec(memory_space=pltpu.VMEM)
ANY_SPEC = pl.BlockSpec(memory_space=pl.ANY)
half = jnp.bfloat16
single = jnp.float32
STEP = 32


def remote(src, dst, send_sem, recv_sem, device):
    return pltpu.make_async_remote_copy(
        src_ref=src, dst_ref=dst, send_sem=send_sem, recv_sem=recv_sem,
        device_id=device, device_id_type=MESH,
    )


def dot(a, b):
    return jnp.dot(a, b, preferred_element_type=single)


def dot_cols(a, b):
    return lax.dot_general(a, b, (((1,), (1,)), ((), ())), preferred_element_type=single)


def dot_rows(a, b):
    return lax.dot_general(a, b, (((0,), (0,)), ((), ())), preferred_element_type=single)


def grad_rows(size):
    return 256 if size % 256 == 0 else 128


def steps(count, step):
    def run(body):
        @pl.loop(0, count // step)
        def _(i):
            body(pl.ds(pl.multiple_of(i * step, step), step))
    return run


class Named:
    def __init__(self, names, refs):
        self.__dict__.update(zip(names, refs, strict=True))


def expert_scratch(E, X, cap, D, Fq):
    P, token = 2 * X, (E, cap, D)
    return dict(
        xh=pltpu.VMEM(token, half), xg=pltpu.VMEM(token, half),
        win=pltpu.VMEM((P, D, Fq), half), wdn=pltpu.VMEM((P, Fq, D), half),
        act=pltpu.VMEM((P, E * cap, Fq), half), gbef=pltpu.VMEM((P, E * cap, Fq), half),
        to=pltpu.VMEM(token, half), tg=pltpu.VMEM(token, half), xh_t=pltpu.VMEM((D, E * cap), half),
        core_in=pltpu.VMEM((X, D, Fq), half), core_dn=pltpu.VMEM((X, Fq, D), half),
        xgate=pltpu.VMEM((E, 8, E * cap), single), raw=pltpu.VMEM(token, half),
        tgg=pltpu.VMEM((E, 8, E * cap), single), ret_gg=pltpu.VMEM((E, 8, E * cap), single),
        send_a=DMA((3, E)), recv_a=DMA((3, E)), send_r=DMA((3, E)), recv_r=DMA((3, E)),
        send_w=DMA((2, X)), recv_w=DMA((2, X)), send_f=DMA((2, X)), recv_f=DMA((2, X)),
        send_d=DMA((2, X)), recv_d=DMA((2, X)), send_s=DMA((2, X)), recv_s=DMA((2, X)),
    )


class Experts:
    def __init__(self, E, X, G, r, gated):
        self.E, self.X, self.G, self.r, self.gated = E, X, G, r, gated
        self.e, self.h = lax.axis_index("expert"), lax.axis_index("hid")
        self.x, self.c = lax.div(self.h, 2), lax.rem(self.h, 2)
        self.cap, self.D = r.out_h.shape[1], r.out_h.shape[2]
        self.Fq = r.win.shape[2]
        self.NG, self.rows = E // G, G * self.cap
        self.core_peer = (self.e, self.x * 2 + 1 - self.c)
        self.landing = r.raw if gated else r.xg

    def expert_at(self, k):
        found, bit = 0, 1
        while bit < self.E:
            a, b = lax.rem(lax.div(self.e, bit), 2), lax.rem(lax.div(k, bit), 2)
            found = found + bit * (a + b - 2 * a * b)
            bit *= 2
        return found

    def x_peer(self, d):
        return (self.e, lax.rem(self.x + d, self.X) * 2 + self.c)

    def part(self, j, core):
        return lax.rem(self.x + j, self.X) * 2 + core

    def greet(self):
        barrier = pltpu.get_barrier_semaphore()

        @pl.loop(1, self.E)
        def _(k):
            pl.semaphore_signal(
                barrier, inc=1, device_id=(self.expert_at(k), self.h), device_id_type=MESH
            )

        for d in range(1, self.X):
            pl.semaphore_signal(barrier, inc=1, device_id=self.x_peer(d), device_id_type=MESH)
        pl.semaphore_signal(barrier, inc=1, device_id=self.core_peer, device_id_type=MESH)

    def meet(self):
        pl.semaphore_wait(pltpu.get_barrier_semaphore(), self.E - 1 + self.X - 1 + 1)

    def weight_to_x(self, i, d):
        r, w, q = self.r, (self.r.win, self.r.wdn)[i], self.part(0, self.c)
        return remote(
            w.at[q], w.at[q], r.send_w.at[i, d], r.recv_w.at[i, self.X - d], self.x_peer(d)
        )

    def weight_to_core(self, i, j, core):
        r, w, q = self.r, (self.r.win, self.r.wdn)[i], self.part(j, core)
        return remote(w.at[q], w.at[q], r.send_f.at[i, j], r.recv_f.at[i, j], self.core_peer)

    def share_weights(self, w_in, w_dn):
        r, q = self.r, self.part(0, self.c)

        @steps(self.D, STEP)
        def _(at):
            r.win[q, at, :] = w_in[at, :].astype(half)

        for d in range(1, self.X):
            self.weight_to_x(0, d).start()

        @steps(self.Fq, STEP)
        def _(at):
            r.wdn[q, at, :] = w_dn[at, :].astype(half)

        for d in range(1, self.X):
            self.weight_to_x(1, d).start()
        for i in range(2):
            self.weight_to_core(i, 0, self.c).start()

    def wait_weights(self, j, core):
        for i in range(2):
            if core == 0:
                if j:
                    self.weight_to_x(i, self.X - j).wait_recv()
                    self.weight_to_core(i, j, self.c).start()
            else:
                self.weight_to_core(i, j, 1 - self.c).wait_recv()

    def end_weights(self):
        for i in range(2):
            for j in range(self.X):
                self.weight_to_core(i, j, self.c).wait_send()
                if j:
                    self.weight_to_x(i, j).wait_send()

    def dispatch(self, k, part):
        r = self.r
        peer = self.expert_at(k)
        if part == 2:
            src, dst = r.gates, r.xgate
        else:
            src, dst = ((r.out_h.at[peer], r.xh), (r.out_g.at[peer], self.landing))[part]
        return remote(src, dst.at[k], r.send_a.at[part, k], r.recv_a.at[part, k], (peer, self.h))

    def send_out(self, *parts):
        r = self.r

        @pl.loop(1, self.E)
        def _(k):
            for part in parts:
                self.dispatch(k, part).start()

        for part in parts:
            if part == 2:
                r.xgate[0] = r.gates[...]
            else:
                src, dst = ((r.out_h, r.xh), (r.out_g, self.landing))[part]
                dst[0] = src[self.e]

    def own_lanes(self):
        shape = (self.cap, self.E * self.cap)
        return iota(shape, 1) == iota(shape, 0) + self.e * self.cap

    def take(self, g):
        r, cap = self.r, self.cap

        @pl.loop(0, self.G)
        def _(i):
            k = g * self.G + i

            @pl.when(k > 0)
            def _():
                for part in (1, 2, 0) if self.gated else (1, 0):
                    self.dispatch(k, part).wait_recv()

            if self.gated:
                gate = jnp.where(self.own_lanes(), r.xgate[k, 0:1, :], 0.0)
                gate = jnp.sum(gate, axis=1, keepdims=True)
                r.xg[k] = (gate * r.raw[k].astype(single)).astype(half)

    def compute(self, g):
        r = self.r
        slots = pl.ds(g * self.G, self.G)
        at = pl.ds(pl.multiple_of(g * self.rows, self.rows), self.rows)
        xh_g = r.xh[slots].reshape(self.rows, self.D)
        xg_g = r.xg[slots].reshape(self.rows, self.D)
        parts = []
        for n in range(2 * self.X):
            j, core = n // 2, n % 2
            q = self.part(j, self.c if core == 0 else 1 - self.c)
            parts.append(q)

            @pl.when(g == 0)
            def _():
                self.wait_weights(j, core)

            v = dot(xh_g, r.win[q])
            ga = dot_cols(xg_g, r.wdn[q])
            cdf = 0.5 * (1.0 + lax.erf(v * (0.5 ** 0.5)))
            slope = cdf + v * (jnp.exp(-0.5 * v * v) * 0.3989422804014327)
            r.act[q, at, :] = (v * cdf).astype(half)
            r.gbef[q, at, :] = (slope * ga).astype(half)
        out = sum(dot(r.act[q, at, :], r.wdn[q]) for q in parts)
        gin = sum(dot_cols(r.gbef[q, at, :], r.win[q]) for q in parts)
        shape = (self.G, self.cap, self.D)
        r.to[slots] = out.astype(half).reshape(shape)
        r.tg[slots] = gin.astype(half).reshape(shape)
        if self.gated:
            @pl.loop(0, self.G)
            def _(i):
                k = g * self.G + i
                toward = jnp.sum(r.raw[k].astype(single) * r.to[k].astype(single), axis=1, keepdims=True)
                row = jnp.sum(jnp.where(self.own_lanes(), toward, 0.0), axis=0, keepdims=True)
                r.tgg[k] = jnp.broadcast_to(row, r.tgg.shape[1:])

    def give_back(self, k, part):
        r = self.r
        src, dst = ((r.to, r.ret_o), (r.tg, r.ret_g), (r.tgg, r.ret_gg))[part]
        return remote(
            src.at[k], dst.at[self.e], r.send_r.at[part, k], r.recv_r.at[part, k],
            (self.expert_at(k), self.h),
        )

    def run(self):
        r = self.r
        parts = (1, 2) if self.gated else (1,)

        @pl.loop(0, self.NG)
        def _(g):
            self.take(g)
            self.compute(g)

            @pl.loop(0, self.G)
            def _(i):
                k = g * self.G + i

                @pl.when(k > 0)
                def _():
                    for part in parts:
                        self.give_back(k, part).start()

        @pl.loop(1, self.E)
        def _(k):
            self.give_back(k, 0).start()

        r.ret_o[self.e] = r.to[0]
        r.ret_g[self.e] = r.tg[0]
        if self.gated:
            r.ret_gg[self.e] = r.tgg[0]

    def grad_to_core(self, i, j):
        r, w, came = self.r, (self.r.win, self.r.wdn)[i], (self.r.core_in, self.r.core_dn)[i]
        return remote(w.at[j], came.at[j], r.send_d.at[i, j], r.recv_d.at[i, j], self.core_peer)

    def grad_to_x(self, i, j):
        r, w, came = self.r, (self.r.win, self.r.wdn)[i], (self.r.in_came, self.r.dn_came)[i]
        return remote(
            w.at[self.X + j], came.at[self.X - j - 1], r.send_s.at[i, j], r.recv_s.at[i, self.X - j],
            self.x_peer(j),
        )

    def grad(self, i, q, at):
        r, T = self.r, self.E * self.cap
        if i == 0:
            return dot(r.xh_t[at, :], r.gbef[q])
        return dot_rows(r.act[q, :, at], r.xg[...].reshape(T, self.D))

    def start_grads(self, j):
        r = self.r
        for i, (w, size) in enumerate(((r.win, self.D), (r.wdn, self.Fq))):
            @steps(size, grad_rows(size))
            def _(at):
                w[j, at, :] = self.grad(i, self.part(j, 1 - self.c), at).astype(half)

            self.grad_to_core(i, j).start()

    def own_grads(self, j, store):
        r = self.r
        for i, (w, came, size) in enumerate(((r.win, r.core_in, self.D), (r.wdn, r.core_dn, self.Fq))):
            self.grad_to_core(i, j).wait_recv()
            if j:
                @steps(size, grad_rows(size))
                def _(at):
                    total = self.grad(i, self.part(j, self.c), at) + came[j, at, :].astype(single)
                    w[self.X + j, at, :] = total.astype(half)

                self.grad_to_x(i, j).start()
            else:
                for first in range(0, size, grad_rows(size)):
                    at = pl.ds(first, grad_rows(size))
                    store(i, at, self.grad(i, self.part(j, self.c), at) + came[j, at, :].astype(single))

    def turn_rows(self):
        self.r.xh_t[...] = self.r.xh[...].reshape(self.E * self.cap, self.D).T

    def wait_returns(self, *parts):
        @pl.loop(1, self.E)
        def _(k):
            for part in parts:
                self.give_back(k, part).wait_recv()

    def end(self):
        for i in range(2):
            for j in range(self.X):
                self.grad_to_core(i, j).wait_send()
                if j:
                    self.grad_to_x(i, j).wait()

        @pl.loop(1, self.E)
        def _(k):
            for part in range(3 if self.gated else 2):
                self.dispatch(k, part).wait_send()
                self.give_back(k, part).wait_send()


def expert_kernel(E, X, G, names, *refs):
    r = Named(names, refs)
    experts = Experts(E, X, G, r, False)
    experts.greet()
    experts.meet()
    experts.send_out(0, 1)
    experts.share_weights(r.w_in, r.w_dn)
    experts.run()
    experts.end_weights()
    experts.turn_rows()

    def store(i, at, value):
        (r.in_grad, r.dn_grad)[i][at, :] = value

    for j in list(range(1, X)) + [0]:
        experts.start_grads(j)
        experts.own_grads(j, store)
    experts.wait_returns(0, 1)
    experts.end()


def group_size(E, cap):
    return max(1, min(E, GROUP_ROWS // cap))


def call(kernel, ins, outs, scratch, collective, name):
    names = list(ins) + list(outs) + list(scratch)
    extra = dict() if collective is None else dict(collective_id=collective, has_side_effects=True)
    pairs = [value if isinstance(value, tuple) else (value, VMEM_SPEC) for value in ins.values()]
    return pl.pallas_call(
        functools.partial(kernel, names),
        out_shape=tuple(jax.ShapeDtypeStruct(value[0], value[1]) for value in outs.values()),
        in_specs=[spec for _, spec in pairs],
        out_specs=tuple(value[2] if len(value) > 2 else VMEM_SPEC for value in outs.values()),
        scratch_shapes=list(scratch.values()),
        compiler_params=pltpu.CompilerParams(vmem_limit_bytes=VMEM_LIMIT, **extra),
        name=name,
    )(*[array for array, _ in pairs])


HEAD_DIM = 64
LANES = 128


def norm_stats(values):
    average = jnp.mean(values, axis=-1, keepdims=True)
    centred = values - average
    spread = jnp.mean(centred * centred, axis=-1, keepdims=True)
    return centred, lax.rsqrt(spread + epsilon)


def norm_back(grad, values, gain):
    centred, rate = norm_stats(values)
    unit = centred * rate
    scaled = grad * gain
    toward = rate * (
        scaled
        - jnp.mean(scaled, axis=-1, keepdims=True)
        - unit * jnp.mean(scaled * unit, axis=-1, keepdims=True)
    )
    gain_grad = jnp.sum(grad * unit, axis=0, keepdims=True)
    shift_grad = jnp.sum(grad, axis=0, keepdims=True)
    return toward, gain_grad, shift_grad


def iota(shape, axis):
    return lax.broadcasted_iota(jnp.int32, shape, axis)


def slot_places(assign, capacity):
    T = assign.shape[1]
    down, across = iota((T, T), 0), iota((T, T), 1)
    column = jnp.sum(jnp.where(down == across, assign, 0.0), axis=1, keepdims=True)
    same = column == assign
    rank_column = jnp.sum(jnp.where(same & (across < down), 1.0, 0.0), axis=1, keepdims=True)
    rank_row = jnp.sum(jnp.where(same & (down < across), 1.0, 0.0), axis=0, keepdims=True)
    place_column = (column * capacity + rank_column).astype(jnp.int32)
    place_row = (assign * capacity + rank_row).astype(jnp.int32)
    return column.astype(jnp.int32), place_column, place_row


def head_probs(q_one, k_pair, allowed):
    scores = dot_cols(q_one, k_pair) * (HEAD_DIM ** -0.5)
    scores = jnp.where(allowed, scores, masked_score)
    powers = jnp.exp(scores - jnp.max(scores, axis=-1, keepdims=True))
    return powers * (1.0 / jnp.sum(powers, axis=-1, keepdims=True))


def head_masks(T):
    first = iota((T, LANES), 1) < HEAD_DIM
    low_lanes = jnp.where(first, 1.0, 0.0).astype(half)
    high_lanes = jnp.where(first, 0.0, 1.0).astype(half)
    return first, (low_lanes, high_lanes)


def columns_of(D):
    return pl.ds(0, 3 * D // 2), pl.ds(3 * D // 2, D // 2)


def pair_columns(D, m, p):
    return pl.ds(pl.multiple_of(m * (D // 2) + p * LANES, LANES), LANES)


def attend(E, r, wts, small, between=lambda: None, then=lambda: None):
    T, D = r.tokens.shape
    first_cols, last_cols = columns_of(D)
    small_t = small[...].astype(single).T
    inputs = r.tokens[...].astype(single)
    centred, rate = norm_stats(inputs)
    r.hid_a[...] = (centred * rate * small_t[E : E + 1] + small_t[E + 1 : E + 2]).astype(half)
    for part in range(2):
        r.qkv[part] = dot(r.hid_a[...], wts[part, :, first_cols]).astype(half)
    between()
    allowed = iota((T, T), 1) <= iota((T, T), 0)
    first, masks = head_masks(T)
    count = D // LANES // 2

    @pl.loop(0, 2 * count)
    def _(i):
        part, p = lax.div(i, count), lax.rem(i, count)
        q_pair, k_pair, v_pair = (r.qkv[part, :, pair_columns(D, m, p)] for m in range(3))
        mixed = [
            dot(head_probs(q_pair * mask, k_pair, allowed).astype(half), v_pair) for mask in masks
        ]
        at = pl.ds(pl.multiple_of(i * LANES, LANES), LANES)
        r.att[:, at] = jnp.where(first, mixed[0], mixed[1]).astype(half)

    then()
    for part in range(2):
        at = pl.ds(part * (D // 2), D // 2)
        r.resid[:, at] = r.tokens[:, at].astype(single) + dot(r.att[...], wts[part, :, last_cols])
    centred, rate = norm_stats(r.resid[...])
    r.hid_b[...] = (centred * rate * small_t[E + 2 : E + 3] + small_t[E + 3 : E + 4]).astype(half)
    lane = iota((T, LANES), 1)
    logits = jnp.where(lane < E, dot(r.hid_b[...], small[...]), -1e30)
    powers = jnp.exp(logits - jnp.max(logits, axis=-1, keepdims=True))
    chance = powers * (1.0 / jnp.sum(powers, axis=-1, keepdims=True))
    r.probs[...] = chance
    return jnp.sum(jnp.where(r.mine[...] > 0.0, chance, 0.0), axis=1, keepdims=True)


def set_places(E, cap, r):
    T = r.tokens.shape[0]
    column, place_column, place_row = slot_places(r.assign[...].astype(single), cap)
    r.pick[...] = jnp.where(iota((E * cap, T), 0) == place_row, 1.0, 0.0).astype(half)
    r.place[...] = jnp.where(iota((T, E * cap), 1) == place_column, 1.0, 0.0).astype(half)
    r.mine[...] = jnp.where(iota((T, LANES), 1) == column, 1.0, 0.0)


def to_slots(r, rows, out):
    out[...] = dot(r.pick[...], rows).astype(half).reshape(out.shape)


def set_output(r):
    slots, D = r.place.shape[1], r.tokens.shape[1]
    gate = jnp.sum(r.mine[...] * r.probs[...], axis=1, keepdims=True)
    expert_tok = dot(r.place[...], r.ret_o[...].reshape(slots, D))
    r.layer_out[...] = (r.resid[...] + gate * expert_tok).astype(half)
    return jnp.sum(r.cotangent[...].astype(single) * expert_tok, axis=1, keepdims=True)


def backward_body(E, total_tokens, r, wts, small, counts, grad_gate):
    T, D = r.tokens.shape
    slots = r.place.shape[1]
    small_t = small[...].astype(single).T
    cot = r.cotangent[...].astype(single)
    lane = iota((T, LANES), 1)
    chance = r.probs[...]
    mine = r.mine[...]
    scale = counts * (balance_weight * E / total_tokens)
    grad_probs = mine * grad_gate + scale
    grad_logits = chance * (grad_probs - jnp.sum(chance * grad_probs, axis=1, keepdims=True))
    grad_logits = jnp.where(lane < E, grad_logits, 0.0).astype(half)
    r.router_sum[...] = dot_rows(r.hid_b[...], grad_logits)
    grad_hidden_b = dot(r.place[...], r.ret_g[...].reshape(slots, D)) + dot_cols(grad_logits, small[...])
    toward, mid_gain, mid_shift = norm_back(grad_hidden_b, r.resid[...], small_t[E + 2 : E + 3])
    r.grad_res[...] = cot + toward
    r.gproj[...] = r.grad_res[...].astype(half)
    _, last_cols = columns_of(D)
    r.gatt[...] = sum(
        dot_cols(r.gproj[:, part * (D // 2) : (part + 1) * (D // 2)], wts[part, :, last_cols])
        for part in range(2)
    ).astype(half)
    return mid_gain, mid_shift


def attend_back(r, part):
    T, D = r.tokens.shape
    allowed = iota((T, T), 1) <= iota((T, T), 0)
    first, masks = head_masks(T)

    @pl.loop(0, D // LANES // 2)
    def _(p):
        q_pair, k_pair, v_pair = (r.qkv[part, :, pair_columns(D, m, p)] for m in range(3))
        g_pair = r.gatt[:, pl.ds(pl.multiple_of(part * (D // 2) + p * LANES, LANES), LANES)]
        found = []
        for mask in masks:
            weights = head_probs(q_pair * mask, k_pair, allowed)
            grad_w = dot_cols(g_pair * mask, v_pair)
            grad_s = weights * (grad_w - jnp.sum(weights * grad_w, axis=-1, keepdims=True))
            grad_s = grad_s.astype(half)
            found.append(
                (
                    dot(grad_s, k_pair) * (HEAD_DIM ** -0.5),
                    dot_rows(grad_s, q_pair) * (HEAD_DIM ** -0.5),
                    dot_rows(weights.astype(half), g_pair),
                )
            )
        for m in range(3):
            r.gqkv[part, :, pair_columns(D, m, p)] = jnp.where(first, found[0][m], found[1][m]).astype(half)


def transposes(r):
    r.hid_a_t[...] = r.hid_a[...].T
    r.att_t[...] = r.att[...].T


def qkv_weight_grad(r, part, write):
    D = r.hid_a_t.shape[0]

    @steps(D, 256 if D % 256 == 0 else LANES)
    def _(rows):
        write(rows, dot(r.hid_a_t[rows, :], r.gqkv[part]))


def proj_weight_grad(r, part, write):
    D = r.att_t.shape[0]
    cols = pl.ds(pl.multiple_of(part * (D // 2), D // 2), D // 2)

    @steps(D, 256 if D % 256 == 0 else LANES)
    def _(rows):
        write(rows, dot(r.att_t[rows, :], r.gproj[:, cols]))


def input_body(E, r, wts, small):
    small_t = small[...].astype(single).T
    first_cols, _ = columns_of(r.tokens.shape[1])
    grad_hidden_a = sum(dot_cols(r.gqkv[part], wts[part, :, first_cols]) for part in range(2))
    toward, pre_gain, pre_shift = norm_back(
        grad_hidden_a, r.tokens[...].astype(single), small_t[E : E + 1]
    )
    r.input_grad[...] = (r.grad_res[...] + toward).astype(half)
    return pre_gain, pre_shift


def small_grads(E, router, rows, chance_sum, block, D):
    lane = iota((D, LANES), 1)
    eight = iota((LANES, D), 0)
    stacked = jnp.zeros((LANES, D), single)
    for i, row in enumerate(rows):
        stacked = jnp.where(eight == E + i, row, stacked)
    packed = jnp.where(lane < E, router, stacked.T)
    if block:
        place = lax.rem(iota((D, LANES), 0), block)
        copy = jnp.sum(jnp.where(place == lane, chance_sum, 0.0), axis=1, keepdims=True)
        packed = jnp.where(lane == E + 4, copy, packed)
    return packed


class Place:
    def __init__(self, E):
        e, h = lax.axis_index("expert"), lax.axis_index("hid")
        self.Z = E // 2
        self.z, self.y = lax.div(e, 2), lax.rem(e, 2)
        self.x, self.c = lax.div(h, 2), lax.rem(h, 2)

    def device(self, z, y, x, c):
        return (z * 2 + y, x * 2 + c)

    def z_at(self, d):
        return lax.rem(self.z + d, self.Z)

    def z_peer(self, d):
        return self.device(self.z_at(d), self.y, self.x, self.c)

    def y_peer(self):
        return self.device(self.z, 1 - self.y, self.x, self.c)

    def x_peer(self):
        return self.device(self.z, self.y, 1 - self.x, self.c)

    def core_peer(self):
        return self.device(self.z, self.y, self.x, 1 - self.c)

    def z_steps(self):
        return sorted(range(1, self.Z), key=lambda d: min(d, self.Z - d))

    def greet(self):
        barrier = pltpu.get_barrier_semaphore()
        peers = [self.z_peer(d) for d in range(1, self.Z)]
        peers += [self.y_peer(), self.x_peer(), self.core_peer()]
        for peer in peers:
            pl.semaphore_signal(barrier, inc=1, device_id=peer, device_id_type=MESH)
        pl.semaphore_wait(barrier, len(peers))


def chip_index(z, y, x):
    return (z * 2 + y) * 2 + x


class Sends:
    def __init__(self, sems):
        self.sems, self.started = sems, []

    def start(self, src, dst, recv_sem, device):
        copy = remote(src, dst, self.sems.at[len(self.started)], recv_sem, device)
        copy.start()
        self.started.append(copy)
        return len(self.started) - 1

    def settle(self, n):
        self.started[n].wait_send()
        self.started[n] = None

    def finish(self):
        for copy in self.started:
            if copy is not None:
                copy.wait_send()


def arrive(dst, send_sem, recv_sem, device):
    remote(dst, dst, send_sem, recv_sem, device).wait_recv()


class Gather:
    def __init__(self, at, sends, wts, small, spans, recv, rows):
        self.at, self.sends, self.wts, self.small, self.spans = at, sends, wts, small, spans
        self.recv, self.span = recv, 2 * rows

    def rows_of(self, chip):
        return pl.ds(pl.multiple_of(chip * self.span, self.span), self.span)

    def block(self, o, chip, core):
        if o == len(self.spans):
            return self.small.at[self.rows_of(chip), :]
        return self.wts.at[core, self.rows_of(chip), self.spans[o]]

    def send(self, o, chip, device):
        block = self.block(o, chip, self.at.c)
        self.sends.start(block, block, self.recv.at[0, o, chip], device)

    def share(self, o, chip):
        if o < len(self.spans):
            block = self.block(o, chip, self.at.c)
            self.sends.start(block, block, self.recv.at[1, o, chip], self.at.core_peer())

    def wait(self, o, chip):
        block = self.block(o, chip, self.at.c)
        arrive(block, self.sends.sems.at[0], self.recv.at[0, o, chip], self.at.core_peer())

    def spread(self, o, chip):
        for d in self.at.z_steps():
            self.send(o, chip, self.at.z_peer(d))
        self.send(o, chip, self.at.y_peer())
        self.share(o, chip)

    def along_x(self, o):
        at = self.at
        self.send(o, chip_index(at.z, at.y, at.x), at.x_peer())

    def own(self, o):
        at = self.at
        self.spread(o, chip_index(at.z, at.y, at.x))

    def second(self, o):
        at = self.at
        chip = chip_index(at.z, at.y, 1 - at.x)
        self.wait(o, chip)
        self.spread(o, chip)

    def third(self, o):
        at = self.at
        for x in (at.x, 1 - at.x):
            for d in at.z_steps():
                chip = chip_index(at.z_at(d), at.y, x)
                self.wait(o, chip)
                self.send(o, chip, at.y_peer())
                self.share(o, chip)

    def fourth(self, o):
        at = self.at
        for x in (at.x, 1 - at.x):
            for d in [0] + at.z_steps():
                chip = chip_index(at.z_at(d), 1 - at.y, x)
                self.wait(o, chip)
                self.share(o, chip)

    def finish(self, o):
        if o < len(self.spans):
            @pl.loop(0, 4 * self.at.Z)
            def _(chip):
                block = self.block(o, chip, 1 - self.at.c)
                arrive(block, self.sends.sems.at[0], self.recv.at[1, o, chip], self.at.core_peer())


class SumScatter:
    def __init__(self, at, sends, cols, r, recv):
        self.at, self.sends, self.cols, self.r, self.recv = at, sends, cols, r, recv
        self.span = r.final.shape[0]

    def rows_of(self, chip):
        return pl.ds(pl.multiple_of(chip * self.span, self.span), self.span)

    def swap(self):
        r = self.r
        self.swapped = self.sends.start(
            r.give.at[:, self.cols], r.got.at[:, self.cols], self.recv.at[0], self.at.core_peer()
        )

    def wait_swap(self):
        self.sends.settle(self.swapped)
        there = self.r.got.at[:, self.cols]
        arrive(there, self.sends.sems.at[0], self.recv.at[0], self.at.core_peer())

    def send(self, slot, chip, value, device):
        r, rows = self.r, self.rows_of(chip)
        r.give[rows, self.cols] = value.astype(half)
        self.sends.start(
            r.give.at[rows, self.cols], r.came.at[slot, :, self.cols], self.recv.at[1 + slot], device
        )

    def take(self, slot):
        there = self.r.came.at[slot, :, self.cols]
        arrive(there, self.sends.sems.at[0], self.recv.at[1 + slot], self.at.core_peer())
        return there[...].astype(single)

    def base(self, chip):
        rows = self.rows_of(chip)
        return self.r.acc[rows, self.cols] + self.r.got[rows, self.cols].astype(single)

    def one(self):
        at = self.at
        for dz in at.z_steps() + [0]:
            for x in range(2):
                chip = chip_index(at.z_at(dz), 1 - at.y, x)
                self.send(dz * 2 + x, chip, self.base(chip), at.y_peer())

    def two(self, dz):
        at = self.at
        for x in range(2):
            chip = chip_index(at.z_at(dz), at.y, x)
            value = self.base(chip) + self.take(dz * 2 + x)
            if dz:
                self.send(2 * at.Z + dz * 2 + x, chip, value, at.z_peer(dz))
            else:
                self.r.acc[self.rows_of(chip), self.cols] = value

    def three(self):
        at = self.at
        for flip in (1, 0):
            x = 1 - at.x if flip else at.x
            chip = chip_index(at.z, at.y, x)
            value = self.r.acc[self.rows_of(chip), self.cols]
            for dz in range(1, at.Z):
                value = value + self.take(2 * at.Z + dz * 2 + x)
            if flip:
                self.send(4 * at.Z, chip, value, at.x_peer())
            else:
                self.r.final[:, self.cols] = value

    def four(self):
        at, r = self.at, self.r
        r.final[:, self.cols] += self.take(4 * at.Z)
        rows = self.span // 2
        there = r.final.at[pl.ds(pl.multiple_of((1 - at.c) * rows, rows), rows), self.cols]
        last = self.recv.shape[0] - 1
        self.sends.start(there, r.final_other.at[:, self.cols], self.recv.at[last], at.core_peer())

    def end(self):
        there = self.r.final_other.at[:, self.cols]
        arrive(there, self.sends.sems.at[0], self.recv.at[self.recv.shape[0] - 1], self.at.core_peer())


VMEM_LIMIT = 62 * 1024 * 1024
GROUP_ROWS = 128


def model_scratch(E, T, D, cap):
    slots = E * cap
    return dict(
        pick=pltpu.VMEM((slots, T), half), place=pltpu.VMEM((T, slots), half),
        mine=pltpu.VMEM((T, LANES), single),
    )


def end_scratch(T, D):
    return dict(
        gqkv=pltpu.VMEM((2, T, 3 * D // 2), half), gproj=pltpu.VMEM((T, D), half), gatt=pltpu.VMEM((T, D), half),
        grad_res=pltpu.VMEM((T, D), single), router_sum=pltpu.VMEM((D, LANES), single),
        hid_a_t=pltpu.VMEM((D, T), half), att_t=pltpu.VMEM((D, T), half),
    )


def start_kernel(E, names, *refs):
    r = Named(names, refs)
    cap = r.out_h.shape[1]
    set_places(E, cap, r)
    gate = attend(E, r, r.wts, r.small)
    to_slots(r, r.hid_b[...], r.out_h)
    to_slots(r, (gate * r.cotangent[...].astype(single)).astype(half), r.out_g)


def end_kernel(E, total_tokens, names, *refs):
    r = Named(names, refs)
    D = r.tokens.shape[1]
    set_places(E, r.ret_o.shape[1], r)
    transposes(r)
    mid_gain, mid_shift = backward_body(E, total_tokens, r, r.wts, r.small, r.counts[0:1], set_output(r))
    first_cols, last_cols = columns_of(D)
    for part in range(2):
        attend_back(r, part)

        def write_first(rows, value):
            r.weight_grads[part, rows, first_cols] = value

        def write_last(rows, value):
            r.weight_grads[part, rows, last_cols] = value

        qkv_weight_grad(r, part, write_first)
        proj_weight_grad(r, part, write_last)
    pre_gain, pre_shift = input_body(E, r, r.wts, r.small)
    chance_sum = jnp.sum(r.probs[...], axis=0, keepdims=True)
    r.small_out[...] = small_grads(
        E, r.router_sum[...], (pre_gain, pre_shift, mid_gain, mid_shift), chance_sum, 0, D
    )


class SmallSum:
    def __init__(self, at, sends, r, rows):
        self.at, self.sends, self.r, self.rows = at, sends, r, rows

    def here(self, z, y, x):
        first = chip_index(z, y, x) * 2 * self.rows + self.at.c * self.rows
        return self.r.pack_other[pl.ds(pl.multiple_of(first, self.rows), self.rows), :]

    def send(self, slot, value, device):
        r = self.r
        r.pack_sent[slot] = value
        self.sends.start(r.pack_sent.at[slot], r.pack_came.at[slot], r.pack_recv.at[1 + slot], device)

    def take(self, slot):
        r = self.r
        arrive(r.pack_came.at[slot], r.send.at[0], r.pack_recv.at[1 + slot], self.at.core_peer())
        return r.pack_came[slot]

    def zero(self):
        r = self.r
        self.sends.start(r.pack, r.pack_other, r.pack_recv.at[0], self.at.core_peer())

    def one(self):
        r, at = self.r, self.at
        arrive(r.pack_other, r.send.at[0], r.pack_recv.at[0], at.core_peer())
        r.pack_other[...] += r.pack[...]
        for dz in range(at.Z):
            for x in range(2):
                self.send(dz * 2 + x, self.here(at.z_at(dz), 1 - at.y, x), at.y_peer())

    def two(self):
        at = self.at
        for dz in at.z_steps():
            for x in range(2):
                value = self.here(at.z_at(dz), at.y, x) + self.take(dz * 2 + x)
                self.send(2 * at.Z + dz * 2 + x, value, at.z_peer(dz))

    def three(self):
        at = self.at
        for flip in (1, 0):
            x = 1 - at.x if flip else at.x
            value = self.here(at.z, at.y, x) + self.take(x)
            for dz in range(1, at.Z):
                value = value + self.take(2 * at.Z + dz * 2 + x)
            if flip:
                self.send(4 * at.Z, value, at.x_peer())
        return value

    def four(self, total):
        return total + self.take(4 * self.at.Z)


def whole_scratch(E, T, D, cap, rows):
    Z = E // 2
    slots = 4 * Z + 1
    token = (E, cap, D)
    return dict(
        wts=pltpu.VMEM((2, D, 2 * D), half), small=pltpu.VMEM((D, LANES), half),
        shard=pltpu.VMEM((2, rows, 2 * D), single), small_shard=pltpu.VMEM((rows, LANES), single),
        other=pltpu.VMEM((rows, 2 * D), single), other_small=pltpu.VMEM((rows, LANES), single),
        square=pltpu.VMEM((LANES, LANES), single), counts=pltpu.VMEM((8, LANES), single),
        hid_a=pltpu.VMEM((T, D), half), qkv=pltpu.VMEM((2, T, 3 * D // 2), half), att=pltpu.VMEM((T, D), half),
        resid=pltpu.VMEM((T, D), single), hid_b=pltpu.VMEM((T, D), half),
        probs=pltpu.VMEM((T, LANES), single), gates=pltpu.VMEM((8, E * cap), single),
        out_h=pltpu.VMEM(token, half), out_g=pltpu.VMEM(token, half),
        ret_o=pltpu.VMEM(token, half), ret_g=pltpu.VMEM(token, half),
        acc=pltpu.VMEM((D, 2 * D), single), give=pltpu.VMEM((D, 2 * D), half), got=pltpu.VMEM((D, 2 * D), half),
        came=pltpu.VMEM((slots, 2 * rows, 2 * D), half),
        final=pltpu.VMEM((2 * rows, 2 * D), single), final_other=pltpu.VMEM((rows, 2 * D), single),
        pack=pltpu.VMEM((D, LANES), single), pack_other=pltpu.VMEM((D, LANES), single),
        pack_sent=pltpu.VMEM((slots, rows, LANES), single),
        pack_came=pltpu.VMEM((slots, rows, LANES), single),
        reads=DMA((10,)), writes=DMA((5,)), local=DMA((4,)), send=DMA((40 * Z + 16,)), gather_recv=DMA((2, 3, 4 * Z)), own_recv=DMA((2,)),
        sum_recv=DMA((2, slots + 2)), pack_recv=DMA((slots + 1,)),
    )


def whole_kernel(E, total_tokens, G, names, *refs):
    r = Named(names, refs)
    rows, D = r.proj_shard.shape
    T = r.tokens.shape[0]
    cap = r.out_h.shape[1]
    pairs = [
        (r.x_qkv, r.qkv_shard), (r.x_proj, r.proj_shard), (r.x_assign, r.assign), (r.x_router, r.router),
        (r.x_pre_gain, r.pre_gain), (r.x_pre_shift, r.pre_shift), (r.x_mid_gain, r.mid_gain),
        (r.x_mid_shift, r.mid_shift), (r.x_tokens, r.tokens), (r.x_cotangent, r.cotangent),
    ]
    reads = [pltpu.make_async_copy(src, there, r.reads.at[i]) for i, (src, there) in enumerate(pairs)]
    at = Place(E)
    experts = Experts(E, 2, G, r, True)
    experts.greet()
    for read in reads:
        read.start()
    sends = Sends(r.send)
    width = D // 2
    first_cols, last_cols = columns_of(D)
    through = r.acc.at[:, 0:D], r.acc.at[:, D : 2 * D]
    loads = [
        pltpu.make_async_copy(w.at[0], there, r.local.at[i])
        for i, (w, there) in enumerate(zip((r.w_in, r.w_dn), through))
    ]
    for load in loads:
        load.start()
    r.square[...] = jnp.zeros_like(r.square)
    for read in reads[:2]:
        read.wait()
    for part in range(2):
        for m in range(3):
            first = m * D + part * width
            r.shard[part, :, m * width : (m + 1) * width] = r.qkv_shard[:, first : first + width]
        r.shard[part, :, 3 * width :] = r.proj_shard[:, part * width : (part + 1) * width]
    for read in reads[2:8]:
        read.wait()
    assign = r.assign[...].astype(single)
    r.square[0:E, 0:rows] = r.router[...]
    for i, gain in enumerate((r.pre_gain, r.pre_shift, r.mid_gain, r.mid_shift)):
        r.square[E + i : E + i + 1, 0:rows] = gain[...]
    numbers = iota((rows, T), 0).astype(single)
    count = jnp.sum(jnp.where(assign == numbers, 1.0, 0.0), axis=1, keepdims=True)
    lane = iota((rows, LANES), 1)
    r.small_shard[...] = jnp.where(lane == E + 4, count, r.square[...].T[0:rows, :])

    experts.meet()
    core = at.core_peer()
    sends.start(r.shard.at[1 - at.c], r.other, r.own_recv.at[0], core)
    sends.start(r.small_shard, r.other_small, r.own_recv.at[1], core)
    gather = Gather(at, sends, r.wts, r.small, (first_cols, last_cols), r.gather_recv, rows)
    own_rows = gather.rows_of(chip_index(at.z, at.y, at.x))

    def both(here, there):
        low, high = jnp.where(at.c == 0, here, there), jnp.where(at.c == 0, there, here)
        return jnp.concatenate([low, high], axis=0).astype(half)

    arrive(r.other, r.send.at[0], r.own_recv.at[0], core)
    r.wts[at.c, own_rows, :] = both(r.shard[at.c], r.other[...])
    gather.along_x(0)
    gather.own(0)
    arrive(r.other_small, r.send.at[0], r.own_recv.at[1], core)
    r.small[own_rows, :] = both(r.small_shard[...], r.other_small[...])
    gather.along_x(2)
    gather.along_x(1)
    gather.own(2)
    for load in loads:
        load.wait()
    experts.share_weights(*through)
    gather.second(0)
    gather.second(2)
    gather.third(0)
    gather.third(2)
    for read in reads[8:]:
        read.wait()
    set_places(E, cap, r)
    to_slots(r, r.cotangent[...], r.out_g)
    gather.own(1)
    gather.fourth(0)
    gather.fourth(2)
    gather.second(1)
    experts.send_out(1)
    gather.finish(0)
    place = lax.rem(iota((D, LANES), 0), rows)
    column = r.small[:, E + 4 : E + 5].astype(single)
    total = jnp.sum(jnp.where(place == iota((D, LANES), 1), column, 0.0), axis=0, keepdims=True)
    r.counts[...] = jnp.broadcast_to(total, r.counts.shape)

    def between():
        gather.third(1)

    def then():
        gather.fourth(1)
        gather.finish(1)

    gate = attend(E, r, r.wts, r.small, between, then)
    to_slots(r, r.hid_b[...], r.out_h)
    gates = jnp.sum(r.place[...].astype(single) * gate, axis=0, keepdims=True)
    r.gates[...] = jnp.broadcast_to(gates, r.gates.shape)
    experts.send_out(2, 0)
    experts.run()
    experts.end_weights()
    experts.turn_rows()
    experts.start_grads(1)
    experts.own_grads(1, None)
    transposes(r)
    experts.wait_returns(1, 2)

    grad_gate = sum(r.ret_gg[i, 0:1, :] for i in range(E))
    grad_gate = jnp.sum(r.place[...].astype(single) * grad_gate, axis=1, keepdims=True)
    mid_gain, mid_shift = backward_body(E, total_tokens, r, r.wts, r.small, r.counts[0:1], grad_gate)
    first = SumScatter(at, sends, first_cols, r, r.sum_recv.at[0])
    last = SumScatter(at, sends, last_cols, r, r.sum_recv.at[1])
    smalls = SmallSum(at, sends, r, rows)

    def give_last(here, value):
        r.give[here, last_cols] = value.astype(half)

    def keep_last(here, value):
        r.acc[here, last_cols] = value

    def give_first(here, value):
        r.give[here, first_cols] = value.astype(half)

    def keep_first(here, value):
        r.acc[here, first_cols] = value

    proj_weight_grad(r, 1 - at.c, give_last)
    last.swap()
    proj_weight_grad(r, at.c, keep_last)
    attend_back(r, 1 - at.c)
    qkv_weight_grad(r, 1 - at.c, give_first)
    first.swap()
    last.wait_swap()
    last.one()
    attend_back(r, at.c)
    qkv_weight_grad(r, at.c, keep_first)
    first.wait_swap()
    first.one()
    for dz in at.z_steps() + [0]:
        last.two(dz)
    pre_gain, pre_shift = input_body(E, r, r.wts, r.small)
    chance_sum = jnp.sum(r.probs[...], axis=0, keepdims=True)
    r.pack[...] = small_grads(
        E, r.router_sum[...], (pre_gain, pre_shift, mid_gain, mid_shift), chance_sum, rows, D
    )
    smalls.zero()
    steps_z = at.z_steps()
    first.two(steps_z[0])
    experts.wait_returns(0)
    set_output(r)
    smalls.one()
    writes = [
        pltpu.make_async_copy(there, dst, r.writes.at[i])
        for i, (there, dst) in enumerate((
            (r.input_grad, r.y_input_grad), (r.layer_out, r.y_layer_out), (r.small_out, r.y_small_out),
            (r.qkv_grad, r.y_qkv_grad), (r.proj_grad, r.y_proj_grad),
        ))
    ]
    for write in writes[:2]:
        write.start()
    if len(steps_z) > 1:
        first.two(steps_z[1])
    pieces = r.resid, r.grad_res
    leaving = []

    def store(i, rows_at, value):
        n = len(leaving) % 2
        if len(leaving) > 1:
            leaving[-2].wait()
        pieces[n][0 : rows_at.size, :] = value
        copy = pltpu.make_async_copy(
            pieces[n].at[0 : rows_at.size], (r.in_own, r.dn_own)[i].at[0, rows_at, :], r.local.at[2 + n]
        )
        copy.start()
        leaving.append(copy)

    experts.start_grads(0)
    for dz in steps_z[2:]:
        first.two(dz)
    smalls.two()
    experts.own_grads(0, store)
    first.two(0)
    last.three()
    first.three()
    last.four()
    total = smalls.three()
    first.four()
    total = smalls.four(total)
    scale = r.counts[0:1] * (balance_weight * E / total_tokens)
    chance = jnp.sum(jnp.where(lane == E + 4, total, 0.0), axis=1, keepdims=True)
    chosen = jnp.where((lane == iota((rows, LANES), 0)) & (lane < E), chance * scale, 0.0)
    loss = jnp.sum(jnp.sum(chosen, axis=1, keepdims=True), axis=0, keepdims=True) / total_tokens
    r.square[0:rows, :] = jnp.where(lane == E + 5, loss, total)
    r.small_out[...] = r.square[...].T[0 : r.small_out.shape[0], :]
    writes[2].start()
    last.end()
    first.end()
    half_rows = pl.ds(pl.multiple_of(at.c * rows, rows), rows)
    mine, theirs = r.final[half_rows, :], r.final_other[...]
    for part, value in enumerate((jnp.where(at.c == 0, mine, theirs), jnp.where(at.c == 0, theirs, mine))):
        for m in range(3):
            begin = m * D + part * width
            r.qkv_grad[:, begin : begin + width] = value[:, m * width : (m + 1) * width]
        r.proj_grad[:, part * width : (part + 1) * width] = value[:, 3 * width :]
    for write in writes[3:]:
        write.start()
    experts.end()
    sends.finish()
    for write in writes + leaving[-2:]:
        write.wait()


def out_kernel(E, names, *refs):
    r = Named(names, refs)
    pairs = [
        (r.in_own, r.h0), (r.in_came, r.h1), (r.dn_own, r.h2), (r.dn_came, r.h3),
        (r.layer_in, r.h4), (r.input_in, r.h5), (r.qkv_in, r.h6), (r.proj_in, r.h7),
    ]
    loads = [pltpu.make_async_copy(src, there, r.sems.at[0, i]) for i, (src, there) in enumerate(pairs)]
    outs = [
        (r.h0, r.in_grad), (r.h2, r.dn_grad), (r.h4, r.layer_out), (r.h5, r.input_grad), (r.h6, r.qkv_grad),
        (r.h7, r.proj_grad),
    ]
    stores = [pltpu.make_async_copy(there, dst, r.sems.at[1, i]) for i, (there, dst) in enumerate(outs)]
    for load in loads:
        load.start()
    rows = r.proj_in.shape[0]
    small_load = pltpu.make_async_copy(r.small_in, r.h8, r.sems.at[0, 8])
    small_load.start()
    small_load.wait()
    r.s_router[...] = r.h8[0:E, 0:rows]
    for i, gain in enumerate((r.s_pre_gain, r.s_pre_shift, r.s_mid_gain, r.s_mid_shift)):
        gain[...] = r.h8[E + i : E + i + 1, 0:rows]
    r.s_loss[...] = r.h8[E + 5 : E + 6, 0:1]
    small_outs = [
        (r.s_router, r.router), (r.s_pre_gain, r.pre_gain), (r.s_pre_shift, r.pre_shift),
        (r.s_mid_gain, r.mid_gain), (r.s_mid_shift, r.mid_shift), (r.s_loss, r.loss),
    ]
    small_stores = [
        pltpu.make_async_copy(there, dst, r.sems.at[2, i]) for i, (there, dst) in enumerate(small_outs)
    ]
    for store in small_stores:
        store.start()
    for i, (own, came) in enumerate(((r.h0, r.h1), (r.h2, r.h3))):
        loads[2 * i].wait()
        loads[2 * i + 1].wait()

        @steps(own.shape[1], STEP)
        def _(at):
            own[0, at, :] += sum(came[j, at, :].astype(single) for j in range(came.shape[0]))

        stores[i].start()
    for load, store in zip(loads[4:], stores[2:]):
        load.wait()
        store.start()
    for store in stores + small_stores:
        store.wait()


def on_device(
    tokens_in, out_cotangent, qkv_weight, proj_weight, router_weight, pre_gain, pre_shift, mid_gain, mid_shift,
    expert_in, expert_down, assignment,
):
    T, D = tokens_in.shape
    E, H = lax.axis_size("expert"), lax.axis_size("hid")
    X = H // 2
    Z = E // 2
    cap = 2 * T // E
    G = group_size(E, cap)
    Fq = expert_in.shape[2]
    total_tokens = T * E * H
    rows = proj_weight.shape[0]
    both = ("expert", "hid")
    assign = assignment.reshape(1, T)
    token = ((T, D), half)
    slot = ((E, cap, D), half)
    vectors = dict(pre_gain=pre_gain, pre_shift=pre_shift, mid_gain=mid_gain, mid_shift=mid_shift)
    if X == 2 and E % 2 == 0 and rows % 8 == 0 and E <= rows <= LANES and Fq == D and D % 256 == 0 and T >= 256:
        small_rows = E + 8
        found = call(
            functools.partial(whole_kernel, E, total_tokens, G),
            dict(
                x_tokens=(tokens_in, ANY_SPEC), x_cotangent=(out_cotangent, ANY_SPEC), x_assign=(assign, ANY_SPEC),
                x_qkv=(qkv_weight, ANY_SPEC), x_proj=(proj_weight, ANY_SPEC), x_router=(router_weight.T, ANY_SPEC),
                x_pre_gain=(pre_gain.reshape(1, rows), ANY_SPEC), x_pre_shift=(pre_shift.reshape(1, rows), ANY_SPEC),
                x_mid_gain=(mid_gain.reshape(1, rows), ANY_SPEC), x_mid_shift=(mid_shift.reshape(1, rows), ANY_SPEC),
                w_in=(expert_in, ANY_SPEC), w_dn=(expert_down, ANY_SPEC),
            ),
            dict(
                y_layer_out=token + (ANY_SPEC,), y_input_grad=token + (ANY_SPEC,),
                y_qkv_grad=((rows, 3 * D), single, ANY_SPEC), y_proj_grad=((rows, D), single, ANY_SPEC),
                y_small_out=((small_rows, LANES), single, ANY_SPEC),
                in_own=((1, D, Fq), single, ANY_SPEC), dn_own=((1, Fq, D), single, ANY_SPEC),
                in_came=((X - 1, D, Fq), half, ANY_SPEC), dn_came=((X - 1, Fq, D), half, ANY_SPEC),
            ),
            dict(
                tokens=pltpu.VMEM(*token), cotangent=pltpu.VMEM(*token), assign=pltpu.VMEM((1, T), jnp.int32),
                qkv_shard=pltpu.VMEM((rows, 3 * D), single), proj_shard=pltpu.VMEM((rows, D), single),
                router=pltpu.VMEM((E, rows), single), pre_gain=pltpu.VMEM((1, rows), single),
                pre_shift=pltpu.VMEM((1, rows), single), mid_gain=pltpu.VMEM((1, rows), single),
                mid_shift=pltpu.VMEM((1, rows), single), layer_out=pltpu.VMEM(*token), input_grad=pltpu.VMEM(*token),
                qkv_grad=pltpu.VMEM((rows, 3 * D), single), proj_grad=pltpu.VMEM((rows, D), single),
                small_out=pltpu.VMEM((small_rows, LANES), single),
                **whole_scratch(E, T, D, cap, rows), **model_scratch(E, T, D, cap), **end_scratch(T, D),
                **expert_scratch(E, X, cap, D, Fq),
            ),
            1, "layer",
        )
        layer_out, input_grad, qkv_grad, proj_grad, small_out, in_own, dn_own, in_came, dn_came = found
        vector = ((1, rows), single, ANY_SPEC)
        found = call(
            functools.partial(out_kernel, E),
            dict(
                layer_in=(layer_out, ANY_SPEC), input_in=(input_grad, ANY_SPEC),
                qkv_in=(qkv_grad, ANY_SPEC), proj_in=(proj_grad, ANY_SPEC),
                in_own=(in_own, ANY_SPEC), dn_own=(dn_own, ANY_SPEC),
                in_came=(in_came, ANY_SPEC), dn_came=(dn_came, ANY_SPEC), small_in=(small_out, ANY_SPEC),
            ),
            dict(
                layer_out=token + (ANY_SPEC,), input_grad=token + (ANY_SPEC,),
                qkv_grad=((rows, 3 * D), single, ANY_SPEC), proj_grad=((rows, D), single, ANY_SPEC),
                in_grad=((1, D, Fq), single, ANY_SPEC), dn_grad=((1, Fq, D), single, ANY_SPEC),
                router=((E, rows), single, ANY_SPEC), pre_gain=vector, pre_shift=vector, mid_gain=vector,
                mid_shift=vector, loss=((1, 1), single, ANY_SPEC),
            ),
            dict(
                h0=pltpu.VMEM((1, D, Fq), single), h1=pltpu.VMEM((X - 1, D, Fq), half),
                h2=pltpu.VMEM((1, Fq, D), single), h3=pltpu.VMEM((X - 1, Fq, D), half),
                h4=pltpu.VMEM(*token), h5=pltpu.VMEM(*token), h6=pltpu.VMEM((rows, 3 * D), single),
                h7=pltpu.VMEM((rows, D), single), h8=pltpu.VMEM((small_rows, LANES), single),
                s_router=pltpu.VMEM((E, rows), single), s_pre_gain=pltpu.VMEM((1, rows), single),
                s_pre_shift=pltpu.VMEM((1, rows), single), s_mid_gain=pltpu.VMEM((1, rows), single),
                s_mid_shift=pltpu.VMEM((1, rows), single), s_loss=pltpu.VMEM((1, 1), single), sems=DMA((3, 9)),
            ),
            None, "results",
        )
        layer_out, input_grad, qkv_grad, proj_grad, in_grad, dn_grad, router, *grads, loss = found
        return (
            layer_out, loss.reshape(()), input_grad, qkv_grad, proj_grad, router.T,
            *[value.reshape(rows) for value in grads], in_grad, dn_grad,
        )

    small_in = jnp.concatenate([router_weight] + [value[:, None] for value in vectors.values()], axis=1)
    small_in = jnp.pad(small_in, ((0, 0), (0, LANES - small_in.shape[1])))
    shard = jnp.concatenate([qkv_weight, proj_weight], axis=1).astype(half)
    wts = lax.all_gather(shard, both, axis=0, tiled=True).reshape(D, 4, 2, D // 2)
    wts = wts.transpose(2, 0, 1, 3).reshape(2, D, 2 * D)
    small = lax.all_gather(small_in.astype(half), both, axis=0, tiled=True)
    onehot = assignment[:, None] == jnp.arange(LANES, dtype=jnp.int32)[None, :]
    counts = lax.psum(jnp.sum(onehot.astype(single), axis=0), both)
    saved = dict(
        hid_a=token, qkv=((2, T, 3 * D // 2), half), att=token, resid=((T, D), single), hid_b=token,
        probs=((T, LANES), single),
    )
    given = dict(tokens=tokens_in, cotangent=out_cotangent, assign=assign, wts=wts, small=small)
    out_h, out_g, *rest = call(
        functools.partial(start_kernel, E), given, dict(out_h=slot, out_g=slot, **saved),
        model_scratch(E, T, D, cap), None, "start",
    )
    ret_o, ret_g, in_own, dn_own, in_came, dn_came = call(
        functools.partial(expert_kernel, E, X, G),
        dict(out_h=out_h, out_g=out_g, w_in=expert_in[0], w_dn=expert_down[0]),
        dict(
            ret_o=slot, ret_g=slot, in_grad=((D, Fq), single), dn_grad=((Fq, D), single),
            in_came=((X - 1, D, Fq), half), dn_came=((X - 1, Fq, D), half),
        ),
        expert_scratch(E, X, cap, D, Fq), 1, "experts",
    )
    in_grad = in_own + jnp.sum(in_came.astype(single), axis=0)
    dn_grad = dn_own + jnp.sum(dn_came.astype(single), axis=0)
    layer_out, input_grad, weight_grads, packed = call(
        functools.partial(end_kernel, E, total_tokens),
        dict(
            **given, counts=jnp.broadcast_to(counts[None, :], (8, LANES)), **dict(zip(saved, rest)),
            ret_o=ret_o, ret_g=ret_g,
        ),
        dict(
            layer_out=token, input_grad=token, weight_grads=((2, D, 2 * D), single),
            small_out=((D, LANES), single),
        ),
        dict(**model_scratch(E, T, D, cap), **end_scratch(T, D)), None, "end",
    )
    gathered = weight_grads.reshape(2, D, 4, D // 2).transpose(1, 2, 0, 3).reshape(D, 4 * D)
    gathered = lax.psum_scatter(gathered, both, scatter_dimension=0, tiled=True)
    small_out = lax.psum_scatter(packed, both, scatter_dimension=0, tiled=True)
    chance = lax.psum(jnp.sum(rest[-1], axis=0), both)
    balance_loss = jnp.sum(chance * counts) * (balance_weight * E / total_tokens) / total_tokens
    return (
        layer_out, balance_loss, input_grad, gathered[:, : 3 * D], gathered[:, 3 * D :], small_out[:, :E],
        *[small_out[:, E + i] for i in range(4)], in_grad[None], dn_grad[None],
    )


def solution(mesh):
    in_specs = (
        P(("expert", "hid"), None),
        P(("expert", "hid"), None),
        P(("expert", "hid"), None),
        P(("expert", "hid"), None),
        P(("expert", "hid"), None),
        P(("expert", "hid")),
        P(("expert", "hid")),
        P(("expert", "hid")),
        P(("expert", "hid")),
        P("expert", None, "hid"),
        P("expert", "hid", None),
        P(("expert", "hid")),
    )
    out_specs = (
        P(("expert", "hid"), None),
        P(),
        P(("expert", "hid"), None),
        P(("expert", "hid"), None),
        P(("expert", "hid"), None),
        P(("expert", "hid"), None),
        P(("expert", "hid")),
        P(("expert", "hid")),
        P(("expert", "hid")),
        P(("expert", "hid")),
        P("expert", None, "hid"),
        P("expert", "hid", None),
    )
    return jax.shard_map(
        on_device, mesh=mesh, in_specs=in_specs, out_specs=out_specs, check_vma=False
    )
```

```python
import functools

import jax
import jax.numpy as jnp
from jax import lax
from jax.experimental import pallas as pl
from jax.experimental.pallas import tpu as pltpu
from jax.sharding import PartitionSpec as P

epsilon = 1e-05
balance_weight = 3.0
masked_score = -1000000000.0


MESH = pl.DeviceIdType.MESH
DMA = pltpu.SemaphoreType.DMA
VMEM_SPEC = pl.BlockSpec(memory_space=pltpu.VMEM)
ANY_SPEC = pl.BlockSpec(memory_space=pl.ANY)
half = jnp.bfloat16
single = jnp.float32
STEP = 32


def remote(src, dst, send_sem, recv_sem, device):
    return pltpu.make_async_remote_copy(
        src_ref=src, dst_ref=dst, send_sem=send_sem, recv_sem=recv_sem,
        device_id=device, device_id_type=MESH,
    )


def dot(a, b):
    return jnp.dot(a, b, preferred_element_type=single)


def dot_cols(a, b):
    return lax.dot_general(a, b, (((1,), (1,)), ((), ())), preferred_element_type=single)


def dot_rows(a, b):
    return lax.dot_general(a, b, (((0,), (0,)), ((), ())), preferred_element_type=single)


def grad_rows(size):
    return 256 if size % 256 == 0 else 128


def steps(count, step):
    def run(body):
        @pl.loop(0, count // step)
        def _(i):
            body(pl.ds(pl.multiple_of(i * step, step), step))
    return run


class Named:
    def __init__(self, names, refs):
        self.__dict__.update(zip(names, refs, strict=True))


def expert_scratch(E, X, cap, D, Fq):
    P, token = 2 * X, (E, cap, D)
    return dict(
        xh=pltpu.VMEM(token, half), xg=pltpu.VMEM(token, half),
        win=pltpu.VMEM((P, D, Fq), half), wdn=pltpu.VMEM((P, Fq, D), half),
        act=pltpu.VMEM((P, E * cap, Fq), half), gbef=pltpu.VMEM((P, E * cap, Fq), half),
        to=pltpu.VMEM(token, half), tg=pltpu.VMEM(token, half), xh_t=pltpu.VMEM((D, E * cap), half),
        core_in=pltpu.VMEM((X, D, Fq), half), core_dn=pltpu.VMEM((X, Fq, D), half),
        xgate=pltpu.VMEM((E, 8, E * cap), single), raw=pltpu.VMEM(token, half),
        tgg=pltpu.VMEM((E, 8, E * cap), single), ret_gg=pltpu.VMEM((E, 8, E * cap), single),
        send_a=DMA((3, E)), recv_a=DMA((3, E)), send_r=DMA((3, E)), recv_r=DMA((3, E)),
        send_w=DMA((2, X)), recv_w=DMA((2, X)), send_f=DMA((2, X)), recv_f=DMA((2, X)),
        send_d=DMA((2, X)), recv_d=DMA((2, X)), send_s=DMA((2, X)), recv_s=DMA((2, X)),
    )


class Experts:
    def __init__(self, E, X, G, r, gated):
        self.E, self.X, self.G, self.r, self.gated = E, X, G, r, gated
        self.e, self.h = lax.axis_index("expert"), lax.axis_index("hid")
        self.x, self.c = lax.div(self.h, 2), lax.rem(self.h, 2)
        self.cap, self.D = r.out_h.shape[1], r.out_h.shape[2]
        self.Fq = r.win.shape[2]
        self.NG, self.rows = E // G, G * self.cap
        self.core_peer = (self.e, self.x * 2 + 1 - self.c)
        self.landing = r.raw if gated else r.xg

    def expert_at(self, k):
        found, bit = 0, 1
        while bit < self.E:
            a, b = lax.rem(lax.div(self.e, bit), 2), lax.rem(lax.div(k, bit), 2)
            found = found + bit * (a + b - 2 * a * b)
            bit *= 2
        return found

    def x_peer(self, d):
        return (self.e, lax.rem(self.x + d, self.X) * 2 + self.c)

    def part(self, j, core):
        return lax.rem(self.x + j, self.X) * 2 + core

    def greet(self):
        barrier = pltpu.get_barrier_semaphore()

        @pl.loop(1, self.E)
        def _(k):
            pl.semaphore_signal(
                barrier, inc=1, device_id=(self.expert_at(k), self.h), device_id_type=MESH
            )

        for d in range(1, self.X):
            pl.semaphore_signal(barrier, inc=1, device_id=self.x_peer(d), device_id_type=MESH)
        pl.semaphore_signal(barrier, inc=1, device_id=self.core_peer, device_id_type=MESH)

    def meet(self):
        pl.semaphore_wait(pltpu.get_barrier_semaphore(), self.E - 1 + self.X - 1 + 1)

    def weight_to_x(self, i, d):
        r, w, q = self.r, (self.r.win, self.r.wdn)[i], self.part(0, self.c)
        return remote(
            w.at[q], w.at[q], r.send_w.at[i, d], r.recv_w.at[i, self.X - d], self.x_peer(d)
        )

    def weight_to_core(self, i, j, core):
        r, w, q = self.r, (self.r.win, self.r.wdn)[i], self.part(j, core)
        return remote(w.at[q], w.at[q], r.send_f.at[i, j], r.recv_f.at[i, j], self.core_peer)

    def share_weights(self, w_in, w_dn):
        r, q = self.r, self.part(0, self.c)

        @steps(self.D, STEP)
        def _(at):
            r.win[q, at, :] = w_in[at, :].astype(half)

        for d in range(1, self.X):
            self.weight_to_x(0, d).start()

        @steps(self.Fq, STEP)
        def _(at):
            r.wdn[q, at, :] = w_dn[at, :].astype(half)

        for d in range(1, self.X):
            self.weight_to_x(1, d).start()
        for i in range(2):
            self.weight_to_core(i, 0, self.c).start()

    def wait_weights(self, j, core):
        for i in range(2):
            if core == 0:
                if j:
                    self.weight_to_x(i, self.X - j).wait_recv()
                    self.weight_to_core(i, j, self.c).start()
            else:
                self.weight_to_core(i, j, 1 - self.c).wait_recv()

    def end_weights(self):
        for i in range(2):
            for j in range(self.X):
                self.weight_to_core(i, j, self.c).wait_send()
                if j:
                    self.weight_to_x(i, j).wait_send()

    def dispatch(self, k, part):
        r = self.r
        peer = self.expert_at(k)
        if part == 2:
            src, dst = r.gates, r.xgate
        else:
            src, dst = ((r.out_h.at[peer], r.xh), (r.out_g.at[peer], self.landing))[part]
        return remote(src, dst.at[k], r.send_a.at[part, k], r.recv_a.at[part, k], (peer, self.h))

    def send_out(self, *parts):
        r = self.r

        @pl.loop(1, self.E)
        def _(k):
            for part in parts:
                self.dispatch(k, part).start()

        for part in parts:
            if part == 2:
                r.xgate[0] = r.gates[...]
            else:
                src, dst = ((r.out_h, r.xh), (r.out_g, self.landing))[part]
                dst[0] = src[self.e]

    def own_lanes(self):
        shape = (self.cap, self.E * self.cap)
        return iota(shape, 1) == iota(shape, 0) + self.e * self.cap

    def take(self, g):
        r, cap = self.r, self.cap

        @pl.loop(0, self.G)
        def _(i):
            k = g * self.G + i

            @pl.when(k > 0)
            def _():
                for part in (1, 2, 0) if self.gated else (1, 0):
                    self.dispatch(k, part).wait_recv()

            if self.gated:
                gate = jnp.where(self.own_lanes(), r.xgate[k, 0:1, :], 0.0)
                gate = jnp.sum(gate, axis=1, keepdims=True)
                r.xg[k] = (gate * r.raw[k].astype(single)).astype(half)

    def compute(self, g):
        r = self.r
        slots = pl.ds(g * self.G, self.G)
        at = pl.ds(pl.multiple_of(g * self.rows, self.rows), self.rows)
        xh_g = r.xh[slots].reshape(self.rows, self.D)
        xg_g = r.xg[slots].reshape(self.rows, self.D)
        parts = []
        for n in range(2 * self.X):
            j, core = n // 2, n % 2
            q = self.part(j, self.c if core == 0 else 1 - self.c)
            parts.append(q)

            @pl.when(g == 0)
            def _():
                self.wait_weights(j, core)

            v = dot(xh_g, r.win[q])
            ga = dot_cols(xg_g, r.wdn[q])
            cdf = 0.5 * (1.0 + lax.erf(v * (0.5 ** 0.5)))
            slope = cdf + v * (jnp.exp(-0.5 * v * v) * 0.3989422804014327)
            r.act[q, at, :] = (v * cdf).astype(half)
            r.gbef[q, at, :] = (slope * ga).astype(half)
        out = sum(dot(r.act[q, at, :], r.wdn[q]) for q in parts)
        gin = sum(dot_cols(r.gbef[q, at, :], r.win[q]) for q in parts)
        shape = (self.G, self.cap, self.D)
        r.to[slots] = out.astype(half).reshape(shape)
        r.tg[slots] = gin.astype(half).reshape(shape)
        if self.gated:
            @pl.loop(0, self.G)
            def _(i):
                k = g * self.G + i
                toward = jnp.sum(r.raw[k].astype(single) * r.to[k].astype(single), axis=1, keepdims=True)
                row = jnp.sum(jnp.where(self.own_lanes(), toward, 0.0), axis=0, keepdims=True)
                r.tgg[k] = jnp.broadcast_to(row, r.tgg.shape[1:])

    def give_back(self, k, part):
        r = self.r
        src, dst = ((r.to, r.ret_o), (r.tg, r.ret_g), (r.tgg, r.ret_gg))[part]
        return remote(
            src.at[k], dst.at[self.e], r.send_r.at[part, k], r.recv_r.at[part, k],
            (self.expert_at(k), self.h),
        )

    def run(self):
        r = self.r
        parts = (1, 2) if self.gated else (1,)

        @pl.loop(0, self.NG)
        def _(g):
            self.take(g)
            self.compute(g)

            @pl.loop(0, self.G)
            def _(i):
                k = g * self.G + i

                @pl.when(k > 0)
                def _():
                    for part in parts:
                        self.give_back(k, part).start()

        r.ret_o[self.e] = r.to[0]
        r.ret_g[self.e] = r.tg[0]
        if self.gated:
            r.ret_gg[self.e] = r.tgg[0]

    def send_outputs(self):
        @pl.loop(1, self.E)
        def _(k):
            self.give_back(k, 0).start()

    def grad_to_core(self, i, j):
        r, w, came = self.r, (self.r.win, self.r.wdn)[i], (self.r.core_in, self.r.core_dn)[i]
        return remote(w.at[j], came.at[j], r.send_d.at[i, j], r.recv_d.at[i, j], self.core_peer)

    def grad_to_x(self, i, j):
        r, w, came = self.r, (self.r.win, self.r.wdn)[i], (self.r.in_came, self.r.dn_came)[i]
        return remote(
            w.at[self.X + j], came.at[self.X - j - 1], r.send_s.at[i, j], r.recv_s.at[i, self.X - j],
            self.x_peer(j),
        )

    def grad(self, i, q, at):
        r, T = self.r, self.E * self.cap
        if i == 0:
            return dot(r.xh_t[at, :], r.gbef[q])
        return dot_rows(r.act[q, :, at], r.xg[...].reshape(T, self.D))

    def start_grads(self, j):
        r = self.r
        for i, (w, size) in enumerate(((r.win, self.D), (r.wdn, self.Fq))):
            @steps(size, grad_rows(size))
            def _(at):
                w[j, at, :] = self.grad(i, self.part(j, 1 - self.c), at).astype(half)

            self.grad_to_core(i, j).start()

    def own_grads(self, j, store):
        r = self.r
        for i, (w, came, size) in enumerate(((r.win, r.core_in, self.D), (r.wdn, r.core_dn, self.Fq))):
            self.grad_to_core(i, j).wait_recv()
            if j:
                @steps(size, grad_rows(size))
                def _(at):
                    total = self.grad(i, self.part(j, self.c), at) + came[j, at, :].astype(single)
                    w[self.X + j, at, :] = total.astype(half)

                self.grad_to_x(i, j).start()
            else:
                for first in range(0, size, grad_rows(size)):
                    at = pl.ds(first, grad_rows(size))
                    store(i, at, self.grad(i, self.part(j, self.c), at) + came[j, at, :].astype(single))

    def turn_rows(self):
        self.r.xh_t[...] = self.r.xh[...].reshape(self.E * self.cap, self.D).T

    def wait_returns(self, *parts):
        @pl.loop(1, self.E)
        def _(k):
            for part in parts:
                self.give_back(k, part).wait_recv()

    def end(self):
        for i in range(2):
            for j in range(self.X):
                self.grad_to_core(i, j).wait_send()
                if j:
                    self.grad_to_x(i, j).wait()

        @pl.loop(1, self.E)
        def _(k):
            for part in range(3 if self.gated else 2):
                self.dispatch(k, part).wait_send()
                self.give_back(k, part).wait_send()


def expert_kernel(E, X, G, names, *refs):
    r = Named(names, refs)
    experts = Experts(E, X, G, r, False)
    experts.greet()
    experts.meet()
    experts.send_out(0, 1)
    experts.share_weights(r.w_in, r.w_dn)
    experts.run()
    experts.send_outputs()
    experts.end_weights()
    experts.turn_rows()

    def store(i, at, value):
        (r.in_grad, r.dn_grad)[i][at, :] = value

    for j in list(range(1, X)) + [0]:
        experts.start_grads(j)
        experts.own_grads(j, store)
    experts.wait_returns(0, 1)
    experts.end()


def group_size(E, cap):
    return max(1, min(E, GROUP_ROWS // cap))


def call(kernel, ins, outs, scratch, collective, name):
    names = list(ins) + list(outs) + list(scratch)
    extra = dict() if collective is None else dict(collective_id=collective, has_side_effects=True)
    pairs = [value if isinstance(value, tuple) else (value, VMEM_SPEC) for value in ins.values()]
    return pl.pallas_call(
        functools.partial(kernel, names),
        out_shape=tuple(jax.ShapeDtypeStruct(value[0], value[1]) for value in outs.values()),
        in_specs=[spec for _, spec in pairs],
        out_specs=tuple(value[2] if len(value) > 2 else VMEM_SPEC for value in outs.values()),
        scratch_shapes=list(scratch.values()),
        compiler_params=pltpu.CompilerParams(vmem_limit_bytes=VMEM_LIMIT, **extra),
        name=name,
    )(*[array for array, _ in pairs])


HEAD_DIM = 64
LANES = 128


def norm_stats(values):
    average = jnp.mean(values, axis=-1, keepdims=True)
    centred = values - average
    spread = jnp.mean(centred * centred, axis=-1, keepdims=True)
    return centred, lax.rsqrt(spread + epsilon)


def norm_back(grad, values, gain):
    centred, rate = norm_stats(values)
    unit = centred * rate
    scaled = grad * gain
    toward = rate * (
        scaled
        - jnp.mean(scaled, axis=-1, keepdims=True)
        - unit * jnp.mean(scaled * unit, axis=-1, keepdims=True)
    )
    gain_grad = jnp.sum(grad * unit, axis=0, keepdims=True)
    shift_grad = jnp.sum(grad, axis=0, keepdims=True)
    return toward, gain_grad, shift_grad


def iota(shape, axis):
    return lax.broadcasted_iota(jnp.int32, shape, axis)


def slot_places(assign, capacity):
    T = assign.shape[1]
    down, across = iota((T, T), 0), iota((T, T), 1)
    column = jnp.sum(jnp.where(down == across, assign, 0.0), axis=1, keepdims=True)
    same = column == assign
    rank_column = jnp.sum(jnp.where(same & (across < down), 1.0, 0.0), axis=1, keepdims=True)
    rank_row = jnp.sum(jnp.where(same & (down < across), 1.0, 0.0), axis=0, keepdims=True)
    place_column = (column * capacity + rank_column).astype(jnp.int32)
    place_row = (assign * capacity + rank_row).astype(jnp.int32)
    return column.astype(jnp.int32), place_column, place_row


def head_probs(q_one, k_pair, allowed):
    scores = dot_cols(q_one, k_pair) * (HEAD_DIM ** -0.5)
    scores = jnp.where(allowed, scores, masked_score)
    powers = jnp.exp(scores - jnp.max(scores, axis=-1, keepdims=True))
    return powers * (1.0 / jnp.sum(powers, axis=-1, keepdims=True))


def head_masks(T):
    first = iota((T, LANES), 1) < HEAD_DIM
    low_lanes = jnp.where(first, 1.0, 0.0).astype(half)
    high_lanes = jnp.where(first, 0.0, 1.0).astype(half)
    return first, (low_lanes, high_lanes)


def columns_of(D):
    return pl.ds(0, 3 * D // 2), pl.ds(3 * D // 2, D // 2)


def pair_columns(D, m, p):
    return pl.ds(pl.multiple_of((3 * p + m) * LANES, LANES), LANES)


def attend(E, r, wts, small, between=lambda: None, then=lambda: None):
    T, D = r.tokens.shape
    first_cols, last_cols = columns_of(D)
    small_t = small[...].astype(single).T
    inputs = r.tokens[...].astype(single)
    centred, rate = norm_stats(inputs)
    r.hid_a[...] = (centred * rate * small_t[E : E + 1] + small_t[E + 1 : E + 2]).astype(half)
    for part in range(2):
        r.qkv[part] = dot(r.hid_a[...], wts[part, :, first_cols]).astype(half)
    between()
    allowed = iota((T, T), 1) <= iota((T, T), 0)
    first, masks = head_masks(T)
    count = D // LANES // 2

    @pl.loop(0, 2 * count)
    def _(i):
        part, p = lax.div(i, count), lax.rem(i, count)
        q_pair, k_pair, v_pair = (r.qkv[part, :, pair_columns(D, m, p)] for m in range(3))
        mixed = [
            dot(head_probs(q_pair * mask, k_pair, allowed).astype(half), v_pair) for mask in masks
        ]
        at = pl.ds(pl.multiple_of(i * LANES, LANES), LANES)
        r.att[:, at] = jnp.where(first, mixed[0], mixed[1]).astype(half)

    then()
    for part in range(2):
        at = pl.ds(part * (D // 2), D // 2)
        r.resid[:, at] = r.tokens[:, at].astype(single) + dot(r.att[...], wts[part, :, last_cols])
    centred, rate = norm_stats(r.resid[...])
    r.hid_b[...] = (centred * rate * small_t[E + 2 : E + 3] + small_t[E + 3 : E + 4]).astype(half)
    lane = iota((T, LANES), 1)
    logits = jnp.where(lane < E, dot(r.hid_b[...], small[...]), -1e30)
    powers = jnp.exp(logits - jnp.max(logits, axis=-1, keepdims=True))
    chance = powers * (1.0 / jnp.sum(powers, axis=-1, keepdims=True))
    r.probs[...] = chance
    return jnp.sum(jnp.where(r.mine[...] > 0.0, chance, 0.0), axis=1, keepdims=True)


def set_places(E, cap, r):
    T = r.tokens.shape[0]
    column, place_column, place_row = slot_places(r.assign[...].astype(single), cap)
    r.pick[...] = jnp.where(iota((E * cap, T), 0) == place_row, 1.0, 0.0).astype(half)
    r.place[...] = jnp.where(iota((T, E * cap), 1) == place_column, 1.0, 0.0).astype(half)
    r.mine[...] = jnp.where(iota((T, LANES), 1) == column, 1.0, 0.0)


def to_slots(r, rows, out):
    out[...] = dot(r.pick[...], rows).astype(half).reshape(out.shape)


def set_output(r):
    slots, D = r.place.shape[1], r.tokens.shape[1]
    gate = jnp.sum(r.mine[...] * r.probs[...], axis=1, keepdims=True)
    expert_tok = dot(r.place[...], r.ret_o[...].reshape(slots, D))
    r.layer_out[...] = (r.resid[...] + gate * expert_tok).astype(half)
    return jnp.sum(r.cotangent[...].astype(single) * expert_tok, axis=1, keepdims=True)


def backward_body(E, total_tokens, r, wts, small, counts, grad_gate):
    T, D = r.tokens.shape
    slots = r.place.shape[1]
    small_t = small[...].astype(single).T
    cot = r.cotangent[...].astype(single)
    lane = iota((T, LANES), 1)
    chance = r.probs[...]
    mine = r.mine[...]
    scale = counts * (balance_weight * E / total_tokens)
    grad_probs = mine * grad_gate + scale
    grad_logits = chance * (grad_probs - jnp.sum(chance * grad_probs, axis=1, keepdims=True))
    grad_logits = jnp.where(lane < E, grad_logits, 0.0).astype(half)
    r.router_sum[...] = dot_rows(r.hid_b[...], grad_logits)
    grad_hidden_b = dot(r.place[...], r.ret_g[...].reshape(slots, D)) + dot_cols(grad_logits, small[...])
    toward, mid_gain, mid_shift = norm_back(grad_hidden_b, r.resid[...], small_t[E + 2 : E + 3])
    r.grad_res[...] = cot + toward
    r.gproj[...] = r.grad_res[...].astype(half)
    _, last_cols = columns_of(D)
    r.gatt[...] = sum(
        dot_cols(r.gproj[:, part * (D // 2) : (part + 1) * (D // 2)], wts[part, :, last_cols])
        for part in range(2)
    ).astype(half)
    return mid_gain, mid_shift


def attend_back(r, part, p):
    T, D = r.tokens.shape
    allowed = iota((T, T), 1) <= iota((T, T), 0)
    first, masks = head_masks(T)
    q_pair, k_pair, v_pair = (r.qkv[part, :, pair_columns(D, m, p)] for m in range(3))
    g_pair = r.gatt[:, pl.ds(pl.multiple_of(part * (D // 2) + p * LANES, LANES), LANES)]
    found = []
    for mask in masks:
        weights = head_probs(q_pair * mask, k_pair, allowed)
        grad_w = dot_cols(g_pair * mask, v_pair)
        grad_s = weights * (grad_w - jnp.sum(weights * grad_w, axis=-1, keepdims=True))
        grad_s = grad_s.astype(half)
        found.append(
            (
                dot(grad_s, k_pair) * (HEAD_DIM ** -0.5),
                dot_rows(grad_s, q_pair) * (HEAD_DIM ** -0.5),
                dot_rows(weights.astype(half), g_pair),
            )
        )
    for m in range(3):
        r.gqkv[part, :, pair_columns(D, m, p)] = jnp.where(first, found[0][m], found[1][m]).astype(half)


def transposes(r):
    r.hid_a_t[...] = r.hid_a[...].T
    r.att_t[...] = r.att[...].T


def qkv_weight_grad(r, part, p, write):
    D = r.hid_a_t.shape[0]
    cols = pl.ds(3 * LANES * p, 3 * LANES)

    @steps(D, 256 if D % 256 == 0 else LANES)
    def _(rows):
        write(rows, cols, dot(r.hid_a_t[rows, :], r.gqkv[part, :, cols]))


def proj_weight_grad(r, part, write):
    D = r.att_t.shape[0]
    cols = pl.ds(pl.multiple_of(part * (D // 2), D // 2), D // 2)

    @steps(D, 256 if D % 256 == 0 else LANES)
    def _(rows):
        write(rows, dot(r.att_t[rows, :], r.gproj[:, cols]))


def input_body(E, r, wts, small):
    small_t = small[...].astype(single).T
    first_cols, _ = columns_of(r.tokens.shape[1])
    grad_hidden_a = sum(dot_cols(r.gqkv[part], wts[part, :, first_cols]) for part in range(2))
    toward, pre_gain, pre_shift = norm_back(
        grad_hidden_a, r.tokens[...].astype(single), small_t[E : E + 1]
    )
    r.input_grad[...] = (r.grad_res[...] + toward).astype(half)
    return pre_gain, pre_shift


def small_grads(E, router, rows, chance_sum, block, D):
    lane = iota((D, LANES), 1)
    eight = iota((LANES, D), 0)
    stacked = jnp.zeros((LANES, D), single)
    for i, row in enumerate(rows):
        stacked = jnp.where(eight == E + i, row, stacked)
    packed = jnp.where(lane < E, router, stacked.T)
    if block:
        place = lax.rem(iota((D, LANES), 0), block)
        copy = jnp.sum(jnp.where(place == lane, chance_sum, 0.0), axis=1, keepdims=True)
        packed = jnp.where(lane == E + 4, copy, packed)
    return packed


class Place:
    def __init__(self, E):
        e, h = lax.axis_index("expert"), lax.axis_index("hid")
        self.Z = E // 2
        self.z, self.y = lax.div(e, 2), lax.rem(e, 2)
        self.x, self.c = lax.div(h, 2), lax.rem(h, 2)

    def device(self, z, y, x, c):
        return (z * 2 + y, x * 2 + c)

    def z_at(self, d):
        return lax.rem(self.z + d, self.Z)

    def z_peer(self, d):
        return self.device(self.z_at(d), self.y, self.x, self.c)

    def y_peer(self):
        return self.device(self.z, 1 - self.y, self.x, self.c)

    def x_peer(self):
        return self.device(self.z, self.y, 1 - self.x, self.c)

    def core_peer(self):
        return self.device(self.z, self.y, self.x, 1 - self.c)

    def z_steps(self):
        return sorted(range(1, self.Z), key=lambda d: min(d, self.Z - d))

    def greet(self):
        barrier = pltpu.get_barrier_semaphore()
        peers = [self.z_peer(d) for d in range(1, self.Z)]
        peers += [self.y_peer(), self.x_peer(), self.core_peer()]
        for peer in peers:
            pl.semaphore_signal(barrier, inc=1, device_id=peer, device_id_type=MESH)
        pl.semaphore_wait(barrier, len(peers))


def chip_index(z, y, x):
    return (z * 2 + y) * 2 + x


class Sends:
    def __init__(self, sems):
        self.sems, self.started = sems, []

    def start(self, src, dst, recv_sem, device):
        copy = remote(src, dst, self.sems.at[len(self.started)], recv_sem, device)
        copy.start()
        self.started.append(copy)
        return len(self.started) - 1

    def settle(self, n):
        self.started[n].wait_send()
        self.started[n] = None

    def finish(self):
        for copy in self.started:
            if copy is not None:
                copy.wait_send()


def arrive(dst, send_sem, recv_sem, device):
    remote(dst, dst, send_sem, recv_sem, device).wait_recv()


class Gather:
    def __init__(self, at, sends, wts, small, spans, recv, rows):
        self.at, self.sends, self.wts, self.small, self.spans = at, sends, wts, small, spans
        self.recv, self.span = recv, 2 * rows

    def rows_of(self, chip):
        return pl.ds(pl.multiple_of(chip * self.span, self.span), self.span)

    def block(self, o, chip, core):
        if o == len(self.spans):
            return self.small.at[self.rows_of(chip), :]
        return self.wts.at[core, self.rows_of(chip), self.spans[o]]

    def send(self, o, chip, device):
        block = self.block(o, chip, self.at.c)
        self.sends.start(block, block, self.recv.at[0, o, chip], device)

    def share(self, o, chip):
        if o < len(self.spans):
            block = self.block(o, chip, self.at.c)
            self.sends.start(block, block, self.recv.at[1, o, chip], self.at.core_peer())

    def wait(self, o, chip):
        block = self.block(o, chip, self.at.c)
        arrive(block, self.sends.sems.at[0], self.recv.at[0, o, chip], self.at.core_peer())

    def spread(self, o, chip):
        for d in self.at.z_steps():
            self.send(o, chip, self.at.z_peer(d))
        self.send(o, chip, self.at.y_peer())
        self.share(o, chip)

    def along_x(self, o):
        at = self.at
        self.send(o, chip_index(at.z, at.y, at.x), at.x_peer())

    def own(self, o):
        at = self.at
        self.spread(o, chip_index(at.z, at.y, at.x))

    def second(self, o):
        at = self.at
        chip = chip_index(at.z, at.y, 1 - at.x)
        self.wait(o, chip)
        self.spread(o, chip)

    def third(self, o):
        at = self.at
        for x in (at.x, 1 - at.x):
            for d in at.z_steps():
                chip = chip_index(at.z_at(d), at.y, x)
                self.wait(o, chip)
                self.send(o, chip, at.y_peer())
                self.share(o, chip)

    def fourth(self, o):
        at = self.at
        for x in (at.x, 1 - at.x):
            for d in [0] + at.z_steps():
                chip = chip_index(at.z_at(d), 1 - at.y, x)
                self.wait(o, chip)
                self.share(o, chip)

    def finish(self, o):
        if o < len(self.spans):
            @pl.loop(0, 4 * self.at.Z)
            def _(chip):
                block = self.block(o, chip, 1 - self.at.c)
                arrive(block, self.sends.sems.at[0], self.recv.at[1, o, chip], self.at.core_peer())


class SumScatter:
    def __init__(self, at, sends, cols, r, recv):
        self.at, self.sends, self.cols, self.r, self.recv = at, sends, cols, r, recv
        self.span = r.final.shape[0]

    def rows_of(self, chip):
        return pl.ds(pl.multiple_of(chip * self.span, self.span), self.span)

    def swap(self):
        r = self.r
        self.swapped = self.sends.start(
            r.give.at[:, self.cols], r.got.at[:, self.cols], self.recv.at[0], self.at.core_peer()
        )

    def wait_swap(self):
        self.sends.settle(self.swapped)
        there = self.r.got.at[:, self.cols]
        arrive(there, self.sends.sems.at[0], self.recv.at[0], self.at.core_peer())

    def send(self, slot, chip, value, device):
        r, rows = self.r, self.rows_of(chip)
        r.give[rows, self.cols] = value.astype(half)
        self.sends.start(
            r.give.at[rows, self.cols], r.came.at[slot, :, self.cols], self.recv.at[1 + slot], device
        )

    def take(self, slot):
        there = self.r.came.at[slot, :, self.cols]
        arrive(there, self.sends.sems.at[0], self.recv.at[1 + slot], self.at.core_peer())
        return there[...].astype(single)

    def base(self, chip):
        rows = self.rows_of(chip)
        return self.r.acc[rows, self.cols] + self.r.got[rows, self.cols].astype(single)

    def one(self):
        at = self.at
        for dz in at.z_steps() + [0]:
            for x in range(2):
                chip = chip_index(at.z_at(dz), 1 - at.y, x)
                self.send(dz * 2 + x, chip, self.base(chip), at.y_peer())

    def two(self, dz):
        at = self.at
        for x in range(2):
            chip = chip_index(at.z_at(dz), at.y, x)
            value = self.base(chip) + self.take(dz * 2 + x)
            if dz:
                self.send(2 * at.Z + dz * 2 + x, chip, value, at.z_peer(dz))
            else:
                self.r.acc[self.rows_of(chip), self.cols] = value

    def three(self):
        at = self.at
        for flip in (1, 0):
            x = 1 - at.x if flip else at.x
            chip = chip_index(at.z, at.y, x)
            value = self.r.acc[self.rows_of(chip), self.cols]
            for dz in range(1, at.Z):
                value = value + self.take(2 * at.Z + dz * 2 + x)
            if flip:
                self.send(4 * at.Z, chip, value, at.x_peer())
            else:
                self.r.final[:, self.cols] = value

    def four(self):
        at, r = self.at, self.r
        r.final[:, self.cols] += self.take(4 * at.Z)
        rows = self.span // 2
        there = r.final.at[pl.ds(pl.multiple_of((1 - at.c) * rows, rows), rows), self.cols]
        last = self.recv.shape[0] - 1
        self.sends.start(there, r.final_other.at[:, self.cols], self.recv.at[last], at.core_peer())

    def end(self):
        there = self.r.final_other.at[:, self.cols]
        arrive(there, self.sends.sems.at[0], self.recv.at[self.recv.shape[0] - 1], self.at.core_peer())


VMEM_LIMIT = 62 * 1024 * 1024
GROUP_ROWS = 128


def model_scratch(E, T, D, cap):
    slots = E * cap
    return dict(
        pick=pltpu.VMEM((slots, T), half), place=pltpu.VMEM((T, slots), half),
        mine=pltpu.VMEM((T, LANES), single),
    )


def end_scratch(T, D):
    return dict(
        gqkv=pltpu.VMEM((2, T, 3 * D // 2), half), gproj=pltpu.VMEM((T, D), half), gatt=pltpu.VMEM((T, D), half),
        grad_res=pltpu.VMEM((T, D), single), router_sum=pltpu.VMEM((D, LANES), single),
        hid_a_t=pltpu.VMEM((D, T), half), att_t=pltpu.VMEM((D, T), half),
    )


def start_kernel(E, names, *refs):
    r = Named(names, refs)
    cap = r.out_h.shape[1]
    set_places(E, cap, r)
    gate = attend(E, r, r.wts, r.small)
    to_slots(r, r.hid_b[...], r.out_h)
    to_slots(r, (gate * r.cotangent[...].astype(single)).astype(half), r.out_g)


def end_kernel(E, total_tokens, names, *refs):
    r = Named(names, refs)
    D = r.tokens.shape[1]
    set_places(E, r.ret_o.shape[1], r)
    transposes(r)
    mid_gain, mid_shift = backward_body(E, total_tokens, r, r.wts, r.small, r.counts[0:1], set_output(r))
    _, last_cols = columns_of(D)
    for part in range(2):
        def write_first(rows, cols, value):
            r.weight_grads[part, rows, cols] = value

        def write_last(rows, value):
            r.weight_grads[part, rows, last_cols] = value

        for p in range(D // LANES // 2):
            attend_back(r, part, p)
            qkv_weight_grad(r, part, p, write_first)
        proj_weight_grad(r, part, write_last)
    pre_gain, pre_shift = input_body(E, r, r.wts, r.small)
    chance_sum = jnp.sum(r.probs[...], axis=0, keepdims=True)
    r.small_out[...] = small_grads(
        E, r.router_sum[...], (pre_gain, pre_shift, mid_gain, mid_shift), chance_sum, 0, D
    )


class SmallSum:
    def __init__(self, at, sends, r, rows):
        self.at, self.sends, self.r, self.rows = at, sends, r, rows

    def here(self, z, y, x):
        first = chip_index(z, y, x) * 2 * self.rows + self.at.c * self.rows
        return self.r.pack_other[pl.ds(pl.multiple_of(first, self.rows), self.rows), :]

    def send(self, slot, value, device):
        r = self.r
        r.pack_sent[slot] = value
        self.sends.start(r.pack_sent.at[slot], r.pack_came.at[slot], r.pack_recv.at[1 + slot], device)

    def take(self, slot):
        r = self.r
        arrive(r.pack_came.at[slot], r.send.at[0], r.pack_recv.at[1 + slot], self.at.core_peer())
        return r.pack_came[slot]

    def zero(self):
        r = self.r
        self.sends.start(r.pack, r.pack_other, r.pack_recv.at[0], self.at.core_peer())

    def one(self):
        r, at = self.r, self.at
        arrive(r.pack_other, r.send.at[0], r.pack_recv.at[0], at.core_peer())
        r.pack_other[...] += r.pack[...]
        for dz in range(at.Z):
            for x in range(2):
                self.send(dz * 2 + x, self.here(at.z_at(dz), 1 - at.y, x), at.y_peer())

    def two(self):
        at = self.at
        for dz in at.z_steps():
            for x in range(2):
                value = self.here(at.z_at(dz), at.y, x) + self.take(dz * 2 + x)
                self.send(2 * at.Z + dz * 2 + x, value, at.z_peer(dz))

    def three(self):
        at = self.at
        for flip in (1, 0):
            x = 1 - at.x if flip else at.x
            value = self.here(at.z, at.y, x) + self.take(x)
            for dz in range(1, at.Z):
                value = value + self.take(2 * at.Z + dz * 2 + x)
            if flip:
                self.send(4 * at.Z, value, at.x_peer())
        return value

    def four(self, total):
        return total + self.take(4 * self.at.Z)


def whole_scratch(E, T, D, cap, rows):
    Z = E // 2
    slots = 4 * Z + 1
    token = (E, cap, D)
    return dict(
        wts=pltpu.VMEM((2, D, 2 * D), half), small=pltpu.VMEM((D, LANES), half),
        shard=pltpu.VMEM((2, rows, 2 * D), single), small_shard=pltpu.VMEM((rows, LANES), single),
        other=pltpu.VMEM((rows, 2 * D), single), other_small=pltpu.VMEM((rows, LANES), single),
        square=pltpu.VMEM((LANES, LANES), single), counts=pltpu.VMEM((8, LANES), single),
        hid_a=pltpu.VMEM((T, D), half), qkv=pltpu.VMEM((2, T, 3 * D // 2), half), att=pltpu.VMEM((T, D), half),
        resid=pltpu.VMEM((T, D), single), hid_b=pltpu.VMEM((T, D), half),
        probs=pltpu.VMEM((T, LANES), single), gates=pltpu.VMEM((8, E * cap), single),
        out_h=pltpu.VMEM(token, half), out_g=pltpu.VMEM(token, half),
        ret_o=pltpu.VMEM(token, half), ret_g=pltpu.VMEM(token, half),
        acc=pltpu.VMEM((D, 2 * D), single), give=pltpu.VMEM((D, 2 * D), half), got=pltpu.VMEM((D, 2 * D), half),
        came=pltpu.VMEM((slots, 2 * rows, 2 * D), half),
        final=pltpu.VMEM((2 * rows, 2 * D), single), final_other=pltpu.VMEM((rows, 2 * D), single),
        pack=pltpu.VMEM((D, LANES), single), pack_other=pltpu.VMEM((D, LANES), single),
        pack_sent=pltpu.VMEM((slots, rows, LANES), single),
        pack_came=pltpu.VMEM((slots, rows, LANES), single),
        reads=DMA((10,)), writes=DMA((5,)), local=DMA((4,)), send=DMA((60 * Z + 32,)), gather_recv=DMA((2, 3, 4 * Z)), own_recv=DMA((2,)),
        sum_recv=DMA((D // LANES // 2 + 1, slots + 2)), pack_recv=DMA((slots + 1,)),
    )


def whole_kernel(E, total_tokens, G, names, *refs):
    r = Named(names, refs)
    rows, D = r.proj_shard.shape
    T = r.tokens.shape[0]
    cap = r.out_h.shape[1]
    pairs = [
        (r.x_qkv, r.qkv_shard), (r.x_proj, r.proj_shard), (r.x_assign, r.assign), (r.x_router, r.router),
        (r.x_pre_gain, r.pre_gain), (r.x_pre_shift, r.pre_shift), (r.x_mid_gain, r.mid_gain),
        (r.x_mid_shift, r.mid_shift), (r.x_tokens, r.tokens), (r.x_cotangent, r.cotangent),
    ]
    reads = [pltpu.make_async_copy(src, there, r.reads.at[i]) for i, (src, there) in enumerate(pairs)]
    at = Place(E)
    experts = Experts(E, 2, G, r, True)
    experts.greet()
    for read in reads:
        read.start()
    sends = Sends(r.send)
    width = D // 2
    pairs_here = width // LANES
    first_cols, last_cols = columns_of(D)
    through = r.acc.at[:, 0:D], r.acc.at[:, D : 2 * D]
    loads = [
        pltpu.make_async_copy(w.at[0], there, r.local.at[i])
        for i, (w, there) in enumerate(zip((r.w_in, r.w_dn), through))
    ]
    for load in loads:
        load.start()
    r.square[...] = jnp.zeros_like(r.square)
    for read in reads[:2]:
        read.wait()
    for part in range(2):
        for p in range(pairs_here):
            for m in range(3):
                first, to = m * D + part * width + p * LANES, (3 * p + m) * LANES
                r.shard[part, :, to : to + LANES] = r.qkv_shard[:, first : first + LANES]
        r.shard[part, :, 3 * width :] = r.proj_shard[:, part * width : (part + 1) * width]
    for read in reads[2:8]:
        read.wait()
    assign = r.assign[...].astype(single)
    r.square[0:E, 0:rows] = r.router[...]
    for i, gain in enumerate((r.pre_gain, r.pre_shift, r.mid_gain, r.mid_shift)):
        r.square[E + i : E + i + 1, 0:rows] = gain[...]
    numbers = iota((rows, T), 0).astype(single)
    count = jnp.sum(jnp.where(assign == numbers, 1.0, 0.0), axis=1, keepdims=True)
    lane = iota((rows, LANES), 1)
    r.small_shard[...] = jnp.where(lane == E + 4, count, r.square[...].T[0:rows, :])

    experts.meet()
    core = at.core_peer()
    sends.start(r.shard.at[1 - at.c], r.other, r.own_recv.at[0], core)
    sends.start(r.small_shard, r.other_small, r.own_recv.at[1], core)
    gather = Gather(at, sends, r.wts, r.small, (first_cols, last_cols), r.gather_recv, rows)
    own_rows = gather.rows_of(chip_index(at.z, at.y, at.x))

    def both(here, there):
        low, high = jnp.where(at.c == 0, here, there), jnp.where(at.c == 0, there, here)
        return jnp.concatenate([low, high], axis=0).astype(half)

    arrive(r.other, r.send.at[0], r.own_recv.at[0], core)
    r.wts[at.c, own_rows, :] = both(r.shard[at.c], r.other[...])
    gather.along_x(0)
    gather.own(0)
    arrive(r.other_small, r.send.at[0], r.own_recv.at[1], core)
    r.small[own_rows, :] = both(r.small_shard[...], r.other_small[...])
    gather.along_x(2)
    gather.along_x(1)
    gather.own(2)
    for load in loads:
        load.wait()
    experts.share_weights(*through)
    gather.second(0)
    gather.second(2)
    gather.third(0)
    gather.third(2)
    for read in reads[8:]:
        read.wait()
    set_places(E, cap, r)
    to_slots(r, r.cotangent[...], r.out_g)
    gather.own(1)
    gather.fourth(0)
    gather.fourth(2)
    gather.second(1)
    experts.send_out(1)
    gather.finish(0)
    place = lax.rem(iota((D, LANES), 0), rows)
    column = r.small[:, E + 4 : E + 5].astype(single)
    total = jnp.sum(jnp.where(place == iota((D, LANES), 1), column, 0.0), axis=0, keepdims=True)
    r.counts[...] = jnp.broadcast_to(total, r.counts.shape)

    def between():
        gather.third(1)

    def then():
        gather.fourth(1)
        gather.finish(1)

    gate = attend(E, r, r.wts, r.small, between, then)
    to_slots(r, r.hid_b[...], r.out_h)
    gates = jnp.sum(r.place[...].astype(single) * gate, axis=0, keepdims=True)
    r.gates[...] = jnp.broadcast_to(gates, r.gates.shape)
    experts.send_out(2, 0)
    experts.run()
    experts.end_weights()
    experts.turn_rows()
    experts.start_grads(1)
    experts.own_grads(1, None)
    transposes(r)
    experts.wait_returns(1, 2)
    experts.send_outputs()

    grad_gate = sum(r.ret_gg[i, 0:1, :] for i in range(E))
    grad_gate = jnp.sum(r.place[...].astype(single) * grad_gate, axis=1, keepdims=True)
    mid_gain, mid_shift = backward_body(E, total_tokens, r, r.wts, r.small, r.counts[0:1], grad_gate)
    last = SumScatter(at, sends, last_cols, r, r.sum_recv.at[pairs_here])
    firsts = [
        SumScatter(at, sends, pl.ds(3 * LANES * p, 3 * LANES), r, r.sum_recv.at[p]) for p in range(pairs_here)
    ]
    smalls = SmallSum(at, sends, r, rows)

    def give_last(here, value):
        r.give[here, last_cols] = value.astype(half)

    def keep_last(here, value):
        r.acc[here, last_cols] = value

    def give_first(here, cols, value):
        r.give[here, cols] = value.astype(half)

    def keep_first(here, cols, value):
        r.acc[here, cols] = value

    proj_weight_grad(r, 1 - at.c, give_last)
    last.swap()
    proj_weight_grad(r, at.c, keep_last)
    for p, first in enumerate(firsts):
        attend_back(r, 1 - at.c, p)
        qkv_weight_grad(r, 1 - at.c, p, give_first)
        first.swap()
        if p == 0:
            last.wait_swap()
            last.one()
        attend_back(r, at.c, p)
        qkv_weight_grad(r, at.c, p, keep_first)
        first.wait_swap()
        first.one()
    steps_z = at.z_steps() + [0]
    for dz in steps_z:
        last.two(dz)
    pre_gain, pre_shift = input_body(E, r, r.wts, r.small)
    chance_sum = jnp.sum(r.probs[...], axis=0, keepdims=True)
    r.pack[...] = small_grads(
        E, r.router_sum[...], (pre_gain, pre_shift, mid_gain, mid_shift), chance_sum, rows, D
    )
    smalls.zero()
    for dz in steps_z:
        firsts[0].two(dz)
    experts.wait_returns(0)
    set_output(r)
    smalls.one()
    writes = [
        pltpu.make_async_copy(there, dst, r.writes.at[i])
        for i, (there, dst) in enumerate((
            (r.input_grad, r.y_input_grad), (r.layer_out, r.y_layer_out), (r.small_out, r.y_small_out),
            (r.qkv_grad, r.y_qkv_grad), (r.proj_grad, r.y_proj_grad),
        ))
    ]
    for write in writes[:2]:
        write.start()
    for first in firsts[1:-1]:
        for dz in steps_z:
            first.two(dz)
    pieces = r.resid, r.grad_res
    leaving = []

    def store(i, rows_at, value):
        n = len(leaving) % 2
        if len(leaving) > 1:
            leaving[-2].wait()
        pieces[n][0 : rows_at.size, :] = value
        copy = pltpu.make_async_copy(
            pieces[n].at[0 : rows_at.size], (r.in_own, r.dn_own)[i].at[0, rows_at, :], r.local.at[2 + n]
        )
        copy.start()
        leaving.append(copy)

    experts.start_grads(0)
    for dz in steps_z if len(firsts) > 1 else ():
        firsts[-1].two(dz)
    smalls.two()
    experts.own_grads(0, store)
    last.three()
    for first in firsts:
        first.three()
    last.four()
    total = smalls.three()
    for first in firsts:
        first.four()
    total = smalls.four(total)
    scale = r.counts[0:1] * (balance_weight * E / total_tokens)
    chance = jnp.sum(jnp.where(lane == E + 4, total, 0.0), axis=1, keepdims=True)
    chosen = jnp.where((lane == iota((rows, LANES), 0)) & (lane < E), chance * scale, 0.0)
    loss = jnp.sum(jnp.sum(chosen, axis=1, keepdims=True), axis=0, keepdims=True) / total_tokens
    r.square[0:rows, :] = jnp.where(lane == E + 5, loss, total)
    r.small_out[...] = r.square[...].T[0 : r.small_out.shape[0], :]
    writes[2].start()
    last.end()
    for first in firsts:
        first.end()
    half_rows = pl.ds(pl.multiple_of(at.c * rows, rows), rows)
    mine, theirs = r.final[half_rows, :], r.final_other[...]
    for part, value in enumerate((jnp.where(at.c == 0, mine, theirs), jnp.where(at.c == 0, theirs, mine))):
        for p in range(pairs_here):
            for m in range(3):
                begin, come = m * D + part * width + p * LANES, (3 * p + m) * LANES
                r.qkv_grad[:, begin : begin + LANES] = value[:, come : come + LANES]
        r.proj_grad[:, part * width : (part + 1) * width] = value[:, 3 * width :]
    for write in writes[3:]:
        write.start()
    experts.end()
    sends.finish()
    for write in writes + leaving[-2:]:
        write.wait()


def out_kernel(E, names, *refs):
    r = Named(names, refs)
    pairs = [
        (r.in_own, r.h0), (r.in_came, r.h1), (r.dn_own, r.h2), (r.dn_came, r.h3),
        (r.layer_in, r.h4), (r.input_in, r.h5), (r.qkv_in, r.h6), (r.proj_in, r.h7),
    ]
    loads = [pltpu.make_async_copy(src, there, r.sems.at[0, i]) for i, (src, there) in enumerate(pairs)]
    outs = [
        (r.h4, r.layer_out), (r.h5, r.input_grad), (r.h6, r.qkv_grad), (r.h7, r.proj_grad),
    ]
    stores = [pltpu.make_async_copy(there, dst, r.sems.at[1, i]) for i, (there, dst) in enumerate(outs)]
    for load in loads[4:] + loads[:4]:
        load.start()
    rows = r.proj_in.shape[0]
    small_load = pltpu.make_async_copy(r.small_in, r.h8, r.sems.at[0, 8])
    small_load.start()
    small_load.wait()
    r.s_router[...] = r.h8[0:E, 0:rows]
    for i, gain in enumerate((r.s_pre_gain, r.s_pre_shift, r.s_mid_gain, r.s_mid_shift)):
        gain[...] = r.h8[E + i : E + i + 1, 0:rows]
    r.s_loss[...] = r.h8[E + 5 : E + 6, 0:1]
    small_outs = [
        (r.s_router, r.router), (r.s_pre_gain, r.pre_gain), (r.s_pre_shift, r.pre_shift),
        (r.s_mid_gain, r.mid_gain), (r.s_mid_shift, r.mid_shift), (r.s_loss, r.loss),
    ]
    small_stores = [
        pltpu.make_async_copy(there, dst, r.sems.at[2, i]) for i, (there, dst) in enumerate(small_outs)
    ]
    for store in small_stores:
        store.start()
    for load, store in zip(loads[4:], stores):
        load.wait()
        store.start()
    for i, (own, came, dst) in enumerate(((r.h0, r.h1, r.in_grad), (r.h2, r.h3, r.dn_grad))):
        loads[2 * i].wait()
        loads[2 * i + 1].wait()
        size = own.shape[1] // 4
        for piece in range(4):
            at = pl.ds(piece * size, size)
            own[0, at, :] += sum(came[j, at, :].astype(single) for j in range(came.shape[0]))
            store = pltpu.make_async_copy(own.at[0, at, :], dst.at[0, at, :], r.sems.at[1, 4 + 4 * i + piece])
            store.start()
            stores.append(store)
    for store in stores + small_stores:
        store.wait()


def on_device(
    tokens_in, out_cotangent, qkv_weight, proj_weight, router_weight, pre_gain, pre_shift, mid_gain, mid_shift,
    expert_in, expert_down, assignment,
):
    T, D = tokens_in.shape
    E, H = lax.axis_size("expert"), lax.axis_size("hid")
    X = H // 2
    Z = E // 2
    cap = 2 * T // E
    G = group_size(E, cap)
    Fq = expert_in.shape[2]
    total_tokens = T * E * H
    rows = proj_weight.shape[0]
    both = ("expert", "hid")
    assign = assignment.reshape(1, T)
    token = ((T, D), half)
    slot = ((E, cap, D), half)
    vectors = dict(pre_gain=pre_gain, pre_shift=pre_shift, mid_gain=mid_gain, mid_shift=mid_shift)
    if X == 2 and E % 2 == 0 and rows % 8 == 0 and E <= rows <= LANES and Fq == D and D % 256 == 0 and T >= 256:
        small_rows = E + 8
        found = call(
            functools.partial(whole_kernel, E, total_tokens, G),
            dict(
                x_tokens=(tokens_in, ANY_SPEC), x_cotangent=(out_cotangent, ANY_SPEC), x_assign=(assign, ANY_SPEC),
                x_qkv=(qkv_weight, ANY_SPEC), x_proj=(proj_weight, ANY_SPEC), x_router=(router_weight.T, ANY_SPEC),
                x_pre_gain=(pre_gain.reshape(1, rows), ANY_SPEC), x_pre_shift=(pre_shift.reshape(1, rows), ANY_SPEC),
                x_mid_gain=(mid_gain.reshape(1, rows), ANY_SPEC), x_mid_shift=(mid_shift.reshape(1, rows), ANY_SPEC),
                w_in=(expert_in, ANY_SPEC), w_dn=(expert_down, ANY_SPEC),
            ),
            dict(
                y_layer_out=token + (ANY_SPEC,), y_input_grad=token + (ANY_SPEC,),
                y_qkv_grad=((rows, 3 * D), single, ANY_SPEC), y_proj_grad=((rows, D), single, ANY_SPEC),
                y_small_out=((small_rows, LANES), single, ANY_SPEC),
                in_own=((1, D, Fq), single, ANY_SPEC), dn_own=((1, Fq, D), single, ANY_SPEC),
                in_came=((X - 1, D, Fq), half, ANY_SPEC), dn_came=((X - 1, Fq, D), half, ANY_SPEC),
            ),
            dict(
                tokens=pltpu.VMEM(*token), cotangent=pltpu.VMEM(*token), assign=pltpu.VMEM((1, T), jnp.int32),
                qkv_shard=pltpu.VMEM((rows, 3 * D), single), proj_shard=pltpu.VMEM((rows, D), single),
                router=pltpu.VMEM((E, rows), single), pre_gain=pltpu.VMEM((1, rows), single),
                pre_shift=pltpu.VMEM((1, rows), single), mid_gain=pltpu.VMEM((1, rows), single),
                mid_shift=pltpu.VMEM((1, rows), single), layer_out=pltpu.VMEM(*token), input_grad=pltpu.VMEM(*token),
                qkv_grad=pltpu.VMEM((rows, 3 * D), single), proj_grad=pltpu.VMEM((rows, D), single),
                small_out=pltpu.VMEM((small_rows, LANES), single),
                **whole_scratch(E, T, D, cap, rows), **model_scratch(E, T, D, cap), **end_scratch(T, D),
                **expert_scratch(E, X, cap, D, Fq),
            ),
            1, "layer",
        )
        layer_out, input_grad, qkv_grad, proj_grad, small_out, in_own, dn_own, in_came, dn_came = found
        vector = ((1, rows), single, ANY_SPEC)
        found = call(
            functools.partial(out_kernel, E),
            dict(
                layer_in=(layer_out, ANY_SPEC), input_in=(input_grad, ANY_SPEC),
                qkv_in=(qkv_grad, ANY_SPEC), proj_in=(proj_grad, ANY_SPEC),
                in_own=(in_own, ANY_SPEC), dn_own=(dn_own, ANY_SPEC),
                in_came=(in_came, ANY_SPEC), dn_came=(dn_came, ANY_SPEC), small_in=(small_out, ANY_SPEC),
            ),
            dict(
                layer_out=token + (ANY_SPEC,), input_grad=token + (ANY_SPEC,),
                qkv_grad=((rows, 3 * D), single, ANY_SPEC), proj_grad=((rows, D), single, ANY_SPEC),
                in_grad=((1, D, Fq), single, ANY_SPEC), dn_grad=((1, Fq, D), single, ANY_SPEC),
                router=((E, rows), single, ANY_SPEC), pre_gain=vector, pre_shift=vector, mid_gain=vector,
                mid_shift=vector, loss=((1, 1), single, ANY_SPEC),
            ),
            dict(
                h0=pltpu.VMEM((1, D, Fq), single), h1=pltpu.VMEM((X - 1, D, Fq), half),
                h2=pltpu.VMEM((1, Fq, D), single), h3=pltpu.VMEM((X - 1, Fq, D), half),
                h4=pltpu.VMEM(*token), h5=pltpu.VMEM(*token), h6=pltpu.VMEM((rows, 3 * D), single),
                h7=pltpu.VMEM((rows, D), single), h8=pltpu.VMEM((small_rows, LANES), single),
                s_router=pltpu.VMEM((E, rows), single), s_pre_gain=pltpu.VMEM((1, rows), single),
                s_pre_shift=pltpu.VMEM((1, rows), single), s_mid_gain=pltpu.VMEM((1, rows), single),
                s_mid_shift=pltpu.VMEM((1, rows), single), s_loss=pltpu.VMEM((1, 1), single), sems=DMA((3, 12)),
            ),
            None, "results",
        )
        layer_out, input_grad, qkv_grad, proj_grad, in_grad, dn_grad, router, *grads, loss = found
        return (
            layer_out, loss.reshape(()), input_grad, qkv_grad, proj_grad, router.T,
            *[value.reshape(rows) for value in grads], in_grad, dn_grad,
        )

    small_in = jnp.concatenate([router_weight] + [value[:, None] for value in vectors.values()], axis=1)
    small_in = jnp.pad(small_in, ((0, 0), (0, LANES - small_in.shape[1])))
    shard = jnp.concatenate([qkv_weight, proj_weight], axis=1).astype(half)
    wts = lax.all_gather(shard, both, axis=0, tiled=True)
    wts = jnp.concatenate(
        [
            wts[:, : 3 * D].reshape(D, 3, 2, D // 2 // LANES, LANES).transpose(2, 0, 3, 1, 4).reshape(2, D, 3 * D // 2),
            wts[:, 3 * D :].reshape(D, 2, D // 2).transpose(1, 0, 2),
        ],
        axis=2,
    )
    small = lax.all_gather(small_in.astype(half), both, axis=0, tiled=True)
    onehot = assignment[:, None] == jnp.arange(LANES, dtype=jnp.int32)[None, :]
    counts = lax.psum(jnp.sum(onehot.astype(single), axis=0), both)
    saved = dict(
        hid_a=token, qkv=((2, T, 3 * D // 2), half), att=token, resid=((T, D), single), hid_b=token,
        probs=((T, LANES), single),
    )
    given = dict(tokens=tokens_in, cotangent=out_cotangent, assign=assign, wts=wts, small=small)
    out_h, out_g, *rest = call(
        functools.partial(start_kernel, E), given, dict(out_h=slot, out_g=slot, **saved),
        model_scratch(E, T, D, cap), None, "start",
    )
    ret_o, ret_g, in_own, dn_own, in_came, dn_came = call(
        functools.partial(expert_kernel, E, X, G),
        dict(out_h=out_h, out_g=out_g, w_in=expert_in[0], w_dn=expert_down[0]),
        dict(
            ret_o=slot, ret_g=slot, in_grad=((D, Fq), single), dn_grad=((Fq, D), single),
            in_came=((X - 1, D, Fq), half), dn_came=((X - 1, Fq, D), half),
        ),
        expert_scratch(E, X, cap, D, Fq), 1, "experts",
    )
    in_grad = in_own + jnp.sum(in_came.astype(single), axis=0)
    dn_grad = dn_own + jnp.sum(dn_came.astype(single), axis=0)
    layer_out, input_grad, weight_grads, packed = call(
        functools.partial(end_kernel, E, total_tokens),
        dict(
            **given, counts=jnp.broadcast_to(counts[None, :], (8, LANES)), **dict(zip(saved, rest)),
            ret_o=ret_o, ret_g=ret_g,
        ),
        dict(
            layer_out=token, input_grad=token, weight_grads=((2, D, 2 * D), single),
            small_out=((D, LANES), single),
        ),
        dict(**model_scratch(E, T, D, cap), **end_scratch(T, D)), None, "end",
    )
    pairs = weight_grads[:, :, : 3 * D // 2].reshape(2, D, D // 2 // LANES, 3, LANES)
    gathered = jnp.concatenate(
        [
            pairs.transpose(1, 3, 0, 2, 4).reshape(D, 3 * D),
            weight_grads[:, :, 3 * D // 2 :].transpose(1, 0, 2).reshape(D, D),
        ],
        axis=1,
    )
    gathered = lax.psum_scatter(gathered, both, scatter_dimension=0, tiled=True)
    small_out = lax.psum_scatter(packed, both, scatter_dimension=0, tiled=True)
    chance = lax.psum(jnp.sum(rest[-1], axis=0), both)
    balance_loss = jnp.sum(chance * counts) * (balance_weight * E / total_tokens) / total_tokens
    return (
        layer_out, balance_loss, input_grad, gathered[:, : 3 * D], gathered[:, 3 * D :], small_out[:, :E],
        *[small_out[:, E + i] for i in range(4)], in_grad[None], dn_grad[None],
    )


def solution(mesh):
    in_specs = (
        P(("expert", "hid"), None),
        P(("expert", "hid"), None),
        P(("expert", "hid"), None),
        P(("expert", "hid"), None),
        P(("expert", "hid"), None),
        P(("expert", "hid")),
        P(("expert", "hid")),
        P(("expert", "hid")),
        P(("expert", "hid")),
        P("expert", None, "hid"),
        P("expert", "hid", None),
        P(("expert", "hid")),
    )
    out_specs = (
        P(("expert", "hid"), None),
        P(),
        P(("expert", "hid"), None),
        P(("expert", "hid"), None),
        P(("expert", "hid"), None),
        P(("expert", "hid"), None),
        P(("expert", "hid")),
        P(("expert", "hid")),
        P(("expert", "hid")),
        P(("expert", "hid")),
        P("expert", None, "hid"),
        P("expert", "hid", None),
    )
    return jax.shard_map(
        on_device, mesh=mesh, in_specs=in_specs, out_specs=out_specs, check_vma=False
    )
```

```python
import functools

import jax
import jax.numpy as jnp
from jax import lax
from jax.experimental import pallas as pl
from jax.experimental.pallas import tpu as pltpu
from jax.sharding import PartitionSpec as P

epsilon = 1e-05
balance_weight = 3.0
masked_score = -1000000000.0


MESH = pl.DeviceIdType.MESH
DMA = pltpu.SemaphoreType.DMA
VMEM_SPEC = pl.BlockSpec(memory_space=pltpu.VMEM)
ANY_SPEC = pl.BlockSpec(memory_space=pl.ANY)
half = jnp.bfloat16
single = jnp.float32
STEP = 32


def remote(src, dst, send_sem, recv_sem, device):
    return pltpu.make_async_remote_copy(
        src_ref=src, dst_ref=dst, send_sem=send_sem, recv_sem=recv_sem,
        device_id=device, device_id_type=MESH,
    )


def dot(a, b):
    return jnp.dot(a, b, preferred_element_type=single)


def dot_cols(a, b):
    return lax.dot_general(a, b, (((1,), (1,)), ((), ())), preferred_element_type=single)


def dot_rows(a, b):
    return lax.dot_general(a, b, (((0,), (0,)), ((), ())), preferred_element_type=single)


def grad_rows(size):
    return 256 if size % 256 == 0 else 128


def steps(count, step):
    def run(body):
        @pl.loop(0, count // step)
        def _(i):
            body(pl.ds(pl.multiple_of(i * step, step), step))
    return run


class Named:
    def __init__(self, names, refs):
        self.__dict__.update(zip(names, refs, strict=True))


def expert_scratch(E, X, cap, D, Fq):
    P, token = 2 * X, (E, cap, D)
    return dict(
        xh=pltpu.VMEM(token, half), xg=pltpu.VMEM(token, half),
        win=pltpu.VMEM((P, D, Fq), half), wdn=pltpu.VMEM((P, Fq, D), half),
        act=pltpu.VMEM((P, E * cap, Fq), half), gbef=pltpu.VMEM((P, E * cap, Fq), half),
        to=pltpu.VMEM(token, half), tg=pltpu.VMEM(token, half), xh_t=pltpu.VMEM((D, E * cap), half),
        core_in=pltpu.VMEM((X, D, Fq), half), core_dn=pltpu.VMEM((X, Fq, D), half),
        xgate=pltpu.VMEM((E, 8, E * cap), single), raw=pltpu.VMEM(token, half),
        tgg=pltpu.VMEM((E, 8, E * cap), single), ret_gg=pltpu.VMEM((E, 8, E * cap), single),
        send_a=DMA((3, E)), recv_a=DMA((3, E)), send_r=DMA((3, E)), recv_r=DMA((3, E)),
        send_w=DMA((2, X)), recv_w=DMA((2, X)), send_f=DMA((2, X)), recv_f=DMA((2, X)),
        send_d=DMA((2, X)), recv_d=DMA((2, X)), send_s=DMA((2, X)), recv_s=DMA((2, X)),
    )


class Experts:
    def __init__(self, E, X, G, r, gated):
        self.E, self.X, self.G, self.r, self.gated = E, X, G, r, gated
        self.e, self.h = lax.axis_index("expert"), lax.axis_index("hid")
        self.x, self.c = lax.div(self.h, 2), lax.rem(self.h, 2)
        self.cap, self.D = r.out_h.shape[1], r.out_h.shape[2]
        self.Fq = r.win.shape[2]
        self.NG, self.rows = E // G, G * self.cap
        self.core_peer = (self.e, self.x * 2 + 1 - self.c)
        self.landing = r.raw if gated else r.xg

    def expert_at(self, k):
        found, bit = 0, 1
        while bit < self.E:
            a, b = lax.rem(lax.div(self.e, bit), 2), lax.rem(lax.div(k, bit), 2)
            found = found + bit * (a + b - 2 * a * b)
            bit *= 2
        return found

    def x_peer(self, d):
        return (self.e, lax.rem(self.x + d, self.X) * 2 + self.c)

    def part(self, j, core):
        return lax.rem(self.x + j, self.X) * 2 + core

    def greet(self):
        barrier = pltpu.get_barrier_semaphore()

        @pl.loop(1, self.E)
        def _(k):
            pl.semaphore_signal(
                barrier, inc=1, device_id=(self.expert_at(k), self.h), device_id_type=MESH
            )

        for d in range(1, self.X):
            pl.semaphore_signal(barrier, inc=1, device_id=self.x_peer(d), device_id_type=MESH)
        pl.semaphore_signal(barrier, inc=1, device_id=self.core_peer, device_id_type=MESH)

    def meet(self):
        pl.semaphore_wait(pltpu.get_barrier_semaphore(), self.E - 1 + self.X - 1 + 1)

    def weight_to_x(self, i, d):
        r, w, q = self.r, (self.r.win, self.r.wdn)[i], self.part(0, self.c)
        return remote(
            w.at[q], w.at[q], r.send_w.at[i, d], r.recv_w.at[i, self.X - d], self.x_peer(d)
        )

    def weight_to_core(self, i, j, core):
        r, w, q = self.r, (self.r.win, self.r.wdn)[i], self.part(j, core)
        return remote(w.at[q], w.at[q], r.send_f.at[i, j], r.recv_f.at[i, j], self.core_peer)

    def share_weights(self, w_in, w_dn):
        r, q = self.r, self.part(0, self.c)

        @steps(self.D, STEP)
        def _(at):
            r.win[q, at, :] = w_in[at, :].astype(half)

        for d in range(1, self.X):
            self.weight_to_x(0, d).start()

        @steps(self.Fq, STEP)
        def _(at):
            r.wdn[q, at, :] = w_dn[at, :].astype(half)

        for d in range(1, self.X):
            self.weight_to_x(1, d).start()
        for i in range(2):
            self.weight_to_core(i, 0, self.c).start()

    def wait_weights(self, j, core):
        for i in range(2):
            if core == 0:
                if j:
                    self.weight_to_x(i, self.X - j).wait_recv()
                    self.weight_to_core(i, j, self.c).start()
            else:
                self.weight_to_core(i, j, 1 - self.c).wait_recv()

    def end_weights(self):
        for i in range(2):
            for j in range(self.X):
                self.weight_to_core(i, j, self.c).wait_send()
                if j:
                    self.weight_to_x(i, j).wait_send()

    def dispatch(self, k, part):
        r = self.r
        peer = self.expert_at(k)
        if part == 2:
            src, dst = r.gates, r.xgate
        else:
            src, dst = ((r.out_h.at[peer], r.xh), (r.out_g.at[peer], self.landing))[part]
        return remote(src, dst.at[k], r.send_a.at[part, k], r.recv_a.at[part, k], (peer, self.h))

    def send_out(self, *parts):
        r = self.r

        @pl.loop(1, self.E)
        def _(k):
            for part in parts:
                self.dispatch(k, part).start()

        for part in parts:
            if part == 2:
                r.xgate[0] = r.gates[...]
            else:
                src, dst = ((r.out_h, r.xh), (r.out_g, self.landing))[part]
                dst[0] = src[self.e]

    def own_lanes(self):
        shape = (self.cap, self.E * self.cap)
        return iota(shape, 1) == iota(shape, 0) + self.e * self.cap

    def take(self, g):
        r, cap = self.r, self.cap

        @pl.loop(0, self.G)
        def _(i):
            k = g * self.G + i

            @pl.when(k > 0)
            def _():
                for part in (1, 2, 0) if self.gated else (1, 0):
                    self.dispatch(k, part).wait_recv()

            if self.gated:
                gate = jnp.where(self.own_lanes(), r.xgate[k, 0:1, :], 0.0)
                gate = jnp.sum(gate, axis=1, keepdims=True)
                r.xg[k] = (gate * r.raw[k].astype(single)).astype(half)

    def compute(self, g):
        r = self.r
        slots = pl.ds(g * self.G, self.G)
        at = pl.ds(pl.multiple_of(g * self.rows, self.rows), self.rows)
        xh_g = r.xh[slots].reshape(self.rows, self.D)
        xg_g = r.xg[slots].reshape(self.rows, self.D)
        parts = []
        for n in range(2 * self.X):
            j, core = n // 2, n % 2
            q = self.part(j, self.c if core == 0 else 1 - self.c)
            parts.append(q)

            @pl.when(g == 0)
            def _():
                self.wait_weights(j, core)

            v = dot(xh_g, r.win[q])
            ga = dot_cols(xg_g, r.wdn[q])
            cdf = 0.5 * (1.0 + lax.erf(v * (0.5 ** 0.5)))
            slope = cdf + v * (jnp.exp(-0.5 * v * v) * 0.3989422804014327)
            r.act[q, at, :] = (v * cdf).astype(half)
            r.gbef[q, at, :] = (slope * ga).astype(half)
        out = sum(dot(r.act[q, at, :], r.wdn[q]) for q in parts)
        gin = sum(dot_cols(r.gbef[q, at, :], r.win[q]) for q in parts)
        shape = (self.G, self.cap, self.D)
        r.to[slots] = out.astype(half).reshape(shape)
        r.tg[slots] = gin.astype(half).reshape(shape)
        if self.gated:
            @pl.loop(0, self.G)
            def _(i):
                k = g * self.G + i
                toward = jnp.sum(r.raw[k].astype(single) * r.to[k].astype(single), axis=1, keepdims=True)
                row = jnp.sum(jnp.where(self.own_lanes(), toward, 0.0), axis=0, keepdims=True)
                r.tgg[k] = jnp.broadcast_to(row, r.tgg.shape[1:])

    def give_back(self, k, part):
        r = self.r
        src, dst = ((r.to, r.ret_o), (r.tg, r.ret_g), (r.tgg, r.ret_gg))[part]
        return remote(
            src.at[k], dst.at[self.e], r.send_r.at[part, k], r.recv_r.at[part, k],
            (self.expert_at(k), self.h),
        )

    def run(self):
        r = self.r
        parts = (1, 2) if self.gated else (1,)

        @pl.loop(0, self.NG)
        def _(g):
            self.take(g)
            self.compute(g)

            @pl.loop(0, self.G)
            def _(i):
                k = g * self.G + i

                @pl.when(k > 0)
                def _():
                    for part in parts:
                        self.give_back(k, part).start()

        r.ret_o[self.e] = r.to[0]
        r.ret_g[self.e] = r.tg[0]
        if self.gated:
            r.ret_gg[self.e] = r.tgg[0]

    def send_outputs(self):
        @pl.loop(1, self.E)
        def _(k):
            self.give_back(k, 0).start()

    def grad_to_core(self, i, j):
        r, w, came = self.r, (self.r.win, self.r.wdn)[i], (self.r.core_in, self.r.core_dn)[i]
        return remote(w.at[j], came.at[j], r.send_d.at[i, j], r.recv_d.at[i, j], self.core_peer)

    def grad_to_x(self, i, j):
        r, w, came = self.r, (self.r.win, self.r.wdn)[i], (self.r.in_came, self.r.dn_came)[i]
        return remote(
            w.at[self.X + j], came.at[self.X - j - 1], r.send_s.at[i, j], r.recv_s.at[i, self.X - j],
            self.x_peer(j),
        )

    def grad(self, i, q, at):
        r, T = self.r, self.E * self.cap
        if i == 0:
            return dot(r.xh_t[at, :], r.gbef[q])
        return dot_rows(r.act[q, :, at], r.xg[...].reshape(T, self.D))

    def start_grads(self, j):
        r = self.r
        for i, (w, size) in enumerate(((r.win, self.D), (r.wdn, self.Fq))):
            @steps(size, grad_rows(size))
            def _(at):
                w[j, at, :] = self.grad(i, self.part(j, 1 - self.c), at).astype(half)

            self.grad_to_core(i, j).start()

    def own_grads(self, j, store):
        r = self.r
        for i, (w, came, size) in enumerate(((r.win, r.core_in, self.D), (r.wdn, r.core_dn, self.Fq))):
            self.grad_to_core(i, j).wait_recv()
            if j:
                @steps(size, grad_rows(size))
                def _(at):
                    total = self.grad(i, self.part(j, self.c), at) + came[j, at, :].astype(single)
                    w[self.X + j, at, :] = total.astype(half)

                self.grad_to_x(i, j).start()
            else:
                for first in range(0, size, grad_rows(size)):
                    at = pl.ds(first, grad_rows(size))
                    store(i, at, self.grad(i, self.part(j, self.c), at) + came[j, at, :].astype(single))

    def turn_rows(self):
        self.r.xh_t[...] = self.r.xh[...].reshape(self.E * self.cap, self.D).T

    def wait_returns(self, *parts):
        @pl.loop(1, self.E)
        def _(k):
            for part in parts:
                self.give_back(k, part).wait_recv()

    def end(self):
        for i in range(2):
            for j in range(self.X):
                self.grad_to_core(i, j).wait_send()
                if j:
                    self.grad_to_x(i, j).wait()

        @pl.loop(1, self.E)
        def _(k):
            for part in range(3 if self.gated else 2):
                self.dispatch(k, part).wait_send()
                self.give_back(k, part).wait_send()


def expert_kernel(E, X, G, names, *refs):
    r = Named(names, refs)
    experts = Experts(E, X, G, r, False)
    experts.greet()
    experts.meet()
    experts.send_out(0, 1)
    experts.share_weights(r.w_in, r.w_dn)
    experts.run()
    experts.send_outputs()
    experts.end_weights()
    experts.turn_rows()

    def store(i, at, value):
        (r.in_grad, r.dn_grad)[i][at, :] = value

    for j in list(range(1, X)) + [0]:
        experts.start_grads(j)
        experts.own_grads(j, store)
    experts.wait_returns(0, 1)
    experts.end()


def group_size(E, cap):
    return max(1, min(E, GROUP_ROWS // cap))


def call(kernel, ins, outs, scratch, collective, name):
    names = list(ins) + list(outs) + list(scratch)
    extra = dict() if collective is None else dict(collective_id=collective, has_side_effects=True)
    pairs = [value if isinstance(value, tuple) else (value, VMEM_SPEC) for value in ins.values()]
    return pl.pallas_call(
        functools.partial(kernel, names),
        out_shape=tuple(jax.ShapeDtypeStruct(value[0], value[1]) for value in outs.values()),
        in_specs=[spec for _, spec in pairs],
        out_specs=tuple(value[2] if len(value) > 2 else VMEM_SPEC for value in outs.values()),
        scratch_shapes=list(scratch.values()),
        compiler_params=pltpu.CompilerParams(vmem_limit_bytes=VMEM_LIMIT, **extra),
        name=name,
    )(*[array for array, _ in pairs])


HEAD_DIM = 64
LANES = 128


def norm_stats(values):
    average = jnp.mean(values, axis=-1, keepdims=True)
    centred = values - average
    spread = jnp.mean(centred * centred, axis=-1, keepdims=True)
    return centred, lax.rsqrt(spread + epsilon)


def norm_back(grad, values, gain):
    centred, rate = norm_stats(values)
    unit = centred * rate
    scaled = grad * gain
    toward = rate * (
        scaled
        - jnp.mean(scaled, axis=-1, keepdims=True)
        - unit * jnp.mean(scaled * unit, axis=-1, keepdims=True)
    )
    gain_grad = jnp.sum(grad * unit, axis=0, keepdims=True)
    shift_grad = jnp.sum(grad, axis=0, keepdims=True)
    return toward, gain_grad, shift_grad


def iota(shape, axis):
    return lax.broadcasted_iota(jnp.int32, shape, axis)


def slot_places(assign, capacity):
    T = assign.shape[1]
    down, across = iota((T, T), 0), iota((T, T), 1)
    column = jnp.sum(jnp.where(down == across, assign, 0.0), axis=1, keepdims=True)
    same = column == assign
    rank_column = jnp.sum(jnp.where(same & (across < down), 1.0, 0.0), axis=1, keepdims=True)
    rank_row = jnp.sum(jnp.where(same & (down < across), 1.0, 0.0), axis=0, keepdims=True)
    place_column = (column * capacity + rank_column).astype(jnp.int32)
    place_row = (assign * capacity + rank_row).astype(jnp.int32)
    return column.astype(jnp.int32), place_column, place_row


def head_probs(q_one, k_pair, allowed):
    scores = dot_cols(q_one, k_pair) * (HEAD_DIM ** -0.5)
    scores = jnp.where(allowed, scores, masked_score)
    powers = jnp.exp(scores - jnp.max(scores, axis=-1, keepdims=True))
    return powers * (1.0 / jnp.sum(powers, axis=-1, keepdims=True))


def head_masks(T):
    first = iota((T, LANES), 1) < HEAD_DIM
    low_lanes = jnp.where(first, 1.0, 0.0).astype(half)
    high_lanes = jnp.where(first, 0.0, 1.0).astype(half)
    return first, (low_lanes, high_lanes)


def columns_of(D):
    return pl.ds(0, 3 * D // 2), pl.ds(3 * D // 2, D // 2)


def pair_columns(D, m, p):
    return pl.ds(pl.multiple_of((3 * p + m) * LANES, LANES), LANES)


def attend(E, r, wts, small, between=lambda: None, then=lambda: None):
    T, D = r.tokens.shape
    first_cols, last_cols = columns_of(D)
    small_t = small[...].astype(single).T
    inputs = r.tokens[...].astype(single)
    centred, rate = norm_stats(inputs)
    r.hid_a[...] = (centred * rate * small_t[E : E + 1] + small_t[E + 1 : E + 2]).astype(half)
    for part in range(2):
        r.qkv[part] = dot(r.hid_a[...], wts[part, :, first_cols]).astype(half)
    between()
    allowed = iota((T, T), 1) <= iota((T, T), 0)
    first, masks = head_masks(T)
    count = D // LANES // 2

    @pl.loop(0, 2 * count)
    def _(i):
        part, p = lax.div(i, count), lax.rem(i, count)
        q_pair, k_pair, v_pair = (r.qkv[part, :, pair_columns(D, m, p)] for m in range(3))
        mixed = [
            dot(head_probs(q_pair * mask, k_pair, allowed).astype(half), v_pair) for mask in masks
        ]
        at = pl.ds(pl.multiple_of(i * LANES, LANES), LANES)
        r.att[:, at] = jnp.where(first, mixed[0], mixed[1]).astype(half)

    then()
    for part in range(2):
        at = pl.ds(part * (D // 2), D // 2)
        r.resid[:, at] = r.tokens[:, at].astype(single) + dot(r.att[...], wts[part, :, last_cols])
    centred, rate = norm_stats(r.resid[...])
    r.hid_b[...] = (centred * rate * small_t[E + 2 : E + 3] + small_t[E + 3 : E + 4]).astype(half)
    lane = iota((T, LANES), 1)
    logits = jnp.where(lane < E, dot(r.hid_b[...], small[...]), -1e30)
    powers = jnp.exp(logits - jnp.max(logits, axis=-1, keepdims=True))
    chance = powers * (1.0 / jnp.sum(powers, axis=-1, keepdims=True))
    r.probs[...] = chance
    return jnp.sum(jnp.where(r.mine[...] > 0.0, chance, 0.0), axis=1, keepdims=True)


def set_places(E, cap, r):
    T = r.tokens.shape[0]
    column, place_column, place_row = slot_places(r.assign[...].astype(single), cap)
    r.pick[...] = jnp.where(iota((E * cap, T), 0) == place_row, 1.0, 0.0).astype(half)
    r.place[...] = jnp.where(iota((T, E * cap), 1) == place_column, 1.0, 0.0).astype(half)
    r.mine[...] = jnp.where(iota((T, LANES), 1) == column, 1.0, 0.0)


def to_slots(r, rows, out):
    out[...] = dot(r.pick[...], rows).astype(half).reshape(out.shape)


def set_output(r):
    slots, D = r.place.shape[1], r.tokens.shape[1]
    gate = jnp.sum(r.mine[...] * r.probs[...], axis=1, keepdims=True)
    expert_tok = dot(r.place[...], r.ret_o[...].reshape(slots, D))
    r.layer_out[...] = (r.resid[...] + gate * expert_tok).astype(half)
    return jnp.sum(r.cotangent[...].astype(single) * expert_tok, axis=1, keepdims=True)


def backward_body(E, total_tokens, r, wts, small, counts, grad_gate):
    T, D = r.tokens.shape
    slots = r.place.shape[1]
    small_t = small[...].astype(single).T
    cot = r.cotangent[...].astype(single)
    lane = iota((T, LANES), 1)
    chance = r.probs[...]
    mine = r.mine[...]
    scale = counts * (balance_weight * E / total_tokens)
    grad_probs = mine * grad_gate + scale
    grad_logits = chance * (grad_probs - jnp.sum(chance * grad_probs, axis=1, keepdims=True))
    grad_logits = jnp.where(lane < E, grad_logits, 0.0).astype(half)
    r.router_sum[...] = dot_rows(r.hid_b[...], grad_logits)
    grad_hidden_b = dot(r.place[...], r.ret_g[...].reshape(slots, D)) + dot_cols(grad_logits, small[...])
    toward, mid_gain, mid_shift = norm_back(grad_hidden_b, r.resid[...], small_t[E + 2 : E + 3])
    r.grad_res[...] = cot + toward
    r.gproj[...] = r.grad_res[...].astype(half)
    _, last_cols = columns_of(D)
    r.gatt[...] = sum(
        dot_cols(r.gproj[:, part * (D // 2) : (part + 1) * (D // 2)], wts[part, :, last_cols])
        for part in range(2)
    ).astype(half)
    return mid_gain, mid_shift


def attend_back(r, part, p):
    T, D = r.tokens.shape
    allowed = iota((T, T), 1) <= iota((T, T), 0)
    first, masks = head_masks(T)
    q_pair, k_pair, v_pair = (r.qkv[part, :, pair_columns(D, m, p)] for m in range(3))
    g_pair = r.gatt[:, pl.ds(pl.multiple_of(part * (D // 2) + p * LANES, LANES), LANES)]
    found = []
    for mask in masks:
        weights = head_probs(q_pair * mask, k_pair, allowed)
        grad_w = dot_cols(g_pair * mask, v_pair)
        grad_s = weights * (grad_w - jnp.sum(weights * grad_w, axis=-1, keepdims=True))
        grad_s = grad_s.astype(half)
        found.append(
            (
                dot(grad_s, k_pair) * (HEAD_DIM ** -0.5),
                dot_rows(grad_s, q_pair) * (HEAD_DIM ** -0.5),
                dot_rows(weights.astype(half), g_pair),
            )
        )
    for m in range(3):
        r.gqkv[part, :, pair_columns(D, m, p)] = jnp.where(first, found[0][m], found[1][m]).astype(half)


def transposes(r):
    r.hid_a_t[...] = r.hid_a[...].T
    r.att_t[...] = r.att[...].T


def qkv_weight_grad(r, part, p, write):
    D = r.hid_a_t.shape[0]
    cols = pl.ds(3 * LANES * p, 3 * LANES)

    @steps(D, 256 if D % 256 == 0 else LANES)
    def _(rows):
        write(rows, cols, dot(r.hid_a_t[rows, :], r.gqkv[part, :, cols]))


def proj_weight_grad(r, part, write):
    D = r.att_t.shape[0]
    cols = pl.ds(pl.multiple_of(part * (D // 2), D // 2), D // 2)

    @steps(D, 256 if D % 256 == 0 else LANES)
    def _(rows):
        write(rows, dot(r.att_t[rows, :], r.gproj[:, cols]))


def input_body(E, r, wts, small):
    small_t = small[...].astype(single).T
    first_cols, _ = columns_of(r.tokens.shape[1])
    grad_hidden_a = sum(dot_cols(r.gqkv[part], wts[part, :, first_cols]) for part in range(2))
    toward, pre_gain, pre_shift = norm_back(
        grad_hidden_a, r.tokens[...].astype(single), small_t[E : E + 1]
    )
    r.input_grad[...] = (r.grad_res[...] + toward).astype(half)
    return pre_gain, pre_shift


def small_grads(E, router, rows, chance_sum, block, D):
    lane = iota((D, LANES), 1)
    eight = iota((LANES, D), 0)
    stacked = jnp.zeros((LANES, D), single)
    for i, row in enumerate(rows):
        stacked = jnp.where(eight == E + i, row, stacked)
    packed = jnp.where(lane < E, router, stacked.T)
    if block:
        place = lax.rem(iota((D, LANES), 0), block)
        copy = jnp.sum(jnp.where(place == lane, chance_sum, 0.0), axis=1, keepdims=True)
        packed = jnp.where(lane == E + 4, copy, packed)
    return packed


class Place:
    def __init__(self, E):
        e, h = lax.axis_index("expert"), lax.axis_index("hid")
        self.Z = E // 2
        self.z, self.y = lax.div(e, 2), lax.rem(e, 2)
        self.x, self.c = lax.div(h, 2), lax.rem(h, 2)

    def device(self, z, y, x, c):
        return (z * 2 + y, x * 2 + c)

    def z_at(self, d):
        return lax.rem(self.z + d, self.Z)

    def z_peer(self, d):
        return self.device(self.z_at(d), self.y, self.x, self.c)

    def y_peer(self):
        return self.device(self.z, 1 - self.y, self.x, self.c)

    def x_peer(self):
        return self.device(self.z, self.y, 1 - self.x, self.c)

    def core_peer(self):
        return self.device(self.z, self.y, self.x, 1 - self.c)

    def z_steps(self):
        return sorted(range(1, self.Z), key=lambda d: min(d, self.Z - d))

    def greet(self):
        barrier = pltpu.get_barrier_semaphore()
        peers = [self.z_peer(d) for d in range(1, self.Z)]
        peers += [self.y_peer(), self.x_peer(), self.core_peer()]
        for peer in peers:
            pl.semaphore_signal(barrier, inc=1, device_id=peer, device_id_type=MESH)
        pl.semaphore_wait(barrier, len(peers))


def chip_index(z, y, x):
    return (z * 2 + y) * 2 + x


class Sends:
    def __init__(self, sems):
        self.sems, self.started = sems, []

    def start(self, src, dst, recv_sem, device):
        copy = remote(src, dst, self.sems.at[len(self.started)], recv_sem, device)
        copy.start()
        self.started.append(copy)
        return len(self.started) - 1

    def settle(self, n):
        self.started[n].wait_send()
        self.started[n] = None

    def finish(self):
        for copy in self.started:
            if copy is not None:
                copy.wait_send()


def arrive(dst, send_sem, recv_sem, device):
    remote(dst, dst, send_sem, recv_sem, device).wait_recv()


class Gather:
    def __init__(self, at, sends, wts, small, spans, recv, rows):
        self.at, self.sends, self.wts, self.small, self.spans = at, sends, wts, small, spans
        self.recv, self.span = recv, 2 * rows

    def rows_of(self, chip):
        return pl.ds(pl.multiple_of(chip * self.span, self.span), self.span)

    def block(self, o, chip, core):
        if o == len(self.spans):
            return self.small.at[self.rows_of(chip), :]
        return self.wts.at[core, self.rows_of(chip), self.spans[o]]

    def send(self, o, chip, device):
        block = self.block(o, chip, self.at.c)
        self.sends.start(block, block, self.recv.at[0, o, chip], device)

    def share(self, o, chip):
        if o < len(self.spans):
            block = self.block(o, chip, self.at.c)
            self.sends.start(block, block, self.recv.at[1, o, chip], self.at.core_peer())

    def wait(self, o, chip):
        block = self.block(o, chip, self.at.c)
        arrive(block, self.sends.sems.at[0], self.recv.at[0, o, chip], self.at.core_peer())

    def spread(self, o, chip):
        for d in self.at.z_steps():
            self.send(o, chip, self.at.z_peer(d))
        self.send(o, chip, self.at.y_peer())
        self.share(o, chip)

    def along_x(self, o):
        at = self.at
        self.send(o, chip_index(at.z, at.y, at.x), at.x_peer())

    def own(self, o):
        at = self.at
        self.spread(o, chip_index(at.z, at.y, at.x))

    def second(self, o):
        at = self.at
        chip = chip_index(at.z, at.y, 1 - at.x)
        self.wait(o, chip)
        self.spread(o, chip)

    def third(self, o):
        at = self.at
        for x in (at.x, 1 - at.x):
            for d in at.z_steps():
                chip = chip_index(at.z_at(d), at.y, x)
                self.wait(o, chip)
                self.send(o, chip, at.y_peer())
                self.share(o, chip)

    def fourth(self, o):
        at = self.at
        for x in (at.x, 1 - at.x):
            for d in [0] + at.z_steps():
                chip = chip_index(at.z_at(d), 1 - at.y, x)
                self.wait(o, chip)
                self.share(o, chip)

    def finish(self, o):
        if o < len(self.spans):
            @pl.loop(0, 4 * self.at.Z)
            def _(chip):
                block = self.block(o, chip, 1 - self.at.c)
                arrive(block, self.sends.sems.at[0], self.recv.at[1, o, chip], self.at.core_peer())


class SumScatter:
    def __init__(self, at, sends, cols, r, recv):
        self.at, self.sends, self.cols, self.r, self.recv = at, sends, cols, r, recv
        self.span = r.final.shape[0]

    def rows_of(self, chip):
        return pl.ds(pl.multiple_of(chip * self.span, self.span), self.span)

    def swap(self):
        r = self.r
        self.swapped = self.sends.start(
            r.give.at[:, self.cols], r.got.at[:, self.cols], self.recv.at[0], self.at.core_peer()
        )

    def wait_swap(self):
        self.sends.settle(self.swapped)
        there = self.r.got.at[:, self.cols]
        arrive(there, self.sends.sems.at[0], self.recv.at[0], self.at.core_peer())

    def send(self, slot, chip, value, device):
        r, rows = self.r, self.rows_of(chip)
        r.give[rows, self.cols] = value.astype(half)
        self.sends.start(
            r.give.at[rows, self.cols], r.came.at[slot, :, self.cols], self.recv.at[1 + slot], device
        )

    def take(self, slot):
        there = self.r.came.at[slot, :, self.cols]
        arrive(there, self.sends.sems.at[0], self.recv.at[1 + slot], self.at.core_peer())
        return there[...].astype(single)

    def base(self, chip):
        rows = self.rows_of(chip)
        return self.r.acc[rows, self.cols] + self.r.got[rows, self.cols].astype(single)

    def one(self):
        at = self.at
        for dz in at.z_steps() + [0]:
            for x in range(2):
                chip = chip_index(at.z_at(dz), 1 - at.y, x)
                self.send(dz * 2 + x, chip, self.base(chip), at.y_peer())

    def two(self, dz):
        at = self.at
        for x in range(2):
            chip = chip_index(at.z_at(dz), at.y, x)
            value = self.base(chip) + self.take(dz * 2 + x)
            if dz:
                self.send(2 * at.Z + dz * 2 + x, chip, value, at.z_peer(dz))
            else:
                self.r.acc[self.rows_of(chip), self.cols] = value

    def three(self):
        at = self.at
        for flip in (1, 0):
            x = 1 - at.x if flip else at.x
            chip = chip_index(at.z, at.y, x)
            value = self.r.acc[self.rows_of(chip), self.cols]
            for dz in range(1, at.Z):
                value = value + self.take(2 * at.Z + dz * 2 + x)
            if flip:
                self.send(4 * at.Z, chip, value, at.x_peer())
            else:
                self.r.final[:, self.cols] = value

    def four(self):
        at, r = self.at, self.r
        r.final[:, self.cols] += self.take(4 * at.Z)
        rows = self.span // 2
        there = r.final.at[pl.ds(pl.multiple_of((1 - at.c) * rows, rows), rows), self.cols]
        last = self.recv.shape[0] - 1
        self.sends.start(there, r.final_other.at[:, self.cols], self.recv.at[last], at.core_peer())

    def end(self):
        there = self.r.final_other.at[:, self.cols]
        arrive(there, self.sends.sems.at[0], self.recv.at[self.recv.shape[0] - 1], self.at.core_peer())


VMEM_LIMIT = 62 * 1024 * 1024
GROUP_ROWS = 128


def model_scratch(E, T, D, cap):
    slots = E * cap
    return dict(
        pick=pltpu.VMEM((slots, T), half), place=pltpu.VMEM((T, slots), half),
        mine=pltpu.VMEM((T, LANES), single),
    )


def end_scratch(T, D):
    return dict(
        gqkv=pltpu.VMEM((2, T, 3 * D // 2), half), gproj=pltpu.VMEM((T, D), half), gatt=pltpu.VMEM((T, D), half),
        grad_res=pltpu.VMEM((T, D), single), router_sum=pltpu.VMEM((D, LANES), single),
        hid_a_t=pltpu.VMEM((D, T), half), att_t=pltpu.VMEM((D, T), half),
    )


def start_kernel(E, names, *refs):
    r = Named(names, refs)
    cap = r.out_h.shape[1]
    set_places(E, cap, r)
    gate = attend(E, r, r.wts, r.small)
    to_slots(r, r.hid_b[...], r.out_h)
    to_slots(r, (gate * r.cotangent[...].astype(single)).astype(half), r.out_g)


def end_kernel(E, total_tokens, names, *refs):
    r = Named(names, refs)
    D = r.tokens.shape[1]
    set_places(E, r.ret_o.shape[1], r)
    transposes(r)
    mid_gain, mid_shift = backward_body(E, total_tokens, r, r.wts, r.small, r.counts[0:1], set_output(r))
    _, last_cols = columns_of(D)
    for part in range(2):
        def write_first(rows, cols, value):
            r.weight_grads[part, rows, cols] = value

        def write_last(rows, value):
            r.weight_grads[part, rows, last_cols] = value

        for p in range(D // LANES // 2):
            attend_back(r, part, p)
            qkv_weight_grad(r, part, p, write_first)
        proj_weight_grad(r, part, write_last)
    pre_gain, pre_shift = input_body(E, r, r.wts, r.small)
    chance_sum = jnp.sum(r.probs[...], axis=0, keepdims=True)
    r.small_out[...] = small_grads(
        E, r.router_sum[...], (pre_gain, pre_shift, mid_gain, mid_shift), chance_sum, 0, D
    )


class SmallSum:
    def __init__(self, at, sends, r, rows):
        self.at, self.sends, self.r, self.rows = at, sends, r, rows

    def here(self, z, y, x):
        first = chip_index(z, y, x) * 2 * self.rows + self.at.c * self.rows
        return self.r.pack_other[pl.ds(pl.multiple_of(first, self.rows), self.rows), :]

    def send(self, slot, value, device):
        r = self.r
        r.pack_sent[slot] = value
        self.sends.start(r.pack_sent.at[slot], r.pack_came.at[slot], r.pack_recv.at[1 + slot], device)

    def take(self, slot):
        r = self.r
        arrive(r.pack_came.at[slot], r.send.at[0], r.pack_recv.at[1 + slot], self.at.core_peer())
        return r.pack_came[slot]

    def zero(self):
        r = self.r
        self.sends.start(r.pack, r.pack_other, r.pack_recv.at[0], self.at.core_peer())

    def one(self):
        r, at = self.r, self.at
        arrive(r.pack_other, r.send.at[0], r.pack_recv.at[0], at.core_peer())
        r.pack_other[...] += r.pack[...]
        for dz in range(at.Z):
            for x in range(2):
                self.send(dz * 2 + x, self.here(at.z_at(dz), 1 - at.y, x), at.y_peer())

    def two(self):
        at = self.at
        for dz in at.z_steps():
            for x in range(2):
                value = self.here(at.z_at(dz), at.y, x) + self.take(dz * 2 + x)
                self.send(2 * at.Z + dz * 2 + x, value, at.z_peer(dz))

    def three(self):
        at = self.at
        for flip in (1, 0):
            x = 1 - at.x if flip else at.x
            value = self.here(at.z, at.y, x) + self.take(x)
            for dz in range(1, at.Z):
                value = value + self.take(2 * at.Z + dz * 2 + x)
            if flip:
                self.send(4 * at.Z, value, at.x_peer())
        return value

    def four(self, total):
        return total + self.take(4 * self.at.Z)


def whole_scratch(E, T, D, cap, rows):
    Z = E // 2
    slots = 4 * Z + 1
    token = (E, cap, D)
    return dict(
        wts=pltpu.VMEM((2, D, 2 * D), half), small=pltpu.VMEM((D, LANES), half),
        shard=pltpu.VMEM((2, rows, 2 * D), single), small_shard=pltpu.VMEM((rows, LANES), single),
        other=pltpu.VMEM((rows, 2 * D), single), other_small=pltpu.VMEM((rows, LANES), single),
        square=pltpu.VMEM((LANES, LANES), single), counts=pltpu.VMEM((8, LANES), single),
        hid_a=pltpu.VMEM((T, D), half), qkv=pltpu.VMEM((2, T, 3 * D // 2), half), att=pltpu.VMEM((T, D), half),
        resid=pltpu.VMEM((T, D), single), hid_b=pltpu.VMEM((T, D), half),
        probs=pltpu.VMEM((T, LANES), single), gates=pltpu.VMEM((8, E * cap), single),
        out_h=pltpu.VMEM(token, half), out_g=pltpu.VMEM(token, half),
        ret_o=pltpu.VMEM(token, half), ret_g=pltpu.VMEM(token, half),
        acc=pltpu.VMEM((D, 2 * D), single), give=pltpu.VMEM((D, 2 * D), half), got=pltpu.VMEM((D, 2 * D), half),
        came=pltpu.VMEM((slots, 2 * rows, 2 * D), half),
        final=pltpu.VMEM((2 * rows, 2 * D), single), final_other=pltpu.VMEM((rows, 2 * D), single),
        pack=pltpu.VMEM((D, LANES), single), pack_other=pltpu.VMEM((D, LANES), single),
        pack_sent=pltpu.VMEM((slots, rows, LANES), single),
        pack_came=pltpu.VMEM((slots, rows, LANES), single),
        reads=DMA((10,)), writes=DMA((5,)), local=DMA((4,)), send=DMA((60 * Z + 32,)), gather_recv=DMA((2, 3, 4 * Z)), own_recv=DMA((2,)),
        sum_recv=DMA((D // LANES // 2 + 1, slots + 2)), pack_recv=DMA((slots + 1,)),
    )


def whole_kernel(E, total_tokens, G, names, *refs):
    r = Named(names, refs)
    rows, D = r.proj_shard.shape
    T = r.tokens.shape[0]
    cap = r.out_h.shape[1]
    pairs = [
        (r.x_qkv, r.qkv_shard), (r.x_proj, r.proj_shard), (r.x_assign, r.assign), (r.x_router, r.router),
        (r.x_pre_gain, r.pre_gain), (r.x_pre_shift, r.pre_shift), (r.x_mid_gain, r.mid_gain),
        (r.x_mid_shift, r.mid_shift), (r.x_tokens, r.tokens), (r.x_cotangent, r.cotangent),
    ]
    reads = [pltpu.make_async_copy(src, there, r.reads.at[i]) for i, (src, there) in enumerate(pairs)]
    at = Place(E)
    experts = Experts(E, 2, G, r, True)
    experts.greet()
    for read in reads:
        read.start()
    sends = Sends(r.send)
    width = D // 2
    pairs_here = width // LANES
    first_cols, last_cols = columns_of(D)
    through = r.acc.at[:, 0:D], r.acc.at[:, D : 2 * D]
    loads = [
        pltpu.make_async_copy(w.at[0], there, r.local.at[i])
        for i, (w, there) in enumerate(zip((r.w_in, r.w_dn), through))
    ]
    for load in loads:
        load.start()
    r.square[...] = jnp.zeros_like(r.square)
    for read in reads[:2]:
        read.wait()
    for part in range(2):
        for p in range(pairs_here):
            for m in range(3):
                first, to = m * D + part * width + p * LANES, (3 * p + m) * LANES
                r.shard[part, :, to : to + LANES] = r.qkv_shard[:, first : first + LANES]
        r.shard[part, :, 3 * width :] = r.proj_shard[:, part * width : (part + 1) * width]
    for read in reads[2:8]:
        read.wait()
    assign = r.assign[...].astype(single)
    r.square[0:E, 0:rows] = r.router[...]
    for i, gain in enumerate((r.pre_gain, r.pre_shift, r.mid_gain, r.mid_shift)):
        r.square[E + i : E + i + 1, 0:rows] = gain[...]
    numbers = iota((rows, T), 0).astype(single)
    count = jnp.sum(jnp.where(assign == numbers, 1.0, 0.0), axis=1, keepdims=True)
    lane = iota((rows, LANES), 1)
    r.small_shard[...] = jnp.where(lane == E + 4, count, r.square[...].T[0:rows, :])

    experts.meet()
    core = at.core_peer()
    sends.start(r.shard.at[1 - at.c], r.other, r.own_recv.at[0], core)
    sends.start(r.small_shard, r.other_small, r.own_recv.at[1], core)
    gather = Gather(at, sends, r.wts, r.small, (first_cols, last_cols), r.gather_recv, rows)
    own_rows = gather.rows_of(chip_index(at.z, at.y, at.x))

    def both(here, there):
        low, high = jnp.where(at.c == 0, here, there), jnp.where(at.c == 0, there, here)
        return jnp.concatenate([low, high], axis=0).astype(half)

    arrive(r.other, r.send.at[0], r.own_recv.at[0], core)
    r.wts[at.c, own_rows, :] = both(r.shard[at.c], r.other[...])
    gather.along_x(0)
    gather.own(0)
    arrive(r.other_small, r.send.at[0], r.own_recv.at[1], core)
    r.small[own_rows, :] = both(r.small_shard[...], r.other_small[...])
    gather.along_x(2)
    gather.along_x(1)
    gather.own(2)
    for load in loads:
        load.wait()
    experts.share_weights(*through)
    gather.second(0)
    gather.second(2)
    gather.third(0)
    gather.third(2)
    for read in reads[8:]:
        read.wait()
    set_places(E, cap, r)
    to_slots(r, r.cotangent[...], r.out_g)
    gather.fourth(0)
    gather.fourth(2)
    gather.own(1)
    gather.second(1)
    experts.send_out(1)
    gather.finish(0)
    place = lax.rem(iota((D, LANES), 0), rows)
    column = r.small[:, E + 4 : E + 5].astype(single)
    total = jnp.sum(jnp.where(place == iota((D, LANES), 1), column, 0.0), axis=0, keepdims=True)
    r.counts[...] = jnp.broadcast_to(total, r.counts.shape)

    def between():
        gather.third(1)

    def then():
        gather.fourth(1)
        gather.finish(1)

    gate = attend(E, r, r.wts, r.small, between, then)
    to_slots(r, r.hid_b[...], r.out_h)
    gates = jnp.sum(r.place[...].astype(single) * gate, axis=0, keepdims=True)
    r.gates[...] = jnp.broadcast_to(gates, r.gates.shape)
    experts.send_out(2, 0)
    experts.run()
    experts.end_weights()
    experts.turn_rows()
    experts.start_grads(1)
    experts.own_grads(1, None)
    transposes(r)
    experts.wait_returns(1, 2)
    experts.send_outputs()

    grad_gate = sum(r.ret_gg[i, 0:1, :] for i in range(E))
    grad_gate = jnp.sum(r.place[...].astype(single) * grad_gate, axis=1, keepdims=True)
    mid_gain, mid_shift = backward_body(E, total_tokens, r, r.wts, r.small, r.counts[0:1], grad_gate)
    last = SumScatter(at, sends, last_cols, r, r.sum_recv.at[pairs_here])
    firsts = [
        SumScatter(at, sends, pl.ds(3 * LANES * p, 3 * LANES), r, r.sum_recv.at[p]) for p in range(pairs_here)
    ]
    smalls = SmallSum(at, sends, r, rows)

    def give_last(here, value):
        r.give[here, last_cols] = value.astype(half)

    def keep_last(here, value):
        r.acc[here, last_cols] = value

    def give_first(here, cols, value):
        r.give[here, cols] = value.astype(half)

    def keep_first(here, cols, value):
        r.acc[here, cols] = value

    proj_weight_grad(r, 1 - at.c, give_last)
    last.swap()
    proj_weight_grad(r, at.c, keep_last)
    for p, first in enumerate(firsts):
        attend_back(r, 1 - at.c, p)
        qkv_weight_grad(r, 1 - at.c, p, give_first)
        first.swap()
        if p == 0:
            last.wait_swap()
            last.one()
        attend_back(r, at.c, p)
        qkv_weight_grad(r, at.c, p, keep_first)
        first.wait_swap()
        first.one()
    steps_z = at.z_steps() + [0]
    for dz in steps_z:
        last.two(dz)
    pre_gain, pre_shift = input_body(E, r, r.wts, r.small)
    chance_sum = jnp.sum(r.probs[...], axis=0, keepdims=True)
    r.pack[...] = small_grads(
        E, r.router_sum[...], (pre_gain, pre_shift, mid_gain, mid_shift), chance_sum, rows, D
    )
    smalls.zero()
    for dz in steps_z:
        firsts[0].two(dz)
    experts.wait_returns(0)
    set_output(r)
    smalls.one()
    writes = [
        pltpu.make_async_copy(there, dst, r.writes.at[i])
        for i, (there, dst) in enumerate((
            (r.input_grad, r.y_input_grad), (r.layer_out, r.y_layer_out), (r.small_out, r.y_small_out),
            (r.qkv_grad, r.y_qkv_grad), (r.proj_grad, r.y_proj_grad),
        ))
    ]
    for write in writes[:2]:
        write.start()
    for first in firsts[1:-1]:
        for dz in steps_z:
            first.two(dz)
    pieces = r.resid, r.grad_res
    leaving = []

    def store(i, rows_at, value):
        n = len(leaving) % 2
        if len(leaving) > 1:
            leaving[-2].wait()
        pieces[n][0 : rows_at.size, :] = value
        copy = pltpu.make_async_copy(
            pieces[n].at[0 : rows_at.size], (r.in_own, r.dn_own)[i].at[0, rows_at, :], r.local.at[2 + n]
        )
        copy.start()
        leaving.append(copy)

    experts.start_grads(0)
    for dz in steps_z if len(firsts) > 1 else ():
        firsts[-1].two(dz)
    smalls.two()
    experts.own_grads(0, store)
    last.three()
    for first in firsts:
        first.three()
    last.four()
    total = smalls.three()
    for first in firsts:
        first.four()
    total = smalls.four(total)
    scale = r.counts[0:1] * (balance_weight * E / total_tokens)
    chance = jnp.sum(jnp.where(lane == E + 4, total, 0.0), axis=1, keepdims=True)
    chosen = jnp.where((lane == iota((rows, LANES), 0)) & (lane < E), chance * scale, 0.0)
    loss = jnp.sum(jnp.sum(chosen, axis=1, keepdims=True), axis=0, keepdims=True) / total_tokens
    r.square[0:rows, :] = jnp.where(lane == E + 5, loss, total)
    r.small_out[...] = r.square[...].T[0 : r.small_out.shape[0], :]
    writes[2].start()
    last.end()
    for first in firsts:
        first.end()
    half_rows = pl.ds(pl.multiple_of(at.c * rows, rows), rows)
    mine, theirs = r.final[half_rows, :], r.final_other[...]
    for part, value in enumerate((jnp.where(at.c == 0, mine, theirs), jnp.where(at.c == 0, theirs, mine))):
        for p in range(pairs_here):
            for m in range(3):
                begin, come = m * D + part * width + p * LANES, (3 * p + m) * LANES
                r.qkv_grad[:, begin : begin + LANES] = value[:, come : come + LANES]
        r.proj_grad[:, part * width : (part + 1) * width] = value[:, 3 * width :]
    for write in writes[3:]:
        write.start()
    experts.end()
    sends.finish()
    for write in writes + leaving[-2:]:
        write.wait()


def out_kernel(E, names, *refs):
    r = Named(names, refs)
    pairs = [
        (r.in_own, r.h0), (r.in_came, r.h1), (r.dn_own, r.h2), (r.dn_came, r.h3),
        (r.layer_in, r.h4), (r.input_in, r.h5), (r.qkv_in, r.h6), (r.proj_in, r.h7),
    ]
    loads = [pltpu.make_async_copy(src, there, r.sems.at[0, i]) for i, (src, there) in enumerate(pairs)]
    outs = [
        (r.h4, r.layer_out), (r.h5, r.input_grad), (r.h6, r.qkv_grad), (r.h7, r.proj_grad),
    ]
    stores = [pltpu.make_async_copy(there, dst, r.sems.at[1, i]) for i, (there, dst) in enumerate(outs)]
    for load in loads[4:] + loads[:4]:
        load.start()
    rows = r.proj_in.shape[0]
    small_load = pltpu.make_async_copy(r.small_in, r.h8, r.sems.at[0, 8])
    small_load.start()
    small_load.wait()
    r.s_router[...] = r.h8[0:E, 0:rows]
    for i, gain in enumerate((r.s_pre_gain, r.s_pre_shift, r.s_mid_gain, r.s_mid_shift)):
        gain[...] = r.h8[E + i : E + i + 1, 0:rows]
    r.s_loss[...] = r.h8[E + 5 : E + 6, 0:1]
    small_outs = [
        (r.s_router, r.router), (r.s_pre_gain, r.pre_gain), (r.s_pre_shift, r.pre_shift),
        (r.s_mid_gain, r.mid_gain), (r.s_mid_shift, r.mid_shift), (r.s_loss, r.loss),
    ]
    small_stores = [
        pltpu.make_async_copy(there, dst, r.sems.at[2, i]) for i, (there, dst) in enumerate(small_outs)
    ]
    for store in small_stores:
        store.start()
    for load, store in zip(loads[4:], stores):
        load.wait()
        store.start()
    for i, (own, came, dst) in enumerate(((r.h0, r.h1, r.in_grad), (r.h2, r.h3, r.dn_grad))):
        loads[2 * i].wait()
        loads[2 * i + 1].wait()
        size = own.shape[1] // 4
        for piece in range(4):
            at = pl.ds(piece * size, size)
            own[0, at, :] += sum(came[j, at, :].astype(single) for j in range(came.shape[0]))
            store = pltpu.make_async_copy(own.at[0, at, :], dst.at[0, at, :], r.sems.at[1, 4 + 4 * i + piece])
            store.start()
            stores.append(store)
    for store in stores + small_stores:
        store.wait()


def on_device(
    tokens_in, out_cotangent, qkv_weight, proj_weight, router_weight, pre_gain, pre_shift, mid_gain, mid_shift,
    expert_in, expert_down, assignment,
):
    T, D = tokens_in.shape
    E, H = lax.axis_size("expert"), lax.axis_size("hid")
    X = H // 2
    Z = E // 2
    cap = 2 * T // E
    G = group_size(E, cap)
    Fq = expert_in.shape[2]
    total_tokens = T * E * H
    rows = proj_weight.shape[0]
    both = ("expert", "hid")
    assign = assignment.reshape(1, T)
    token = ((T, D), half)
    slot = ((E, cap, D), half)
    vectors = dict(pre_gain=pre_gain, pre_shift=pre_shift, mid_gain=mid_gain, mid_shift=mid_shift)
    if X == 2 and E % 2 == 0 and rows % 8 == 0 and E <= rows <= LANES and Fq == D and D % 256 == 0 and T >= 256:
        small_rows = E + 8
        found = call(
            functools.partial(whole_kernel, E, total_tokens, G),
            dict(
                x_tokens=(tokens_in, ANY_SPEC), x_cotangent=(out_cotangent, ANY_SPEC), x_assign=(assign, ANY_SPEC),
                x_qkv=(qkv_weight, ANY_SPEC), x_proj=(proj_weight, ANY_SPEC), x_router=(router_weight.T, ANY_SPEC),
                x_pre_gain=(pre_gain.reshape(1, rows), ANY_SPEC), x_pre_shift=(pre_shift.reshape(1, rows), ANY_SPEC),
                x_mid_gain=(mid_gain.reshape(1, rows), ANY_SPEC), x_mid_shift=(mid_shift.reshape(1, rows), ANY_SPEC),
                w_in=(expert_in, ANY_SPEC), w_dn=(expert_down, ANY_SPEC),
            ),
            dict(
                y_layer_out=token + (ANY_SPEC,), y_input_grad=token + (ANY_SPEC,),
                y_qkv_grad=((rows, 3 * D), single, ANY_SPEC), y_proj_grad=((rows, D), single, ANY_SPEC),
                y_small_out=((small_rows, LANES), single, ANY_SPEC),
                in_own=((1, D, Fq), single, ANY_SPEC), dn_own=((1, Fq, D), single, ANY_SPEC),
                in_came=((X - 1, D, Fq), half, ANY_SPEC), dn_came=((X - 1, Fq, D), half, ANY_SPEC),
            ),
            dict(
                tokens=pltpu.VMEM(*token), cotangent=pltpu.VMEM(*token), assign=pltpu.VMEM((1, T), jnp.int32),
                qkv_shard=pltpu.VMEM((rows, 3 * D), single), proj_shard=pltpu.VMEM((rows, D), single),
                router=pltpu.VMEM((E, rows), single), pre_gain=pltpu.VMEM((1, rows), single),
                pre_shift=pltpu.VMEM((1, rows), single), mid_gain=pltpu.VMEM((1, rows), single),
                mid_shift=pltpu.VMEM((1, rows), single), layer_out=pltpu.VMEM(*token), input_grad=pltpu.VMEM(*token),
                qkv_grad=pltpu.VMEM((rows, 3 * D), single), proj_grad=pltpu.VMEM((rows, D), single),
                small_out=pltpu.VMEM((small_rows, LANES), single),
                **whole_scratch(E, T, D, cap, rows), **model_scratch(E, T, D, cap), **end_scratch(T, D),
                **expert_scratch(E, X, cap, D, Fq),
            ),
            1, "layer",
        )
        layer_out, input_grad, qkv_grad, proj_grad, small_out, in_own, dn_own, in_came, dn_came = found
        vector = ((1, rows), single, ANY_SPEC)
        found = call(
            functools.partial(out_kernel, E),
            dict(
                layer_in=(layer_out, ANY_SPEC), input_in=(input_grad, ANY_SPEC),
                qkv_in=(qkv_grad, ANY_SPEC), proj_in=(proj_grad, ANY_SPEC),
                in_own=(in_own, ANY_SPEC), dn_own=(dn_own, ANY_SPEC),
                in_came=(in_came, ANY_SPEC), dn_came=(dn_came, ANY_SPEC), small_in=(small_out, ANY_SPEC),
            ),
            dict(
                layer_out=token + (ANY_SPEC,), input_grad=token + (ANY_SPEC,),
                qkv_grad=((rows, 3 * D), single, ANY_SPEC), proj_grad=((rows, D), single, ANY_SPEC),
                in_grad=((1, D, Fq), single, ANY_SPEC), dn_grad=((1, Fq, D), single, ANY_SPEC),
                router=((E, rows), single, ANY_SPEC), pre_gain=vector, pre_shift=vector, mid_gain=vector,
                mid_shift=vector, loss=((1, 1), single, ANY_SPEC),
            ),
            dict(
                h0=pltpu.VMEM((1, D, Fq), single), h1=pltpu.VMEM((X - 1, D, Fq), half),
                h2=pltpu.VMEM((1, Fq, D), single), h3=pltpu.VMEM((X - 1, Fq, D), half),
                h4=pltpu.VMEM(*token), h5=pltpu.VMEM(*token), h6=pltpu.VMEM((rows, 3 * D), single),
                h7=pltpu.VMEM((rows, D), single), h8=pltpu.VMEM((small_rows, LANES), single),
                s_router=pltpu.VMEM((E, rows), single), s_pre_gain=pltpu.VMEM((1, rows), single),
                s_pre_shift=pltpu.VMEM((1, rows), single), s_mid_gain=pltpu.VMEM((1, rows), single),
                s_mid_shift=pltpu.VMEM((1, rows), single), s_loss=pltpu.VMEM((1, 1), single), sems=DMA((3, 12)),
            ),
            None, "results",
        )
        layer_out, input_grad, qkv_grad, proj_grad, in_grad, dn_grad, router, *grads, loss = found
        return (
            layer_out, loss.reshape(()), input_grad, qkv_grad, proj_grad, router.T,
            *[value.reshape(rows) for value in grads], in_grad, dn_grad,
        )

    small_in = jnp.concatenate([router_weight] + [value[:, None] for value in vectors.values()], axis=1)
    small_in = jnp.pad(small_in, ((0, 0), (0, LANES - small_in.shape[1])))
    shard = jnp.concatenate([qkv_weight, proj_weight], axis=1).astype(half)
    wts = lax.all_gather(shard, both, axis=0, tiled=True)
    wts = jnp.concatenate(
        [
            wts[:, : 3 * D].reshape(D, 3, 2, D // 2 // LANES, LANES).transpose(2, 0, 3, 1, 4).reshape(2, D, 3 * D // 2),
            wts[:, 3 * D :].reshape(D, 2, D // 2).transpose(1, 0, 2),
        ],
        axis=2,
    )
    small = lax.all_gather(small_in.astype(half), both, axis=0, tiled=True)
    onehot = assignment[:, None] == jnp.arange(LANES, dtype=jnp.int32)[None, :]
    counts = lax.psum(jnp.sum(onehot.astype(single), axis=0), both)
    saved = dict(
        hid_a=token, qkv=((2, T, 3 * D // 2), half), att=token, resid=((T, D), single), hid_b=token,
        probs=((T, LANES), single),
    )
    given = dict(tokens=tokens_in, cotangent=out_cotangent, assign=assign, wts=wts, small=small)
    out_h, out_g, *rest = call(
        functools.partial(start_kernel, E), given, dict(out_h=slot, out_g=slot, **saved),
        model_scratch(E, T, D, cap), None, "start",
    )
    ret_o, ret_g, in_own, dn_own, in_came, dn_came = call(
        functools.partial(expert_kernel, E, X, G),
        dict(out_h=out_h, out_g=out_g, w_in=expert_in[0], w_dn=expert_down[0]),
        dict(
            ret_o=slot, ret_g=slot, in_grad=((D, Fq), single), dn_grad=((Fq, D), single),
            in_came=((X - 1, D, Fq), half), dn_came=((X - 1, Fq, D), half),
        ),
        expert_scratch(E, X, cap, D, Fq), 1, "experts",
    )
    in_grad = in_own + jnp.sum(in_came.astype(single), axis=0)
    dn_grad = dn_own + jnp.sum(dn_came.astype(single), axis=0)
    layer_out, input_grad, weight_grads, packed = call(
        functools.partial(end_kernel, E, total_tokens),
        dict(
            **given, counts=jnp.broadcast_to(counts[None, :], (8, LANES)), **dict(zip(saved, rest)),
            ret_o=ret_o, ret_g=ret_g,
        ),
        dict(
            layer_out=token, input_grad=token, weight_grads=((2, D, 2 * D), single),
            small_out=((D, LANES), single),
        ),
        dict(**model_scratch(E, T, D, cap), **end_scratch(T, D)), None, "end",
    )
    pairs = weight_grads[:, :, : 3 * D // 2].reshape(2, D, D // 2 // LANES, 3, LANES)
    gathered = jnp.concatenate(
        [
            pairs.transpose(1, 3, 0, 2, 4).reshape(D, 3 * D),
            weight_grads[:, :, 3 * D // 2 :].transpose(1, 0, 2).reshape(D, D),
        ],
        axis=1,
    )
    gathered = lax.psum_scatter(gathered, both, scatter_dimension=0, tiled=True)
    small_out = lax.psum_scatter(packed, both, scatter_dimension=0, tiled=True)
    chance = lax.psum(jnp.sum(rest[-1], axis=0), both)
    balance_loss = jnp.sum(chance * counts) * (balance_weight * E / total_tokens) / total_tokens
    return (
        layer_out, balance_loss, input_grad, gathered[:, : 3 * D], gathered[:, 3 * D :], small_out[:, :E],
        *[small_out[:, E + i] for i in range(4)], in_grad[None], dn_grad[None],
    )


def solution(mesh):
    in_specs = (
        P(("expert", "hid"), None),
        P(("expert", "hid"), None),
        P(("expert", "hid"), None),
        P(("expert", "hid"), None),
        P(("expert", "hid"), None),
        P(("expert", "hid")),
        P(("expert", "hid")),
        P(("expert", "hid")),
        P(("expert", "hid")),
        P("expert", None, "hid"),
        P("expert", "hid", None),
        P(("expert", "hid")),
    )
    out_specs = (
        P(("expert", "hid"), None),
        P(),
        P(("expert", "hid"), None),
        P(("expert", "hid"), None),
        P(("expert", "hid"), None),
        P(("expert", "hid"), None),
        P(("expert", "hid")),
        P(("expert", "hid")),
        P(("expert", "hid")),
        P(("expert", "hid")),
        P("expert", None, "hid"),
        P("expert", "hid", None),
    )
    return jax.shard_map(
        on_device, mesh=mesh, in_specs=in_specs, out_specs=out_specs, check_vma=False
    )
```
